256 devices in a mesh: node: 32 (over y, z), rep: 8 (over x, core).
Axes of the slice: x: 4, y: 4, z: 8, core: 2. Of those that a mesh axis runs over, the one named last changes fastest.
Arguments:
- memory: float32 [32768, 256], P('node'), may hold values from -3 to 3
- hot_memory: float32 [1024, 256], replicated, may hold values from -3 to 3
- cot_cold: float32 [32768, 256], P('node'), may hold values from -6 to 6
- cot_hot: float32 [1024, 256], replicated, may hold values from -6 to 6
- src_local: int32 [262144], P(('node', 'rep')), may hold values from 0 to 1023
- dst_ids: int32 [262144], P(('node', 'rep')), may hold values from 0 to 33791, as said below
- times: int32 [262144], P(('node', 'rep')), may hold values from 0 to 4095
- edge_feat: bfloat16 [262144, 128], P(('node', 'rep')), may hold values from -6 to 6
- cold_list: int32 [8192, 32], P(('node', 'rep')), may hold values from 0 to 1023, as said below
- cold_count: int32 [8192], P(('node', 'rep')), may hold values from 0 to 32, as said below
- hot_ids: int32 [1024], replicated, may hold values from 32768 to 33791, as said below
- time_freq: float32 [128], replicated, may hold values from 0.001 to 1
- time_phase: float32 [128], replicated, may hold values from -3.140625 to 3.140625
- w_msg: bfloat16 [512, 512], replicated, may hold values from -0.25 to 0.25
- b_msg: float32 [512], replicated, may hold values from -3 to 3
- w_in: bfloat16 [512, 768], replicated, may hold values from -0.25 to 0.25
- w_hid: bfloat16 [256, 768], replicated, may hold values from -0.375 to 0.375
Outputs:
- new_memory: float32 [32768, 256], P('node')
- new_hot: float32 [1024, 256], replicated
- grad_in: float32 [512, 768], replicated
- grad_hid: float32 [256, 768], replicated
The draws below stay inside these ranges and needn't reach their ends.
Inputs may be any that keep to these rules, and one draw needn't show every extreme that they name: `dst_ids`: each device's events split into cold ones, each named in exactly one used slot of its owner's list, and hot ones whose destination is in hot_ids; cold destinations are node ids below 32768, hot ones 32768 or more. The hot destinations of device d are among the ids 32768 + ((d * 4 + j) mod 1024) for j below 16. `cold_list`: used slots hold distinct event indices of the device; unused slots hold 0. `cold_count`: some owner's list is full on every device. `hot_ids`: A permutation of the hot node ids 32768 to 33791.
All inputs are finite; a program needn't handle non-finite values.
Results may differ from the reference program's by a relative error of at most 0.0018.
The reference program's roundings to bfloat16 on the way (of `src_mem`, `enc`, `messages` and `agg`) count: a program that leaves them out, or rounds other values in their place, can miss the bound.
Values may be sent and summed in bfloat16 or wider, within the bound.
No kernel may reach another device: no remote copies, remote signals or barrier semaphores. Data moves between devices by JAX's collectives and lax.ppermute only.
A program may use at most 128 MiB of HBM per device.

```python
import math
import jax
import jax.numpy as jnp
from jax import lax

DM = 256
EF = 128
TE = 128
MSG = 512
HOT = 1024
NODES_DEV = 1024
E_DEV = 1024
T_BINS = 4096
CAP = 32
NODES = 32768
EVENTS = 262144
N_NODE = 32
N_REP = 8


def event_plan(key):
    key_heavy, key_light, key_big, key_perm, key_row, key_hot = jax.random.split(key, 6)
    devices = N_NODE * N_REP
    heavy = jax.random.permutation(key_heavy, N_NODE)[:4]
    is_heavy = jnp.zeros((N_NODE,), jnp.int32).at[heavy].set(1)
    light = jax.random.randint(key_light, (devices, N_NODE), CAP // 8, CAP // 2 + 1)
    big = jax.random.randint(key_big, (devices, N_NODE), 3 * CAP // 4, CAP + 1)
    counts = jnp.where(is_heavy[None, :] == 1, big, light)
    counts = counts.at[:, heavy[0]].set(CAP)
    ends = jnp.cumsum(counts, axis=1)
    starts = ends - counts
    perms = jax.vmap(lambda k: jax.random.permutation(k, E_DEV))(jax.random.split(key_perm, devices)).astype(jnp.int32)
    slots = jnp.arange(CAP, dtype=jnp.int32)
    valid = slots[None, None, :] < counts[:, :, None]
    where_at = jnp.where(valid, starts[:, :, None] + slots[None, None, :], 0).reshape(devices, N_NODE * CAP)
    lists = jnp.take_along_axis(perms, where_at, axis=1).reshape(devices, N_NODE, CAP)
    lists = jnp.where(valid, lists, 0)
    place = jnp.arange(E_DEV, dtype=jnp.int32)
    owner_at = jnp.sum((place[None, :, None] >= ends[:, None, :]).astype(jnp.int32), axis=2)
    cold_at = place[None, :] < ends[:, -1:]
    rows = jax.random.randint(key_row, (devices, E_DEV), 0, NODES_DEV)
    band = HOT // devices
    offsets = jax.random.randint(key_hot, (devices, E_DEV), 0, 4 * band)
    firsts = jnp.arange(devices, dtype=jnp.int32)[:, None] * band
    hots = NODES + (firsts + offsets) % HOT
    dst_at = jnp.where(cold_at, jnp.minimum(owner_at, N_NODE - 1) * NODES_DEV + rows, hots)
    dst = jax.vmap(lambda p, v: jnp.zeros((E_DEV,), jnp.int32).at[p].set(v))(perms, dst_at.astype(jnp.int32))
    return (counts.astype(jnp.int32), lists.astype(jnp.int32), dst)


def draw_dst_ids(key, part):
    counts, lists, dst = event_plan(key)
    return dst.reshape(-1)


def draw_cold_list(key, part):
    counts, lists, dst = event_plan(key)
    return lists.reshape(N_NODE * N_REP * N_NODE, CAP)


def draw_cold_count(key, part):
    counts, lists, dst = event_plan(key)
    return counts.reshape(-1)


def draw_hot_ids(key, part):
    key = jax.random.fold_in(key, 7)
    return (NODES + jax.random.permutation(key, HOT)).astype(jnp.int32)


def plant(values, key, smallest, high):
    spot = [jax.random.randint(jax.random.fold_in(key, axis), (), 0, length) for axis, length in enumerate(values.shape)]
    longest = values.shape.index(max(values.shape))
    neighbour = spot[:longest] + [(spot[longest] + 1) % values.shape[longest]] + spot[longest + 1:]
    return values.at[tuple(spot)].set(smallest).at[tuple(neighbour)].set(high)


def block_levels(own_key, dims, cuts, low, top_value):
    loudness = 1.0
    for dim, blocks in cuts:
        steps = jax.random.uniform(jax.random.fold_in(jax.random.fold_in(own_key, 6), dim), (blocks,), jnp.float32, low / len(cuts), top_value / len(cuts))
        loudness = loudness * jnp.repeat(jnp.exp(steps), dims[dim] // blocks).reshape((-1,) + (1,) * (len(dims) - 1 - dim))
    return loudness


def normal_values(own_key, shape, spread, reach, pieces=(), kind=jnp.bfloat16):
    array = spread * jax.random.normal(own_key, shape, jnp.float32)
    if pieces:
        array = array * block_levels(own_key, shape, pieces, -0.22, 0.18)
    return jnp.clip(array, -reach, reach).astype(kind)


def setup_inputs(seed: int = 0) -> dict:
    arg_keys = jax.random.split(jax.random.key(seed), 18)
    return {
        "memory": normal_values(arg_keys[0], (NODES, DM), 0.5, 3.0, ((0, 32),), jnp.float32),
        "hot_memory": normal_values(arg_keys[1], (HOT, DM), 0.5, 3.0, (), jnp.float32),
        "cot_cold": normal_values(arg_keys[2], (NODES, DM), 1.0, 6.0, ((0, 32),), jnp.float32),
        "cot_hot": normal_values(arg_keys[3], (HOT, DM), 1.0, 6.0, (), jnp.float32),
        "src_local": plant(jax.random.randint(arg_keys[4], (EVENTS,), 0, NODES_DEV), jax.random.fold_in(arg_keys[4], 1), 0, NODES_DEV - 1).astype(jnp.int32),
        "dst_ids": draw_dst_ids(jax.random.fold_in(arg_keys[17], 71), 0),
        "times": plant(jax.random.randint(arg_keys[6], (EVENTS,), 0, T_BINS), jax.random.fold_in(arg_keys[6], 1), 0, T_BINS - 1).astype(jnp.int32),
        "edge_feat": normal_values(arg_keys[7], (EVENTS, EF), 1.0, 6.0, ((0, 256),)),
        "cold_list": draw_cold_list(jax.random.fold_in(arg_keys[17], 71), 0),
        "cold_count": draw_cold_count(jax.random.fold_in(arg_keys[17], 71), 0),
        "hot_ids": draw_hot_ids(jax.random.fold_in(arg_keys[17], 71), 0),
        "time_freq": jnp.clip(jnp.exp(jax.random.uniform(arg_keys[11], (TE,), jnp.float32, math.log(0.001), math.log(1.0))), 0.001, 1.0),
        "time_phase": jnp.clip(jax.random.uniform(arg_keys[12], (TE,), jnp.float32, -3.140625, 3.140625), -3.140625, 3.140625),
        "w_msg": normal_values(arg_keys[13], (MSG, MSG), MSG ** -0.5, 0.25),
        "b_msg": normal_values(arg_keys[14], (MSG,), 0.5, 3.0, (), jnp.float32),
        "w_in": normal_values(arg_keys[15], (MSG, 3 * DM), MSG ** -0.5, 0.25),
        "w_hid": normal_values(arg_keys[16], (DM, 3 * DM), DM ** -0.5, 0.375),
    }


GRAD_SCALE = 1.0 / 64.0


def gru_forward(agg, mem, w_in, w_hid):
    width = mem.shape[1]
    gate_in = jnp.dot(agg, w_in, preferred_element_type=jnp.float32)
    gate_hid = jnp.dot(mem.astype(jnp.bfloat16), w_hid, preferred_element_type=jnp.float32)
    reset = jax.nn.sigmoid(gate_in[:, :width] + gate_hid[:, :width])
    update = jax.nn.sigmoid(gate_in[:, width:2 * width] + gate_hid[:, width:2 * width])
    cand = jnp.tanh(gate_in[:, 2 * width:] + reset * gate_hid[:, 2 * width:])
    fresh = (1.0 - update) * cand + update * mem
    return fresh, (reset, update, cand, gate_hid[:, 2 * width:])


def gru_grads(agg, mem, saved, cot):
    reset, update, cand, hid_cand = saved
    d_cand = cot * (1.0 - update) * (1.0 - cand * cand)
    d_upd = cot * (mem - cand) * update * (1.0 - update)
    d_reset = d_cand * hid_cand * reset * (1.0 - reset)
    d_input = jnp.concatenate([d_reset, d_upd, d_cand], axis=1)
    d_hidden = jnp.concatenate([d_reset, d_upd, d_cand * reset], axis=1)
    mem_round = lax.optimization_barrier(mem.astype(jnp.bfloat16)).astype(jnp.float32)
    grad_a = jnp.dot(agg.astype(jnp.float32).T, d_input, precision=lax.Precision.HIGHEST)
    grad_b = jnp.dot(mem_round.T, d_hidden, precision=lax.Precision.HIGHEST)
    return grad_a, grad_b


def update_rows(total, count, mem, cot, w_in, w_hid):
    agg = (total / jnp.maximum(count, 1.0)[:, None]).astype(jnp.bfloat16)
    fresh, saved = gru_forward(agg, mem, w_in, w_hid)
    live = (count > 0)[:, None]
    result = jnp.where(live, fresh, mem)
    grad_a, grad_b = gru_grads(agg, mem, saved, jnp.where(live, cot, 0.0))
    return result, grad_a, grad_b


def reference(memory, hot_memory, cot_cold, cot_hot, src_local, dst_ids, times, edge_feat, cold_list, cold_count, hot_ids, time_freq, time_phase, w_msg, b_msg, w_in, w_hid):
    devices = N_NODE * N_REP
    owner_base = (jnp.arange(devices, dtype=jnp.int32) // N_REP) * NODES_DEV
    src_global = (owner_base[:, None] + src_local.reshape(devices, E_DEV)).reshape(-1)
    src_mem = jnp.take(memory, src_global, axis=0).astype(jnp.bfloat16)
    enc = jnp.cos(times.astype(jnp.float32)[:, None] * time_freq[None, :] + time_phase[None, :]).astype(jnp.bfloat16)
    raw = jnp.concatenate([src_mem, edge_feat, enc], axis=1)
    messages = jax.nn.silu(jnp.dot(raw, w_msg, preferred_element_type=jnp.float32) + b_msg[None, :]).astype(jnp.bfloat16)
    lists = cold_list.reshape(devices, N_NODE * CAP)
    slots = jnp.arange(CAP, dtype=jnp.int32)
    valid = (slots[None, :] < cold_count[:, None]).reshape(devices, N_NODE * CAP)
    event_idx = (jnp.arange(devices, dtype=jnp.int32)[:, None] * E_DEV + lists).reshape(-1)
    seg = jnp.where(valid.reshape(-1), jnp.take(dst_ids, event_idx), NODES).astype(jnp.int32)
    picked = jnp.take(messages, event_idx, axis=0).astype(jnp.float32)
    cold_total = jax.ops.segment_sum(picked, seg, num_segments=NODES + 1)[:NODES]
    cold_cnt = jax.ops.segment_sum(jnp.ones(seg.shape, jnp.float32), seg, num_segments=NODES + 1)[:NODES]
    inverse = jnp.zeros((HOT,), jnp.int32).at[hot_ids - NODES].set(jnp.arange(HOT, dtype=jnp.int32))
    is_hot = dst_ids >= NODES
    hot_seg = jnp.where(is_hot, jnp.take(inverse, jnp.clip(dst_ids - NODES, 0, HOT - 1)), HOT).astype(jnp.int32)
    hot_total = jax.ops.segment_sum(messages.astype(jnp.float32), hot_seg, num_segments=HOT + 1)[:HOT]
    hot_cnt = jax.ops.segment_sum(jnp.ones(hot_seg.shape, jnp.float32), hot_seg, num_segments=HOT + 1)[:HOT]
    new_memory, grad_a, grad_b = update_rows(cold_total, cold_cnt, memory, cot_cold, w_in, w_hid)
    new_hot, hot_a, hot_b = update_rows(hot_total, hot_cnt, hot_memory, cot_hot, w_in, w_hid)
    return new_memory, new_hot, (grad_a + hot_a) * GRAD_SCALE, (grad_b + hot_b) * GRAD_SCALE
```

```python
import jax
import jax.numpy as jnp
from jax import lax
from jax.experimental import pallas as pl
from jax.experimental.pallas import tpu as pltpu
from jax.sharding import PartitionSpec as P

GRAD_SCALE = 1.0 / 64.0
DEAD = 2.0**100
F32, BF16, I32 = jnp.float32, jnp.bfloat16, jnp.int32
PARAMS = pltpu.CompilerParams(vmem_limit_bytes=48 * 1024 * 1024)
VM = pl.BlockSpec(memory_space=pltpu.VMEM)
SM = pl.BlockSpec(memory_space=pltpu.SMEM)


def iota(shape, dim):
    return lax.broadcasted_iota(I32, shape, dim)


def one_hot(mask):
    return jnp.where(mask, 1.0, 0.0).astype(BF16)


def mm(a, b, dims=((1,), (0,))):
    return lax.dot_general(a, b, (dims, ((), ())), preferred_element_type=F32)


def call(body, out_shape, n_smem, args, scratch=()):
    return pl.pallas_call(
        body,
        out_shape=out_shape,
        in_specs=[SM] * n_smem + [VM] * (len(args) - n_smem),
        out_specs=jax.tree.map(lambda _: VM, out_shape),
        scratch_shapes=list(scratch),
        compiler_params=PARAMS,
    )(*args)


def message_kernel(pos, idx, mem, edge, enc, w, b, send, hot, msgs, cols):
    cols[...] = idx[...].T
    mem16 = mem[...].astype(BF16)
    n_ev = idx.shape[1]
    step = 256
    for e in range(0, n_ev, step):
        src = cols[e : e + step, 0:1]
        src_mem = mm(one_hot(iota((step, mem.shape[0]), 1) == src), mem16).astype(BF16)
        raw = jnp.concatenate([src_mem, edge[e : e + step, :], enc[e : e + step, :]], axis=1)
        pre = mm(raw, w[...]) + b[...]
        msgs[e : e + step, 0:512] = (pre * jax.nn.sigmoid(pre)).astype(BF16)
        row = cols[e : e + step, 2:3] & 1023
        lane = iota((step, 128), 1)
        tail = jnp.where(lane == 0, row >> 5, jnp.where(lane == 1, row & 31, jnp.where(lane == 2, 1, 0)))
        msgs[e : e + step, 512:640] = tail.astype(F32).astype(BF16)
    for s in range(0, n_ev, step):
        pick = one_hot(iota((step, n_ev), 1) == cols[s : s + step, 3:4])
        send[s : s + step, :] = mm(pick, msgs[...]).astype(BF16)
    dst = idx[2:3, :]
    window = jnp.where(dst >= 32768, (dst - 32768 - 32 * pos[0] + 1024) & 1023, -1)
    q = iota((96, n_ev), 0)
    hit = one_hot(4 * (q >> 3) + (q & 3) == window)
    total = mm(hit, msgs[:, 0:512])
    count = jnp.sum(hit.astype(F32), axis=1, keepdims=True)
    hot[...] = jnp.where((iota((96, 512), 0) & 7) < 4, total, count)


def cold_kernel(pos, recv, keep, send):
    tail = recv[:, 512:640].astype(F32).T
    row = jnp.where(tail[2:3, :] > 0.5, tail[0:1, :] * 32.0 + tail[1:2, :], -1.0).astype(I32)
    ones = jnp.ones((8, recv.shape[0]), BF16)
    for out, core in ((send, 1 - pos[1]), (keep, pos[1])):
        q = iota((512, recv.shape[0]), 0)
        hit = one_hot(((q >> 7) * 256 + (q & 127) + core * 128) == row)
        total = mm(hit, recv[:, 0:512])
        count = mm(ones, hit, ((1,), (1,)))
        for j in range(4):
            out[j, 0:128, :] = total[128 * j : 128 * j + 128, :]
            out[j, 128:136, 0:128] = count[:, 128 * j : 128 * j + 128]
            out[j, 128:136, 128:512] = jnp.zeros((8, 384), F32)


def add_kernel(pos, keep, recv, o0, o1, o2, o3):
    for d, out in enumerate((o0, o1, o2, o3)):
        j = (pos[0] + d) & 3
        out[...] = keep[j] + recv[j]


def agg_kernel(p0, p1, p2, p3, hot, out):
    total = p0[...] + p1[...] + p2[...] + p3[...]
    count = total[128:129, 0:128]
    count = jnp.sum(jnp.where(iota((128, 128), 0) == iota((128, 128), 1), count, 0.0), axis=1, keepdims=True)
    agg = jnp.where(count > 0.0, total[0:128, :] / jnp.maximum(count, 1.0), DEAD)
    out[0:128, :] = agg.astype(BF16)
    out[128:144, :] = hot[...]


def gates(agg, mem, w_in, w_hid):
    gi = mm(agg, w_in)
    gh = mm(mem.astype(BF16), w_hid)
    reset = jax.nn.sigmoid(gi[:, 0:256] + gh[:, 0:256])
    update = jax.nn.sigmoid(gi[:, 256:512] + gh[:, 256:512])
    cand = jnp.tanh(gi[:, 512:768] + reset * gh[:, 512:768])
    return reset, update, cand, gh[:, 512:768]


def hot_kernel(parts, mem, w_in, w_hid, agg_out, new_out):
    total = parts[0]
    for k in range(1, 8):
        total = total + parts[k]
    count = total[4:8, :]
    agg = jnp.where(count > 0.0, total[0:4, :] / jnp.maximum(count, 1.0), DEAD)
    agg = jnp.concatenate([agg, jnp.full((12, 512), DEAD, F32)], axis=0).astype(BF16)
    agg_out[...] = agg
    live = agg[:, 0:256].astype(F32) < DEAD * 0.5
    mem = mem[...]
    wide = agg.astype(F32)
    agg = jnp.where(wide < DEAD * 0.5, wide, 0.0).astype(BF16)
    reset, update, cand, _ = gates(agg, mem, w_in[...], w_hid[...])
    new_out[...] = jnp.where(live, (1.0 - update) * cand + update * mem, mem)[0:8, :]


def update_kernel(pos, a0, a1, a2, a3, b0, b1, b2, b3, mem, cot, w_in, w_hid, new, grad, agg, acc):
    x, core, rep = pos[0], pos[1], pos[2]
    for group, c in (((a0, a1, a2, a3), core), ((b0, b1, b2, b3), 1 - core)):
        for d, part in enumerate(group):
            block = 2 * ((x - d + 4) & 3) + c
            agg[pl.ds(pl.multiple_of(block * 128, 128), 128), :] = part[0:128, :]
            agg[pl.ds(pl.multiple_of(1024 + block * 16, 16), 16), :] = part[128:144, :]
    k, q = iota((512, 128), 0), iota((512, 128), 1)
    sel_a = one_hot((k == 64 * rep + q) & (q < 64))
    k, q = iota((256, 128), 0), iota((256, 128), 1)
    sel_m = one_hot((k == 32 * rep + q - 64) & (q >= 64) & (q < 96))
    step = 384
    for s in range(0, 1152, step):
        wide = agg[s : s + step, :].astype(F32)
        live = wide[:, 0:1] < DEAD * 0.5
        a = jnp.where(live, wide, 0.0).astype(BF16)
        m = mem[s : s + step, :]
        reset, update, cand, hid_cand = gates(a, m, w_in[...], w_hid[...])
        fresh = jnp.where(live, (1.0 - update) * cand + update * m, m)
        rows = min(step, 1024 - s)
        new[s : s + rows, :] = fresh[0:rows, :]
        g = jnp.where(live, cot[s : s + step, :], 0.0)
        d_cand = g * (1.0 - update) * (1.0 - cand * cand)
        d_upd = g * (m - cand) * update * (1.0 - update)
        d_reset = d_cand * hid_cand * reset * (1.0 - reset)
        left = (mm(a, sel_a) + mm(m.astype(BF16), sel_m)).astype(BF16)
        for j, d in enumerate((d_reset, d_upd, d_cand, d_cand * reset)):
            hi = d.astype(BF16)
            rest = d - hi.astype(F32)
            mid = rest.astype(BF16)
            low = (rest - mid.astype(F32)).astype(BF16)
            dims = ((0,), (0,))
            part = mm(left, hi, dims) + (mm(left, mid, dims) + mm(left, low, dims))
            cols = slice(256 * j, 256 * j + 256)
            if s == 0:
                acc[:, cols] = part
            else:
                acc[:, cols] += part
    total = acc[...] * GRAD_SCALE
    third = jnp.where(iota((128, 256), 0) < 64, total[:, 512:768], total[:, 768:1024])
    total = jnp.concatenate([total[:, 0:512], third], axis=1)
    for p in range(32):
        i, j = p // 2, p % 2
        grad[p] = total[8 * i : 8 * i + 8, 384 * j : 384 * j + 384]


def piece_kernel(parts, out):
    total = parts[0]
    for k in range(1, 32):
        total = total + parts[k]
    for k in range(32):
        out[k] = total


def place_kernel(pos, a0, a1, a2, a3, b0, b1, b2, b3, g_in, g_hid):
    x, core = pos[0], pos[1]
    for group, c in (((a0, a1, a2, a3), core), ((b0, b1, b2, b3), 1 - core)):
        for d, part in enumerate(group):
            block = 2 * ((x - d + 4) & 3) + c
            for p in range(24):
                i, j = p // 2, p % 2
                cols = slice(384 * j, 384 * j + 384)
                if i < 8:
                    g_in[pl.ds(pl.multiple_of(block * 64 + 8 * i, 8), 8), cols] = part[p]
                else:
                    g_hid[pl.ds(pl.multiple_of(block * 32 + 8 * (i - 8), 8), 8), cols] = part[p]


def swap_core(v):
    return lax.ppermute(v, "rep", [(k, k ^ 1) for k in range(8)])


def shift_x(v, d):
    return lax.ppermute(v, "rep", [(k, (k + 2 * d) % 8) for k in range(8)])


def gather_rep(v):
    own = [v] + [shift_x(v, d) for d in (1, 2, 3)]
    return own + [swap_core(u) for u in own]


def on_device(
    memory,
    hot_memory,
    cot_cold,
    cot_hot,
    src_local,
    dst_ids,
    times,
    edge_feat,
    cold_list,
    cold_count,
    hot_ids,
    time_freq,
    time_phase,
    w_msg,
    b_msg,
    w_in,
    w_hid,
):
    node = lax.axis_index("node")
    rep = lax.axis_index("rep")
    pos = jnp.stack([rep // 2, rep % 2, rep]).astype(I32)
    sds = jax.ShapeDtypeStruct

    slots = jnp.arange(32, dtype=I32)
    listed = jnp.where(slots[None, :] < cold_count[:, None], cold_list, -1).reshape(-1)
    zero = jnp.zeros_like(listed)
    idx = jnp.stack([src_local, times, dst_ids, listed, zero, zero, zero, zero])
    enc = jnp.cos(times.astype(F32)[:, None] * time_freq[None, :] + time_phase[None, :]).astype(BF16)
    send, hot = call(
        message_kernel,
        (sds((1024, 640), BF16), sds((96, 512), F32)),
        1,
        (node.astype(I32)[None], idx, memory, edge_feat, enc, w_msg, b_msg[None, :]),
        (pltpu.VMEM((1024, 640), BF16), pltpu.VMEM((1024, 8), I32)),
    )
    recv = lax.all_to_all(send, "node", split_axis=0, concat_axis=0, tiled=True)

    spill = lax.ppermute(hot[64:96], "node", [(k, (k + 1) % 32) for k in range(32)])
    hot_main = jnp.concatenate([hot[0:32] + spill, hot[32:64]], axis=0)
    hot_parts = lax.all_to_all(hot_main, "rep", split_axis=0, concat_axis=0, tiled=True)
    k = jnp.arange(128, dtype=I32)
    want = 32768 + 32 * node + 4 * (k // 16) + k % 4
    at = jnp.sum(jnp.where(want[:, None] == hot_ids[None, :], jnp.arange(1024, dtype=I32)[None, :], 0), axis=1)
    hot_mem = jnp.take(hot_memory, at, axis=0)
    mem_all = jnp.concatenate([memory, hot_mem], axis=0)
    cot_all = jnp.concatenate([cot_cold, jnp.take(cot_hot, at, axis=0)], axis=0)
    own_mem = lax.dynamic_slice_in_dim(hot_mem, 16 * rep, 16, 0)
    hot_agg, hot_new = call(
        hot_kernel,
        (sds((16, 512), BF16), sds((8, 256), F32)),
        0,
        (hot_parts.reshape(8, 8, 512), own_mem, w_in, w_hid),
    )
    hot_all = lax.all_gather(hot_new[0:4], ("node", "rep"), axis=0, tiled=True)
    new_hot = jnp.take(hot_all, hot_ids - 32768, axis=0)

    block = sds((136, 512), F32)
    keep, give = call(cold_kernel, (sds((4, 136, 512), F32),) * 2, 1, (pos, recv))
    parts = call(add_kernel, (block,) * 4, 1, (pos, keep, swap_core(give)))
    parts = [parts[0]] + [shift_x(parts[d], d) for d in (1, 2, 3)]
    agg = call(agg_kernel, sds((144, 512), BF16), 0, (*parts, hot_agg))
    new_memory, grad = call(
        update_kernel,
        (sds((1024, 256), F32), sds((32, 8, 384), F32)),
        1,
        (pos, *gather_rep(agg), mem_all, cot_all, w_in, w_hid),
        (pltpu.VMEM((1152, 512), BF16), pltpu.VMEM((128, 1024), F32)),
    )

    grad = lax.all_to_all(grad, "node", split_axis=0, concat_axis=0, tiled=True)
    grad = call(piece_kernel, sds((32, 8, 384), F32), 0, (grad,))
    grad = lax.all_to_all(grad, "node", split_axis=0, concat_axis=0, tiled=True)
    grad_in, grad_hid = call(
        place_kernel,
        (sds((512, 768), F32), sds((256, 768), F32)),
        1,
        (pos, *gather_rep(grad[0:24])),
    )
    return (new_memory, new_hot, grad_in, grad_hid)


def solution(mesh):
    in_specs = (
        P("node", None),
        P(),
        P("node", None),
        P(),
        P(("node", "rep")),
        P(("node", "rep")),
        P(("node", "rep")),
        P(("node", "rep"), None),
        P(("node", "rep"), None),
        P(("node", "rep")),
        P(),
        P(),
        P(),
        P(),
        P(),
        P(),
        P(),
    )
    out_specs = (P("node", None), P(), P(), P())
    return jax.shard_map(
        on_device, mesh=mesh, in_specs=in_specs, out_specs=out_specs, check_vma=False
    )
```

```python
import jax
import jax.numpy as jnp
from jax import lax
from jax.experimental import pallas as pl
from jax.experimental.pallas import tpu as pltpu
from jax.sharding import PartitionSpec as P

GRAD_SCALE = 1.0 / 64.0
DEAD = 2.0**100
F32, BF16, I32 = jnp.float32, jnp.bfloat16, jnp.int32
PARAMS = pltpu.CompilerParams(vmem_limit_bytes=48 * 1024 * 1024)
VM = pl.BlockSpec(memory_space=pltpu.VMEM)
SM = pl.BlockSpec(memory_space=pltpu.SMEM)
HB = pl.BlockSpec(memory_space=pl.ANY)


def iota(shape, dim):
    return lax.broadcasted_iota(I32, shape, dim)


def one_hot(mask):
    return jnp.where(mask, 1.0, 0.0).astype(BF16)


def mm(a, b, dims=((1,), (0,))):
    return lax.dot_general(a, b, (dims, ((), ())), preferred_element_type=F32)


def call(body, out_shape, places, args, scratch=(), out_places=None):
    if out_places is None:
        out_places = jax.tree.map(lambda _: VM, out_shape)
    return pl.pallas_call(
        body,
        out_shape=out_shape,
        in_specs=list(places) + [VM] * (len(args) - len(places)),
        out_specs=out_places,
        scratch_shapes=list(scratch),
        compiler_params=PARAMS,
    )(*args)


def column(row):
    return jnp.broadcast_to(row, (8, row.shape[1])).T[:, 0:1]


def cosine(x):
    k = jnp.round(x * 0.15915494309189535)
    r = x - k * 6.28125
    r = r - k * 0.0019350051879882812
    r = r - k * 3.019916e-07
    u = 1.5707963267948966 - jnp.abs(r)
    u2 = u * u
    p = 2.6083159809786593e-06
    for c in (-0.00019810690719168633, 0.0083330785855650902, -0.16666659712791443, 1.0):
        p = p * u2 + c
    return u * p


def message_kernel(
    pos, mem_h, edge_h, w_h, src, times, dst_ref, listed, used, freq, phase, b, send_h, hot,
    mem, edge, w, msgs, out, cols, sems,
):
    loads = [
        pltpu.make_async_copy(h, v, sems.at[i])
        for i, (h, v) in enumerate(((mem_h, mem), (edge_h, edge), (w_h, w)))
    ]
    for c in loads:
        c.start()
    n_ev, step = 1024, 256
    dst = dst_ref[...]
    line = iota((8, n_ev), 0)
    packed = jnp.where(line == 0, src[...], jnp.where(line == 1, times[...], dst))
    cols[...] = packed.T
    slot = iota((32, 32), 0)
    eye = one_hot(slot == iota((32, 32), 1))
    names = listed[...]
    hi = mm(eye, (names >> 5).astype(F32).astype(BF16), ((1,), (1,)))
    lo = mm(eye, (names & 31).astype(F32).astype(BF16), ((1,), (1,)))
    names = jnp.where(slot < used[...], (hi * 32.0 + lo).astype(I32), -1)
    for c in loads:
        c.wait()
    mem16 = mem[...].astype(BF16)
    for e in range(0, n_ev, step):
        at = cols[e : e + step, :]
        src_mem = mm(one_hot(iota((step, 1024), 1) == at[:, 0:1]), mem16).astype(BF16)
        enc = cosine(at[:, 1:2].astype(F32) * freq[...] + phase[...]).astype(BF16)
        raw = jnp.concatenate([src_mem, edge[e : e + step, :], enc], axis=1)
        pre = mm(raw, w[...]) + b[...]
        msgs[e : e + step, :] = (pre * jax.nn.sigmoid(pre)).astype(BF16)
    row = dst & 1023
    facts = jnp.where(line == 0, row >> 5, jnp.where(line == 1, row & 31, jnp.where(line == 2, 1, 0)))
    facts = facts.astype(F32).astype(BF16)
    lane = iota((8, 128), 1)
    stores = []
    for t in range(4):
        pick = jnp.concatenate(
            [one_hot(iota((32, n_ev), 1) == names[:, o : o + 1]) for o in range(8 * t, 8 * t + 8)], axis=0
        )
        moved = mm(pick, msgs[...]).astype(BF16)
        tail = mm(facts, pick, ((1,), (1,)))
        for i in range(8):
            o = 8 * t + i
            for q in range(4):
                out[o, 32 * q : 32 * q + 32, :] = moved[32 * i : 32 * i + 32, 128 * q : 128 * q + 128]
            k = o % 4
            own = tail[:, 128 * (i // 4) : 128 * (i // 4) + 128]
            own = jnp.where((lane >> 5) == k, own, 0.0)
            own = pltpu.roll(own, ((pos[0] & 3) + 4 - k) * 32 & 127, 1)
            out[o, 128:144, :] = jnp.concatenate([own, jnp.zeros((8, 128), F32)], axis=0).astype(BF16)
        here = pl.ds(8 * t, 8)
        stores.append(pltpu.make_async_copy(out.at[here], send_h.at[here], sems.at[3 + t]))
        stores[-1].start()
    window = jnp.where(dst >= 32768, (dst - 32768 - 32 * pos[0] + 1024) & 1023, -1)
    q = iota((96, n_ev), 0)
    block = jnp.where(q < 64, 2 * ((q >> 3) & 3) + ((q >> 5) & 1), 8 + 2 * ((q >> 3) & 1) + ((q >> 4) & 1))
    hit = one_hot(4 * block + (q & 3) == window)
    total = mm(hit, msgs[...])
    count = jnp.sum(hit.astype(F32), axis=1, keepdims=True)
    hot[...] = jnp.where((iota((96, 512), 0) & 7) < 4, total, count)
    for c in stores:
        c.wait()


def cold_kernel(pos, own_h, peer_h, tie, o0, o1_h, o2_h, o3_h, got, msgs, out, sems):
    loads = [pltpu.make_async_copy(h, got.at[i], sems.at[i]) for i, h in enumerate((own_h, peer_h))]
    for c in loads:
        c.start()
    q = iota((512, 128), 0)
    want = (q & 127) + 256 * ((pos[0] + (q >> 7)) & 3) + 128 * pos[1]
    hits = []
    for h in range(2):
        loads[h].wait()
        for g in range(8):
            tail = got[h, 4 * g, 128:144, :].astype(F32)
            for i in range(1, 4):
                tail = tail + got[h, 4 * g + i, 128:144, :].astype(F32)
            row = jnp.where(tail[2:3, :] > 0.5, tail[0:1, :] * 32.0 + tail[1:2, :], -1.0).astype(I32)
            hits.append(one_hot(want == row))
        for s in range(32):
            for k in range(4):
                here = slice(1024 * h + 32 * s, 1024 * h + 32 * s + 32)
                msgs[here, 128 * k : 128 * k + 128] = got[h, s, 32 * k : 32 * k + 32, :]
    hit = jnp.concatenate(hits, axis=1)
    count = mm(jnp.ones((8, 2048), BF16), hit, ((1,), (1,)))
    stores = []
    for n in range(2):
        cols = slice(256 * n, 256 * n + 256)
        total = mm(hit, msgs[:, cols])
        for d in (2, 1, 3, 0):
            here = slice(128 * d, 128 * d + 128)
            to = o0 if d == 0 else out.at[d - 1]
            to[0:128, cols] = total[here, :]
            if n == 0:
                to[128:136, 0:128] = count[:, here]
                to[128:136, 128:256] = jnp.zeros((8, 128), F32)
            else:
                to[128:136, cols] = jnp.zeros((8, 256), F32)
            if d > 0:
                dst = (o1_h, o2_h, o3_h)[d - 1]
                c = pltpu.make_async_copy(out.at[d - 1, :, cols], dst.at[:, cols], sems.at[2 + 3 * n + d - 1])
                c.start()
                stores.append(c)
    for c in stores:
        c.wait()


def agg_kernel(p1_h, p2_h, p3_h, p0, hot, out_h, part, out, sems):
    loads = [pltpu.make_async_copy(h, part.at[i], sems.at[i]) for i, h in enumerate((p1_h, p2_h, p3_h))]
    for c in loads:
        c.start()
    out[128:144, :] = hot[...]
    for c in loads:
        c.wait()
    total = p0[...] + part[0] + part[1] + part[2]
    count = column(total[128:129, 0:128])
    agg = jnp.where(count > 0.0, total[0:128, :] / jnp.maximum(count, 1.0), DEAD)
    out[0:128, :] = agg.astype(BF16)
    store = pltpu.make_async_copy(out, out_h, sems.at[3])
    store.start()
    store.wait()


def gates(agg, mem, w_in, w_hid):
    gi = mm(agg, w_in)
    gh = mm(mem.astype(BF16), w_hid)
    reset = jax.nn.sigmoid(gi[:, 0:256] + gh[:, 0:256])
    update = jax.nn.sigmoid(gi[:, 256:512] + gh[:, 256:512])
    cand = jnp.tanh(gi[:, 512:768] + reset * gh[:, 512:768])
    return reset, update, cand, gh[:, 512:768]


def hot_kernel(p0, p1, p2, p3, mem, w_in, w_hid, agg_out, new_out):
    total = p0[...] + p1[...] + p2[...] + p3[...]
    count = total[4:8, :]
    agg = jnp.where(count > 0.0, total[0:4, :] / jnp.maximum(count, 1.0), DEAD)
    agg = jnp.concatenate([agg, jnp.full((12, 512), DEAD, F32)], axis=0).astype(BF16)
    agg_out[...] = agg
    live = agg[:, 0:256].astype(F32) < DEAD * 0.5
    mem = mem[...]
    wide = agg.astype(F32)
    agg = jnp.where(wide < DEAD * 0.5, wide, 0.0).astype(BF16)
    reset, update, cand, _ = gates(agg, mem, w_in[...], w_hid[...])
    new_out[...] = jnp.where(live, (1.0 - update) * cand + update * mem, mem)[0:8, :]


def hot_place_kernel(ids, rows, out):
    names = column(ids[...]) - 32768
    at = 8 * (names >> 2) + (names & 3)
    full = rows[...]
    hi = full.astype(BF16)
    rest = full - hi.astype(F32)
    mid = rest.astype(BF16)
    low = (rest - mid.astype(F32)).astype(BF16)
    for h in range(0, 1024, 256):
        pick = one_hot(iota((256, 2048), 1) == at[h : h + 256, :])
        out[h : h + 256, :] = mm(pick, hi) + (mm(pick, mid) + mm(pick, low))


def update_kernel(pos, a0, a1, a2, a3, b0, b1, b2, b3, mem, cot, w_in, w_hid, new, grad, agg, acc):
    x, core, rep = pos[0], pos[1], pos[2]
    for group, c in (((a0, a1, a2, a3), core), ((b0, b1, b2, b3), 1 - core)):
        for d, part in enumerate(group):
            block = 2 * ((x - d + 4) & 3) + c
            agg[pl.ds(pl.multiple_of(block * 128, 128), 128), :] = part[0:128, :]
            agg[pl.ds(pl.multiple_of(1024 + block * 16, 16), 16), :] = part[128:144, :]
    k, q = iota((512, 128), 0), iota((512, 128), 1)
    sel_a = one_hot((k == 64 * rep + q) & (q < 64))
    k, q = iota((256, 128), 0), iota((256, 128), 1)
    sel_m = one_hot((k == 32 * rep + q - 64) & (q >= 64) & (q < 96))
    step = 384
    for s in range(0, 1152, step):
        wide = agg[s : s + step, :].astype(F32)
        live = wide[:, 0:1] < DEAD * 0.5
        a = jnp.where(live, wide, 0.0).astype(BF16)
        m = mem[s : s + step, :]
        reset, update, cand, hid_cand = gates(a, m, w_in[...], w_hid[...])
        fresh = jnp.where(live, (1.0 - update) * cand + update * m, m)
        rows = min(step, 1024 - s)
        new[s : s + rows, :] = fresh[0:rows, :]
        g = jnp.where(live, cot[s : s + step, :], 0.0)
        d_cand = g * (1.0 - update) * (1.0 - cand * cand)
        d_upd = g * (m - cand) * update * (1.0 - update)
        d_reset = d_cand * hid_cand * reset * (1.0 - reset)
        left = (mm(a, sel_a) + mm(m.astype(BF16), sel_m)).astype(BF16)
        for j, d in enumerate((d_reset, d_upd, d_cand, d_cand * reset)):
            hi = d.astype(BF16)
            rest = d - hi.astype(F32)
            mid = rest.astype(BF16)
            low = (rest - mid.astype(F32)).astype(BF16)
            dims = ((0,), (0,))
            part = mm(left, hi, dims) + (mm(left, mid, dims) + mm(left, low, dims))
            cols = slice(256 * j, 256 * j + 256)
            if s == 0:
                acc[:, cols] = part
            else:
                acc[:, cols] += part
    total = acc[...] * GRAD_SCALE
    third = jnp.where(iota((128, 256), 0) < 64, total[:, 512:768], total[:, 768:1024])
    total = jnp.concatenate([total[:, 0:512], third], axis=1)
    for p in range(32):
        i, j = p // 2, p % 2
        grad[p] = total[8 * i : 8 * i + 8, 384 * j : 384 * j + 384]


def piece_kernel(parts, out):
    total = parts[0]
    for k in range(1, 32):
        total = total + parts[k]
    for k in range(32):
        out[k] = total


def place_kernel(pos, a0, a1, a2, a3, b0, b1, b2, b3, g_in, g_hid):
    x, core = pos[0], pos[1]
    for group, c in (((a0, a1, a2, a3), core), ((b0, b1, b2, b3), 1 - core)):
        for d, part in enumerate(group):
            block = 2 * ((x - d + 4) & 3) + c
            for p in range(24):
                i, j = p // 2, p % 2
                cols = slice(384 * j, 384 * j + 384)
                if i < 8:
                    g_in[pl.ds(pl.multiple_of(block * 64 + 8 * i, 8), 8), cols] = part[p]
                else:
                    g_hid[pl.ds(pl.multiple_of(block * 32 + 8 * (i - 8), 8), 8), cols] = part[p]


def swap_core(v):
    return lax.ppermute(v, "rep", [(k, k ^ 1) for k in range(8)])


def shift_x(v, d):
    return lax.ppermute(v, "rep", [(k, (k + 2 * d) % 8) for k in range(8)])


def gather_rep(v):
    own = [v] + [shift_x(v, d) for d in (1, 2, 3)]
    return own + [swap_core(u) for u in own]


def on_device(
    memory,
    hot_memory,
    cot_cold,
    cot_hot,
    src_local,
    dst_ids,
    times,
    edge_feat,
    cold_list,
    cold_count,
    hot_ids,
    time_freq,
    time_phase,
    w_msg,
    b_msg,
    w_in,
    w_hid,
):
    node = lax.axis_index("node")
    rep = lax.axis_index("rep")
    pos = jnp.stack([rep // 2, rep % 2, rep]).astype(I32)
    sds = jax.ShapeDtypeStruct

    chip, core = rep // 2, rep % 2
    send, hot = call(
        message_kernel,
        (sds((32, 144, 128), BF16), sds((96, 512), F32)),
        (SM, HB, HB, HB),
        (
            node.astype(I32)[None], memory, edge_feat, w_msg, src_local[None, :], times[None, :],
            dst_ids[None, :], cold_list, cold_count[None, :], time_freq[None, :], time_phase[None, :],
            b_msg[None, :],
        ),
        (
            pltpu.VMEM((1024, 256), F32), pltpu.VMEM((1024, 128), BF16), pltpu.VMEM((512, 512), BF16),
            pltpu.VMEM((1024, 512), BF16), pltpu.VMEM((32, 144, 128), BF16), pltpu.VMEM((1024, 8), I32),
            pltpu.SemaphoreType.DMA((7,)),
        ),
        (HB, VM),
    )
    recv = lax.all_to_all(send, "node", split_axis=0, concat_axis=0, tiled=True)

    spill = lax.ppermute(hot[64:96], "node", [(k, (k + 1) % 32) for k in range(32)]).reshape(2, 2, 8, 512)
    hot = hot[0:64].reshape(2, 4, 8, 512)
    hot = jnp.concatenate([hot[:, 0:2] + spill, hot[:, 2:4]], axis=1)
    got = swap_core(lax.dynamic_index_in_dim(hot, 1 - core, 0, False))
    hot = lax.dynamic_index_in_dim(hot, core, 0, False) + got
    hot = [lax.dynamic_index_in_dim(hot, (chip + d) % 4, 0, False) for d in range(4)]
    hot = [hot[0]] + [shift_x(hot[d], d) for d in (1, 2, 3)]
    k = jnp.arange(128, dtype=I32)
    want = 32768 + 32 * node + 4 * (k // 16) + k % 4
    at = jnp.sum(jnp.where(want[:, None] == hot_ids[None, :], jnp.arange(1024, dtype=I32)[None, :], 0), axis=1)
    hot_mem = jnp.take(hot_memory, at, axis=0, mode="clip")
    mem_all = jnp.concatenate([memory, hot_mem], axis=0)
    cot_all = jnp.concatenate([cot_cold, jnp.take(cot_hot, at, axis=0, mode="clip")], axis=0)
    own_mem = lax.dynamic_slice_in_dim(hot_mem, 16 * rep, 16, 0)
    hot_agg, hot_new = call(
        hot_kernel,
        (sds((16, 512), BF16), sds((8, 256), F32)),
        (),
        (*hot, own_mem, w_in, w_hid),
    )
    hot_all = lax.all_gather(hot_new, ("node", "rep"), axis=0, tiled=True)
    new_hot = call(hot_place_kernel, sds((1024, 256), F32), (), (hot_ids[None, :], hot_all))

    recv, hot_agg, mem_all, cot_all = lax.optimization_barrier((recv, hot_agg, mem_all, cot_all))
    block = sds((136, 512), F32)
    parts = call(
        cold_kernel,
        (block,) * 4,
        (SM, HB, HB, HB),
        (pos, recv, swap_core(recv), hot_agg),
        (
            pltpu.VMEM((2, 32, 144, 128), BF16), pltpu.VMEM((2048, 512), BF16), pltpu.VMEM((3, 136, 512), F32),
            pltpu.SemaphoreType.DMA((8,)),
        ),
        (VM, HB, HB, HB),
    )
    parts = [parts[0]] + [shift_x(parts[d], d) for d in (1, 2, 3)]
    agg = call(
        agg_kernel,
        sds((144, 512), BF16),
        (HB, HB, HB),
        (*parts[1:], parts[0], hot_agg),
        (pltpu.VMEM((3, 136, 512), F32), pltpu.VMEM((144, 512), BF16), pltpu.SemaphoreType.DMA((4,))),
        HB,
    )
    new_memory, grad = call(
        update_kernel,
        (sds((1024, 256), F32), sds((32, 8, 384), F32)),
        (SM,),
        (pos, *gather_rep(agg), mem_all, cot_all, w_in, w_hid),
        (pltpu.VMEM((1152, 512), BF16), pltpu.VMEM((128, 1024), F32)),
    )

    grad = lax.all_to_all(grad, "node", split_axis=0, concat_axis=0, tiled=True)
    grad = call(piece_kernel, sds((32, 8, 384), F32), (), (grad,))
    grad = lax.all_to_all(grad, "node", split_axis=0, concat_axis=0, tiled=True)
    grad_in, grad_hid = call(
        place_kernel,
        (sds((512, 768), F32), sds((256, 768), F32)),
        (SM,),
        (pos, *gather_rep(grad[0:24])),
    )
    return (new_memory, new_hot, grad_in, grad_hid)


def solution(mesh):
    in_specs = (
        P("node", None),
        P(),
        P("node", None),
        P(),
        P(("node", "rep")),
        P(("node", "rep")),
        P(("node", "rep")),
        P(("node", "rep"), None),
        P(("node", "rep"), None),
        P(("node", "rep")),
        P(),
        P(),
        P(),
        P(),
        P(),
        P(),
        P(),
    )
    out_specs = (P("node", None), P(), P(), P())
    return jax.shard_map(
        on_device, mesh=mesh, in_specs=in_specs, out_specs=out_specs, check_vma=False
    )
```

```python
import jax
import jax.numpy as jnp
from jax import lax
from jax.experimental import pallas as pl
from jax.experimental.pallas import tpu as pltpu
from jax.sharding import PartitionSpec as P

GRAD_SCALE = 1.0 / 64.0
DEAD = 2.0**100
F32, BF16, I32 = jnp.float32, jnp.bfloat16, jnp.int32
VM = pl.BlockSpec(memory_space=pltpu.VMEM)
SM = pl.BlockSpec(memory_space=pltpu.SMEM)
HB = pl.BlockSpec(memory_space=pltpu.HBM)
ANY = pl.BlockSpec(memory_space=pl.ANY)


def iota(shape, dim):
    return lax.broadcasted_iota(I32, shape, dim)


def one_hot(mask):
    return jnp.where(mask, 1.0, 0.0).astype(BF16)


def mm(a, b, dims=((1,), (0,))):
    return lax.dot_general(a, b, (dims, ((), ())), preferred_element_type=F32)


def call(body, out_shape, places, args, scratch=(), out_places=None, mib=48):
    if out_places is None:
        out_places = jax.tree.map(lambda _: VM, out_shape)
    return pl.pallas_call(
        body,
        out_shape=out_shape,
        in_specs=list(places) + [VM] * (len(args) - len(places)),
        out_specs=out_places,
        scratch_shapes=list(scratch),
        compiler_params=pltpu.CompilerParams(vmem_limit_bytes=mib * 1024 * 1024),
    )(*args)


def column(row):
    return jnp.broadcast_to(row, (8, row.shape[1])).T[:, 0:1]


def cosine(x):
    k = jnp.round(x * 0.15915494309189535)
    r = x - k * 6.28125
    r = r - k * 0.0019350051879882812
    r = r - k * 3.019916e-07
    u = 1.5707963267948966 - jnp.abs(r)
    u2 = u * u
    p = 2.6083159809786593e-06
    for c in (-0.00019810690719168633, 0.0083330785855650902, -0.16666659712791443, 1.0):
        p = p * u2 + c
    return u * p


def message_kernel(
    pos, mem_h, edge_h, w_h, src_h, times_h, dst_h, listed_h, used_h, freq_h, phase_h, b_h, send_h, hot,
    mem, edge, w, src, times, dst_v, listed, used, freq, phase, b, msgs, out, cols, sems,
):
    loads = [
        pltpu.make_async_copy(h, v, sems.at[i])
        for i, (h, v) in enumerate(
            (
                (src_h, src), (times_h, times), (dst_h, dst_v), (listed_h, listed), (used_h, used),
                (freq_h, freq), (phase_h, phase), (b_h, b), (mem_h, mem), (edge_h, edge), (w_h, w),
            )
        )
    ]
    for c in loads:
        c.start()
    for c in loads[:8]:
        c.wait()
    n_ev, step = 1024, 256
    dst = dst_v[...]
    line = iota((8, n_ev), 0)
    packed = jnp.where(line == 0, src[...], jnp.where(line == 1, times[...], dst))
    cols[...] = packed.T
    slot = iota((32, 32), 0)
    eye = one_hot(slot == iota((32, 32), 1))
    names = listed[...]
    hi = mm(eye, (names >> 5).astype(F32).astype(BF16), ((1,), (1,)))
    lo = mm(eye, (names & 31).astype(F32).astype(BF16), ((1,), (1,)))
    names = jnp.where(slot < used[...], (hi * 32.0 + lo).astype(I32), -1)
    for c in loads[8:]:
        c.wait()
    mem16 = mem[...].astype(BF16)
    for e in range(0, n_ev, step):
        at = cols[e : e + step, :]
        src_mem = mm(one_hot(iota((step, 1024), 1) == at[:, 0:1]), mem16).astype(BF16)
        enc = cosine(at[:, 1:2].astype(F32) * freq[...] + phase[...]).astype(BF16)
        raw = jnp.concatenate([src_mem, edge[e : e + step, :], enc], axis=1)
        pre = mm(raw, w[...]) + b[...]
        msgs[e : e + step, :] = (pre * jax.nn.sigmoid(pre)).astype(BF16)
    row = dst & 1023
    facts = jnp.where(line == 0, row >> 5, jnp.where(line == 1, row & 31, jnp.where(line == 2, 1, 0)))
    facts = facts.astype(F32).astype(BF16)
    lane = iota((8, 128), 1)
    stores = []
    for t in range(4):
        pick = jnp.concatenate(
            [one_hot(iota((32, n_ev), 1) == names[:, o : o + 1]) for o in range(8 * t, 8 * t + 8)], axis=0
        )
        moved = mm(pick, msgs[...]).astype(BF16)
        tail = mm(facts, pick, ((1,), (1,)))
        for i in range(8):
            o = 8 * t + i
            for q in range(4):
                out[o, 32 * q : 32 * q + 32, :] = moved[32 * i : 32 * i + 32, 128 * q : 128 * q + 128]
            k = o % 4
            own = tail[:, 128 * (i // 4) : 128 * (i // 4) + 128]
            own = jnp.where((lane >> 5) == k, own, 0.0)
            own = pltpu.roll(own, ((pos[0] & 3) + 4 - k) * 32 & 127, 1)
            out[o, 128:144, :] = jnp.concatenate([own, jnp.zeros((8, 128), F32)], axis=0).astype(BF16)
        here = pl.ds(8 * t, 8)
        stores.append(pltpu.make_async_copy(out.at[here], send_h.at[here], sems.at[11 + t]))
        stores[-1].start()
    window = jnp.where(dst >= 32768, (dst - 32768 - 32 * pos[0] + 1024) & 1023, -1)
    q = iota((96, n_ev), 0)
    block = jnp.where(q < 64, 2 * ((q >> 3) & 3) + ((q >> 5) & 1), 8 + 2 * ((q >> 3) & 1) + ((q >> 4) & 1))
    hit = one_hot(4 * block + (q & 3) == window)
    total = mm(hit, msgs[...])
    count = jnp.sum(hit.astype(F32), axis=1, keepdims=True)
    hot[...] = jnp.where((iota((96, 512), 0) & 7) < 4, total, count)
    for c in stores:
        c.wait()


def cold_kernel(pos, own, peer, hot, spill, o0, o1_h, o2_h, o3_h, msgs, out, sems):
    got = (own, peer)
    q = iota((512, 128), 0)
    want = (q & 127) + 256 * ((pos[0] + (q >> 7)) & 3) + 128 * pos[1]
    hits = []
    for h in range(2):
        for g in range(8):
            tail = got[h][4 * g, 128:144, :].astype(F32)
            for i in range(1, 4):
                tail = tail + got[h][4 * g + i, 128:144, :].astype(F32)
            row = jnp.where(tail[2:3, :] > 0.5, tail[0:1, :] * 32.0 + tail[1:2, :], -1.0).astype(I32)
            hits.append(one_hot(want == row))
        for s in range(32):
            for k in range(4):
                here = slice(1024 * h + 32 * s, 1024 * h + 32 * s + 32)
                msgs[here, 128 * k : 128 * k + 128] = got[h][s, 32 * k : 32 * k + 32, :]
    hit = jnp.concatenate(hits, axis=1)
    count = mm(jnp.ones((8, 2048), BF16), hit, ((1,), (1,)))
    stores = []
    for n in range(2):
        cols = slice(256 * n, 256 * n + 256)
        total = mm(hit, msgs[:, cols])
        for d in (2, 1, 3, 0):
            here = slice(128 * d, 128 * d + 128)
            to = o0 if d == 0 else out.at[d - 1]
            to[0:128, cols] = total[here, :]
            j = (pos[0] + d) & 3
            tile = hot[j, :, cols] + jnp.where(j < 2, 1.0, 0.0) * spill[j & 1, :, cols]
            if n == 0:
                rows = jnp.concatenate([count[:, here], tile[:, 128:256]], axis=1)
                tile = jnp.where((iota((8, 256), 0) >= 4) & (iota((8, 256), 1) < 128), rows, tile)
            to[128:136, cols] = tile
            if d > 0:
                dst = (o1_h, o2_h, o3_h)[d - 1]
                c = pltpu.make_async_copy(out.at[d - 1, :, cols], dst.at[:, cols], sems.at[3 * n + d - 1])
                c.start()
                stores.append(c)
    for c in stores:
        c.wait()


def agg_kernel(p1_h, p2_h, p3_h, p0, out_h, part, out, sems):
    loads = [pltpu.make_async_copy(h, part.at[i], sems.at[i]) for i, h in enumerate((p1_h, p2_h, p3_h))]
    for c in loads:
        c.start()
    for c in loads:
        c.wait()
    total = p0[...] + part[0] + part[1] + part[2]
    count = column(total[132:133, 0:128])
    agg = jnp.where(count > 0.0, total[0:128, :] / jnp.maximum(count, 1.0), DEAD)
    out[0:128, :] = agg.astype(BF16)
    count = total[132:136, 128:129]
    agg = jnp.where(count > 0.0, total[128:132, :] / jnp.maximum(count, 1.0), DEAD)
    out[128:144, :] = jnp.concatenate([agg, jnp.full((12, 512), DEAD, F32)], axis=0).astype(BF16)
    store = pltpu.make_async_copy(out, out_h, sems.at[3])
    store.start()
    store.wait()


def gates(agg, mem, w_in, w_hid):
    gi = mm(agg, w_in)
    gh = mm(mem.astype(BF16), w_hid)
    reset = jax.nn.sigmoid(gi[:, 0:256] + gh[:, 0:256])
    update = jax.nn.sigmoid(gi[:, 256:512] + gh[:, 256:512])
    cand = jnp.tanh(gi[:, 512:768] + reset * gh[:, 512:768])
    return reset, update, cand, gh[:, 512:768]


def hot_place_kernel(pos, ids, a0, a1, a2, a3, b0, b1, b2, b3, out, rows):
    x, core = pos[0], pos[1]
    for group, c in (((a0, a1, a2, a3), core), ((b0, b1, b2, b3), 1 - core)):
        for d, part in enumerate(group):
            block = 2 * ((x - d + 4) & 3) + c
            for n in range(32):
                rows[block, 4 * n : 4 * n + 4, 0:128] = part[n, 0:4, :]
                rows[block, 4 * n : 4 * n + 4, 128:256] = part[n, 4:8, :]
    name = column(ids[...]) - 32768
    at = 128 * ((name >> 2) & 7) + 4 * (name >> 5) + (name & 3)
    full = rows[...].reshape(1024, 256)
    hi = full.astype(BF16)
    rest = full - hi.astype(F32)
    mid = rest.astype(BF16)
    low = (rest - mid.astype(F32)).astype(BF16)
    for h in range(0, 1024, 256):
        pick = one_hot(iota((256, 1024), 1) == at[h : h + 256, :])
        out[h : h + 256, :] = mm(pick, hi) + (mm(pick, mid) + mm(pick, low))


def update_kernel(pos, a0, a1, a2, a3, b0, b1, b2, b3, mem, cot, w_in, w_hid, new, grad, agg, acc, hot):
    x, core, rep = pos[0], pos[1], pos[2]
    for group, c in (((a0, a1, a2, a3), core), ((b0, b1, b2, b3), 1 - core)):
        for d, part in enumerate(group):
            block = 2 * ((x - d + 4) & 3) + c
            agg[pl.ds(pl.multiple_of(block * 128, 128), 128), :] = part[0:128, :]
            agg[pl.ds(pl.multiple_of(1024 + block * 16, 16), 16), :] = part[128:144, :]
    k, q = iota((512, 128), 0), iota((512, 128), 1)
    sel_a = one_hot((k == 64 * rep + q) & (q < 64))
    k, q = iota((256, 128), 0), iota((256, 128), 1)
    sel_m = one_hot((k == 32 * rep + q - 64) & (q >= 64) & (q < 96))
    step = 384
    for s in range(0, 1152, step):
        wide = agg[s : s + step, :].astype(F32)
        live = wide[:, 0:1] < DEAD * 0.5
        a = jnp.where(live, wide, 0.0).astype(BF16)
        m = mem[s : s + step, :]
        reset, update, cand, hid_cand = gates(a, m, w_in[...], w_hid[...])
        fresh = jnp.where(live, (1.0 - update) * cand + update * m, m)
        rows = min(step, 1024 - s)
        new[s : s + rows, :] = fresh[0:rows, :]
        if rows < step:
            hot[...] = fresh[rows:step, :]
        g = jnp.where(live, cot[s : s + step, :], 0.0)
        d_cand = g * (1.0 - update) * (1.0 - cand * cand)
        d_upd = g * (m - cand) * update * (1.0 - update)
        d_reset = d_cand * hid_cand * reset * (1.0 - reset)
        left = (mm(a, sel_a) + mm(m.astype(BF16), sel_m)).astype(BF16)
        for j, d in enumerate((d_reset, d_upd, d_cand, d_cand * reset)):
            hi = d.astype(BF16)
            rest = d - hi.astype(F32)
            mid = rest.astype(BF16)
            low = (rest - mid.astype(F32)).astype(BF16)
            dims = ((0,), (0,))
            part = mm(left, hi, dims) + (mm(left, mid, dims) + mm(left, low, dims))
            cols = slice(256 * j, 256 * j + 256)
            if s == 0:
                acc[:, cols] = part
            else:
                acc[:, cols] += part
    total = acc[...] * GRAD_SCALE
    third = jnp.where(iota((128, 256), 0) < 64, total[:, 512:768], total[:, 768:1024])
    total = jnp.concatenate([total[:, 0:512], third], axis=1)
    own = hot[pl.ds(pl.multiple_of(16 * rep, 16), 8), :]
    own = jnp.concatenate([own[0:4, 0:128], own[0:4, 128:256]], axis=0)
    for p in range(32):
        i, j = p // 2, p % 2
        grad[p, :, 0:384] = total[8 * i : 8 * i + 8, 384 * j : 384 * j + 384]
        grad[p, :, 384:512] = own


def piece_kernel(parts, out, hot):
    total = parts[0, :, 0:384]
    for k in range(1, 32):
        total = total + parts[k, :, 0:384]
    for k in range(32):
        out[k] = total
        hot[k] = parts[k, :, 384:512]


def place_kernel(pos, a0, a1, a2, a3, b0, b1, b2, b3, g_in, g_hid):
    x, core = pos[0], pos[1]
    for group, c in (((a0, a1, a2, a3), core), ((b0, b1, b2, b3), 1 - core)):
        for d, part in enumerate(group):
            block = 2 * ((x - d + 4) & 3) + c
            for p in range(24):
                i, j = p // 2, p % 2
                cols = slice(384 * j, 384 * j + 384)
                if i < 8:
                    g_in[pl.ds(pl.multiple_of(block * 64 + 8 * i, 8), 8), cols] = part[p]
                else:
                    g_hid[pl.ds(pl.multiple_of(block * 32 + 8 * (i - 8), 8), 8), cols] = part[p]


def swap_core(v):
    return lax.ppermute(v, "rep", [(k, k ^ 1) for k in range(8)])


def shift_x(v, d):
    return lax.ppermute(v, "rep", [(k, (k + 2 * d) % 8) for k in range(8)])


def gather_rep(v):
    own = [v] + [shift_x(v, d) for d in (1, 2, 3)]
    return own + [swap_core(u) for u in own]


def on_device(
    memory,
    hot_memory,
    cot_cold,
    cot_hot,
    src_local,
    dst_ids,
    times,
    edge_feat,
    cold_list,
    cold_count,
    hot_ids,
    time_freq,
    time_phase,
    w_msg,
    b_msg,
    w_in,
    w_hid,
):
    node = lax.axis_index("node")
    rep = lax.axis_index("rep")
    pos = jnp.stack([rep // 2, rep % 2, rep]).astype(I32)
    sds = jax.ShapeDtypeStruct

    chip, core = rep // 2, rep % 2
    send, hot = call(
        message_kernel,
        (sds((32, 144, 128), BF16), sds((96, 512), F32)),
        (SM,) + (HB,) * 11,
        (
            node.astype(I32)[None], memory, edge_feat, w_msg, src_local[None, :], times[None, :],
            dst_ids[None, :], cold_list, cold_count[None, :], time_freq[None, :], time_phase[None, :],
            b_msg[None, :],
        ),
        (
            pltpu.VMEM((1024, 256), F32), pltpu.VMEM((1024, 128), BF16), pltpu.VMEM((512, 512), BF16),
            pltpu.VMEM((1, 1024), I32), pltpu.VMEM((1, 1024), I32), pltpu.VMEM((1, 1024), I32),
            pltpu.VMEM((32, 32), I32), pltpu.VMEM((1, 32), I32), pltpu.VMEM((1, 128), F32),
            pltpu.VMEM((1, 128), F32), pltpu.VMEM((1, 512), F32),
            pltpu.VMEM((1024, 512), BF16), pltpu.VMEM((32, 144, 128), BF16), pltpu.VMEM((1024, 8), I32),
            pltpu.SemaphoreType.DMA((15,)),
        ),
        (ANY, VM),
        63,
    )
    recv = lax.all_to_all(send, "node", split_axis=0, concat_axis=0, tiled=True)

    hot = hot + swap_core(hot)
    spill = lax.dynamic_slice_in_dim(hot, 64 + 16 * core, 16, 0)
    spill = lax.ppermute(spill, "node", [(k, (k + 1) % 32) for k in range(32)])
    hot = lax.dynamic_slice_in_dim(hot, 32 * core, 32, 0)
    k = jnp.arange(128, dtype=I32)
    want = 32768 + 32 * node + 4 * (k // 16) + k % 4
    at = jnp.sum(jnp.where(want[:, None] == hot_ids[None, :], jnp.arange(1024, dtype=I32)[None, :], 0), axis=1)
    mem_all = jnp.concatenate([memory, jnp.take(hot_memory, at, axis=0, mode="clip")], axis=0)
    cot_all = jnp.concatenate([cot_cold, jnp.take(cot_hot, at, axis=0, mode="clip")], axis=0)

    recv, spill, mem_all, cot_all = lax.optimization_barrier((recv, spill, mem_all, cot_all))
    block = sds((136, 512), F32)
    parts = call(
        cold_kernel,
        (block,) * 4,
        (SM,),
        (pos, recv, swap_core(recv), hot.reshape(4, 8, 512), spill.reshape(2, 8, 512)),
        (pltpu.VMEM((2048, 512), BF16), pltpu.VMEM((3, 136, 512), F32), pltpu.SemaphoreType.DMA((6,))),
        (VM, ANY, ANY, ANY),
    )
    parts = [parts[0]] + [shift_x(parts[d], d) for d in (1, 2, 3)]
    agg = call(
        agg_kernel,
        sds((144, 512), BF16),
        (ANY, ANY, ANY),
        (*parts[1:], parts[0]),
        (pltpu.VMEM((3, 136, 512), F32), pltpu.VMEM((144, 512), BF16), pltpu.SemaphoreType.DMA((4,))),
        ANY,
    )
    new_memory, grad = call(
        update_kernel,
        (sds((1024, 256), F32), sds((32, 8, 512), F32)),
        (SM,),
        (pos, *gather_rep(agg), mem_all, cot_all, w_in, w_hid),
        (pltpu.VMEM((1152, 512), BF16), pltpu.VMEM((128, 1024), F32), pltpu.VMEM((128, 256), F32)),
    )

    grad = lax.all_to_all(grad, "node", split_axis=0, concat_axis=0, tiled=True)
    grad, hot_new = call(piece_kernel, (sds((32, 8, 384), F32), sds((32, 8, 128), F32)), (), (grad,))
    grad = lax.all_to_all(grad, "node", split_axis=0, concat_axis=0, tiled=True)
    hot_parts = gather_rep(hot_new)
    grad, hot_parts = lax.optimization_barrier((grad, hot_parts))
    new_hot = call(
        hot_place_kernel,
        sds((1024, 256), F32),
        (SM,),
        (pos, hot_ids[None, :], *hot_parts),
        (pltpu.VMEM((8, 128, 256), F32),),
    )
    grad_in, grad_hid = call(
        place_kernel,
        (sds((512, 768), F32), sds((256, 768), F32)),
        (SM,),
        (pos, *gather_rep(grad[0:24])),
    )
    return (new_memory, new_hot, grad_in, grad_hid)


def solution(mesh):
    in_specs = (
        P("node", None),
        P(),
        P("node", None),
        P(),
        P(("node", "rep")),
        P(("node", "rep")),
        P(("node", "rep")),
        P(("node", "rep"), None),
        P(("node", "rep"), None),
        P(("node", "rep")),
        P(),
        P(),
        P(),
        P(),
        P(),
        P(),
        P(),
    )
    out_specs = (P("node", None), P(), P(), P())
    return jax.shard_map(
        on_device, mesh=mesh, in_specs=in_specs, out_specs=out_specs, check_vma=False
    )
```

```python
import functools

import jax
import jax.numpy as jnp
from jax import lax
from jax.experimental import pallas as pl
from jax.experimental.pallas import tpu as pltpu
from jax.sharding import PartitionSpec as P

GRAD_SCALE = 1.0 / 64.0
DEAD = 2.0**100
F32, BF16, I32 = jnp.float32, jnp.bfloat16, jnp.int32
VM = pl.BlockSpec(memory_space=pltpu.VMEM)
SM = pl.BlockSpec(memory_space=pltpu.SMEM)
HB = pl.BlockSpec(memory_space=pltpu.HBM)
ANY = pl.BlockSpec(memory_space=pl.ANY)


def iota(shape, dim):
    return lax.broadcasted_iota(I32, shape, dim)


def one_hot(mask):
    return jnp.where(mask, 1.0, 0.0).astype(BF16)


def mm(a, b, dims=((1,), (0,))):
    return lax.dot_general(a, b, (dims, ((), ())), preferred_element_type=F32)


def call(body, out_shape, places, args, scratch=(), out_places=None, mib=48):
    if out_places is None:
        out_places = jax.tree.map(lambda _: VM, out_shape)
    return pl.pallas_call(
        body,
        out_shape=out_shape,
        in_specs=list(places) + [VM] * (len(args) - len(places)),
        out_specs=out_places,
        scratch_shapes=list(scratch),
        compiler_params=pltpu.CompilerParams(vmem_limit_bytes=mib * 1024 * 1024),
    )(*args)


def column(row):
    return jnp.broadcast_to(row, (8, row.shape[1])).T[:, 0:1]


def cosine(x):
    k = jnp.round(x * 0.15915494309189535)
    r = x - k * 6.28125
    r = r - k * 0.0019350051879882812
    r = r - k * 3.019916e-07
    u = 1.5707963267948966 - jnp.abs(r)
    u2 = u * u
    p = 2.6083159809786593e-06
    for c in (-0.00019810690719168633, 0.0083330785855650902, -0.16666659712791443, 1.0):
        p = p * u2 + c
    return u * p


def message_kernel(
    pos, mem_h, edge_h, w_h, src_h, times_h, dst_h, listed_h, used_h, freq_h, phase_h, b_h, send_h, hot,
    mem, edge, w, src, times, dst_v, listed, used, freq, phase, b, encs, msgs, out, cols, sems,
):
    loads = [
        pltpu.make_async_copy(h, v, sems.at[i])
        for i, (h, v) in enumerate(
            (
                (src_h, src), (times_h, times), (dst_h, dst_v), (listed_h, listed), (used_h, used),
                (freq_h, freq), (phase_h, phase), (b_h, b), (mem_h, mem), (edge_h, edge), (w_h, w),
            )
        )
    ]
    for c in loads:
        c.start()
    for c in loads[:8]:
        c.wait()
    n_ev, step = 1024, 256
    dst = dst_v[...]
    line = iota((8, n_ev), 0)
    packed = jnp.where(line == 0, src[...], jnp.where(line == 1, times[...], dst))
    cols[...] = packed.T
    slot = iota((32, 32), 0)
    eye = one_hot(slot == iota((32, 32), 1))
    names = listed[...]
    hi = mm(eye, (names >> 5).astype(F32).astype(BF16), ((1,), (1,)))
    lo = mm(eye, (names & 31).astype(F32).astype(BF16), ((1,), (1,)))
    names = jnp.where(slot < used[...], (hi * 32.0 + lo).astype(I32), -1)
    encs[...] = cosine(cols[:, 1:2].astype(F32) * freq[...] + phase[...]).astype(BF16)
    for c in loads[8:]:
        c.wait()
    mem16 = mem[...].astype(BF16)
    for e in range(0, n_ev, step):
        at = cols[e : e + step, :]
        src_mem = mm(one_hot(iota((step, 1024), 1) == at[:, 0:1]), mem16).astype(BF16)
        raw = jnp.concatenate([src_mem, edge[e : e + step, :], encs[e : e + step, :]], axis=1)
        pre = mm(raw, w[...]) + b[...]
        msgs[e : e + step, :] = (pre * jax.nn.sigmoid(pre)).astype(BF16)
    row = dst & 1023
    facts = jnp.where(line == 0, row >> 5, jnp.where(line == 1, row & 31, jnp.where(line == 2, 1, 0)))
    facts = facts.astype(F32).astype(BF16)
    lane = iota((8, 128), 1)
    stores = []
    for t in range(4):
        pick = jnp.concatenate(
            [one_hot(iota((32, n_ev), 1) == names[:, o : o + 1]) for o in range(8 * t, 8 * t + 8)], axis=0
        )
        moved = mm(pick, msgs[...]).astype(BF16)
        tail = mm(facts, pick, ((1,), (1,)))
        for i in range(8):
            o = 8 * t + i
            for q in range(4):
                out[o, 32 * q : 32 * q + 32, :] = moved[32 * i : 32 * i + 32, 128 * q : 128 * q + 128]
            k = o % 4
            own = tail[:, 128 * (i // 4) : 128 * (i // 4) + 128]
            own = jnp.where((lane >> 5) == k, own, 0.0)
            own = pltpu.roll(own, ((pos[0] & 3) + 4 - k) * 32 & 127, 1)
            out[o, 128:144, :] = jnp.concatenate([own, jnp.zeros((8, 128), F32)], axis=0).astype(BF16)
        here = pl.ds(8 * t, 8)
        stores.append(pltpu.make_async_copy(out.at[here], send_h.at[here], sems.at[11 + t]))
        stores[-1].start()
    window = jnp.where(dst >= 32768, (dst - 32768 - 32 * pos[0] + 1024) & 1023, -1)
    q = iota((96, n_ev), 0)
    block = jnp.where(q < 64, 2 * ((q >> 3) & 3) + ((q >> 5) & 1), 8 + 2 * ((q >> 3) & 1) + ((q >> 4) & 1))
    hit = one_hot(4 * block + (q & 3) == window)
    total = mm(hit, msgs[...])
    count = jnp.sum(hit.astype(F32), axis=1, keepdims=True)
    hot[...] = jnp.where((iota((96, 512), 0) & 7) < 4, total, count)
    for c in stores:
        c.wait()


def cold_kernel(pos, own, peer, hot, spill, o0, o1, o2, o3):
    q = iota((512, 128), 0)
    want = (q & 127) + 256 * ((pos[0] + (q >> 7)) & 3) + 128 * pos[1]
    hits = []
    for got in (own, peer):
        for g in range(8):
            tail = got[4 * g, 128:144, :].astype(F32)
            for i in range(1, 4):
                tail = tail + got[4 * g + i, 128:144, :].astype(F32)
            row = jnp.where(tail[2:3, :] > 0.5, tail[0:1, :] * 32.0 + tail[1:2, :], -1.0).astype(I32)
            hits.append(one_hot(want == row))
    hit = jnp.concatenate(hits, axis=1)
    count = mm(jnp.ones((8, 2048), BF16), hit, ((1,), (1,)))
    for n in range(2):
        cols = slice(256 * n, 256 * n + 256)
        msgs = jnp.concatenate(
            [
                jnp.concatenate(
                    [got[:, 32 * k : 32 * k + 32, :].reshape(1024, 128) for k in (2 * n, 2 * n + 1)], axis=1
                )
                for got in (own, peer)
            ],
            axis=0,
        )
        total = mm(hit, msgs)
        for d, to in enumerate((o0, o1, o2, o3)):
            here = slice(128 * d, 128 * d + 128)
            to[0:128, cols] = total[here, :]
            j = (pos[0] + d) & 3
            tile = hot[4 * pos[1] + j, :, cols] + jnp.where(j < 2, 1.0, 0.0) * spill[j & 1, :, cols]
            if n == 0:
                rows = jnp.concatenate([count[:, here], tile[:, 128:256]], axis=1)
                tile = jnp.where((iota((8, 256), 0) >= 4) & (iota((8, 256), 1) < 128), rows, tile)
            to[128:136, cols] = tile


def agg_kernel(p1_h, p2_h, p3_h, p0, out_h, part, out, sems):
    loads = [pltpu.make_async_copy(h, part.at[i], sems.at[i]) for i, h in enumerate((p1_h, p2_h, p3_h))]
    for c in loads:
        c.start()
    for c in loads:
        c.wait()
    total = p0[...] + part[0] + part[1] + part[2]
    count = column(total[132:133, 0:128])
    agg = jnp.where(count > 0.0, total[0:128, :] / jnp.maximum(count, 1.0), DEAD)
    out[0:128, :] = agg.astype(BF16)
    count = total[132:136, 128:129]
    agg = jnp.where(count > 0.0, total[128:132, :] / jnp.maximum(count, 1.0), DEAD)
    out[128:144, :] = jnp.concatenate([agg, jnp.full((12, 512), DEAD, F32)], axis=0).astype(BF16)
    store = pltpu.make_async_copy(out, out_h, sems.at[3])
    store.start()
    store.wait()


def gates(agg, mem, w_in, w_hid):
    gi = mm(agg, w_in)
    gh = mm(mem.astype(BF16), w_hid)
    reset = jax.nn.sigmoid(gi[:, 0:256] + gh[:, 0:256])
    update = jax.nn.sigmoid(gi[:, 256:512] + gh[:, 256:512])
    cand = jnp.tanh(gi[:, 512:768] + reset * gh[:, 512:768])
    return reset, update, cand, gh[:, 512:768]


def hot_place_kernel(pos, ids, a0, a1, a2, a3, b0, b1, b2, b3, out, rows):
    x, core = pos[0], pos[1]
    for group, c in (((a0, a1, a2, a3), core), ((b0, b1, b2, b3), 1 - core)):
        for d, part in enumerate(group):
            block = 2 * ((x - d + 4) & 3) + c
            for n in range(32):
                rows[block, 4 * n : 4 * n + 4, 0:128] = part[n, 0:4, :]
                rows[block, 4 * n : 4 * n + 4, 128:256] = part[n, 4:8, :]
    name = column(ids[...]) - 32768
    at = 128 * ((name >> 2) & 7) + 4 * (name >> 5) + (name & 3)
    full = rows[...].reshape(1024, 256)
    hi = full.astype(BF16)
    rest = full - hi.astype(F32)
    mid = rest.astype(BF16)
    low = (rest - mid.astype(F32)).astype(BF16)
    for h in range(0, 1024, 256):
        pick = one_hot(iota((256, 1024), 1) == at[h : h + 256, :])
        out[h : h + 256, :] = mm(pick, hi) + (mm(pick, mid) + mm(pick, low))


def update_kernel(ds, last, pos, *refs):
    parts, refs = refs[: 2 * len(ds)], refs[2 * len(ds) :]
    mem, cot, hot_mem, hot_cot, w_in, w_hid = refs[:6]
    if last:
        own_new, own_hot, own_acc, new, grad, acc = refs[6:]
        acc[...] = own_acc[...]
        new[pl.ds(pl.multiple_of(256 * pos[0], 256), 256), :] = own_new[...]
    else:
        new, hot, acc = refs[6:]
    x, core, rep = pos[0], pos[1], pos[2]
    k, q = iota((512, 128), 0), iota((512, 128), 1)
    sel_a = one_hot((k == 64 * rep + q) & (q < 64))
    k, q = iota((256, 128), 0), iota((256, 128), 1)
    sel_m = one_hot((k == 32 * rep + q - 64) & (q >= 64) & (q < 96))
    for i, d in enumerate(ds):
        chip = (x - d + 4) & 3
        at = pl.ds(pl.multiple_of(256 * chip, 256), 256)
        hot_at = pl.ds(pl.multiple_of(32 * chip, 32), 32)
        mine, other = parts[2 * i][...], parts[2 * i + 1][...]
        low = jnp.where(core == 0, mine, other)
        high = jnp.where(core == 0, other, mine)
        wide = jnp.concatenate([low[0:128], high[0:128], low[128:144], high[128:144]], axis=0).astype(F32)
        live = wide[:, 0:1] < DEAD * 0.5
        a = jnp.where(live, wide, 0.0).astype(BF16)
        m = jnp.concatenate([mem[at, :], hot_mem[hot_at, :]], axis=0)
        reset, update, cand, hid_cand = gates(a, m, w_in[...], w_hid[...])
        fresh = jnp.where(live, (1.0 - update) * cand + update * m, m)
        if last:
            new[at, :] = fresh[0:256, :]
        else:
            new[...] = fresh[0:256, :]
            own = jnp.where(core == 0, fresh[256:264, :], fresh[272:280, :])
            hot[...] = jnp.concatenate([own[0:4, 0:128], own[0:4, 128:256]], axis=0)
        g = jnp.where(live, jnp.concatenate([cot[at, :], hot_cot[hot_at, :]], axis=0), 0.0)
        d_cand = g * (1.0 - update) * (1.0 - cand * cand)
        d_upd = g * (m - cand) * update * (1.0 - update)
        d_reset = d_cand * hid_cand * reset * (1.0 - reset)
        left = (mm(a, sel_a) + mm(m.astype(BF16), sel_m)).astype(BF16)
        for j, v in enumerate((d_reset, d_upd, d_cand, d_cand * reset)):
            hi = v.astype(BF16)
            low = (v - hi.astype(F32)).astype(BF16)
            part = mm(left, hi, ((0,), (0,))) + mm(left, low, ((0,), (0,)))
            cols = slice(256 * j, 256 * j + 256)
            if i == 0 and not last:
                acc[:, cols] = part
            else:
                acc[:, cols] += part
    if last:
        total = acc[...] * GRAD_SCALE
        third = jnp.where(iota((128, 256), 0) < 64, total[:, 512:768], total[:, 768:1024])
        total = jnp.concatenate([total[:, 0:512], third], axis=1)
        for p in range(32):
            i, j = p // 2, p % 2
            grad[p, :, 0:384] = total[8 * i : 8 * i + 8, 384 * j : 384 * j + 384]
            grad[p, :, 384:512] = own_hot[...]


def piece_kernel(parts, out, hot):
    total = parts[0, :, 0:384]
    for k in range(1, 32):
        total = total + parts[k, :, 0:384]
    for k in range(32):
        out[k] = total
        hot[k] = parts[k, :, 384:512]


def place_kernel(pos, a0, a1, a2, a3, b0, b1, b2, b3, g_in, g_hid, both, sems):
    x, core = pos[0], pos[1]
    stores = []
    for group, c in (((a0, a1, a2, a3), core), ((b0, b1, b2, b3), 1 - core)):
        for d, part in enumerate(group):
            block = 2 * ((x - d + 4) & 3) + c
            k = len(stores)
            for p in range(24):
                i, j = p // 2, p % 2
                both[96 * (k // 2) + 8 * i : 96 * (k // 2) + 8 * i + 8, 384 * j : 384 * j + 384] = part[p]
            for rows, at, dst in (
                (64, 96 * (k // 2), g_in.at[pl.ds(pl.multiple_of(block * 64, 64), 64)]),
                (32, 96 * (k // 2) + 64, g_hid.at[pl.ds(pl.multiple_of(block * 32, 32), 32)]),
            ):
                stores.append(pltpu.make_async_copy(both.at[at : at + rows], dst, sems.at[len(stores)]))
                stores[-1].start()
    for c in stores:
        c.wait()


def swap_core(v):
    return lax.ppermute(v, "rep", [(k, k ^ 1) for k in range(8)])


def shift_x(v, d):
    return lax.ppermute(v, "rep", [(k, (k + 2 * d) % 8) for k in range(8)])


def gather_rep(v):
    own = [v] + [shift_x(v, d) for d in (1, 2, 3)]
    return own + [swap_core(u) for u in own]


def on_device(
    memory,
    hot_memory,
    cot_cold,
    cot_hot,
    src_local,
    dst_ids,
    times,
    edge_feat,
    cold_list,
    cold_count,
    hot_ids,
    time_freq,
    time_phase,
    w_msg,
    b_msg,
    w_in,
    w_hid,
):
    node = lax.axis_index("node")
    rep = lax.axis_index("rep")
    pos = jnp.stack([rep // 2, rep % 2, rep]).astype(I32)
    sds = jax.ShapeDtypeStruct

    chip, core = rep // 2, rep % 2
    send, hot = call(
        message_kernel,
        (sds((32, 144, 128), BF16), sds((96, 512), F32)),
        (SM,) + (HB,) * 11,
        (
            node.astype(I32)[None], memory, edge_feat, w_msg, src_local[None, :], times[None, :],
            dst_ids[None, :], cold_list, cold_count[None, :], time_freq[None, :], time_phase[None, :],
            b_msg[None, :],
        ),
        (
            pltpu.VMEM((1024, 256), F32), pltpu.VMEM((1024, 128), BF16), pltpu.VMEM((512, 512), BF16),
            pltpu.VMEM((1, 1024), I32), pltpu.VMEM((1, 1024), I32), pltpu.VMEM((1, 1024), I32),
            pltpu.VMEM((32, 32), I32), pltpu.VMEM((1, 32), I32), pltpu.VMEM((1, 128), F32),
            pltpu.VMEM((1, 128), F32), pltpu.VMEM((1, 512), F32),
            pltpu.VMEM((1024, 128), BF16), pltpu.VMEM((1024, 512), BF16), pltpu.VMEM((32, 144, 128), BF16),
            pltpu.VMEM((1024, 8), I32),
            pltpu.SemaphoreType.DMA((15,)),
        ),
        (ANY, VM),
        63,
    )
    recv = lax.all_to_all(send, "node", split_axis=0, concat_axis=0, tiled=True)

    hot = hot + swap_core(hot)
    spill = lax.dynamic_slice_in_dim(hot, 64 + 16 * core, 16, 0)
    spill = lax.ppermute(spill, "node", [(k, (k + 1) % 32) for k in range(32)])
    k = jnp.arange(128, dtype=I32)
    want = 32768 + 32 * node + 4 * (k // 16) + k % 4
    at = jnp.sum(jnp.where(want[:, None] == hot_ids[None, :], jnp.arange(1024, dtype=I32)[None, :], 0), axis=1)
    hot_mem = jnp.take(hot_memory, at, axis=0, mode="clip")
    hot_cot = jnp.take(cot_hot, at, axis=0, mode="clip")

    recv, hot_mem, hot_cot, _ = lax.optimization_barrier((recv, hot_mem, hot_cot, spill))
    block = sds((136, 512), F32)
    parts = call(
        cold_kernel,
        (block,) * 4,
        (SM,),
        (pos, recv, swap_core(recv), hot.reshape(12, 8, 512), spill.reshape(2, 8, 512)),
    )
    parts = [parts[0]] + [shift_x(parts[d], d) for d in (1, 2, 3)]
    agg = call(
        agg_kernel,
        sds((144, 512), BF16),
        (ANY, ANY, ANY),
        (*parts[1:], parts[0]),
        (pltpu.VMEM((3, 136, 512), F32), pltpu.VMEM((144, 512), BF16), pltpu.SemaphoreType.DMA((4,))),
        ANY,
    )
    parts = gather_rep(agg)
    shared = (memory, cot_cold, hot_mem, hot_cot, w_in, w_hid)
    own = call(
        functools.partial(update_kernel, (0,), False),
        (sds((256, 256), F32), sds((8, 128), F32), sds((128, 1024), F32)),
        (SM,),
        (pos, parts[0], parts[4], *shared),
    )
    new_memory, grad = call(
        functools.partial(update_kernel, (3, 2, 1), True),
        (sds((1024, 256), F32), sds((32, 8, 512), F32)),
        (SM,),
        (pos, parts[3], parts[7], parts[2], parts[6], parts[1], parts[5], *shared, *own),
        (pltpu.VMEM((128, 1024), F32),),
    )

    grad = lax.all_to_all(grad, "node", split_axis=0, concat_axis=0, tiled=True)
    grad, hot_new = call(piece_kernel, (sds((32, 8, 384), F32), sds((32, 8, 128), F32)), (), (grad,))
    grad = lax.all_to_all(grad, "node", split_axis=0, concat_axis=0, tiled=True)
    new_hot = call(
        hot_place_kernel,
        sds((1024, 256), F32),
        (SM,),
        (pos, hot_ids[None, :], *gather_rep(hot_new)),
        (pltpu.VMEM((8, 128, 256), F32),),
    )
    grad, new_hot = lax.optimization_barrier((grad, new_hot))
    grad_in, grad_hid = call(
        place_kernel,
        (sds((512, 768), F32), sds((256, 768), F32)),
        (SM,),
        (pos, *gather_rep(grad[0:24])),
        (pltpu.VMEM((768, 768), F32), pltpu.SemaphoreType.DMA((16,))),
        (ANY, ANY),
    )
    return (new_memory, new_hot, grad_in, grad_hid)


def solution(mesh):
    in_specs = (
        P("node", None),
        P(),
        P("node", None),
        P(),
        P(("node", "rep")),
        P(("node", "rep")),
        P(("node", "rep")),
        P(("node", "rep"), None),
        P(("node", "rep"), None),
        P(("node", "rep")),
        P(),
        P(),
        P(),
        P(),
        P(),
        P(),
        P(),
    )
    out_specs = (P("node", None), P(), P(), P())
    return jax.shard_map(
        on_device, mesh=mesh, in_specs=in_specs, out_specs=out_specs, check_vma=False
    )
```

```python
import functools

import jax
import jax.numpy as jnp
from jax import lax
from jax.experimental import pallas as pl
from jax.experimental.pallas import tpu as pltpu
from jax.sharding import PartitionSpec as P

GRAD_SCALE = 1.0 / 64.0
DEAD = 2.0**100
F32, BF16, I32 = jnp.float32, jnp.bfloat16, jnp.int32
VM = pl.BlockSpec(memory_space=pltpu.VMEM)
SM = pl.BlockSpec(memory_space=pltpu.SMEM)
HB = pl.BlockSpec(memory_space=pltpu.HBM)
ANY = pl.BlockSpec(memory_space=pl.ANY)


def iota(shape, dim):
    return lax.broadcasted_iota(I32, shape, dim)


def one_hot(mask):
    return jnp.where(mask, 1.0, 0.0).astype(BF16)


def mm(a, b, dims=((1,), (0,))):
    return lax.dot_general(a, b, (dims, ((), ())), preferred_element_type=F32)


def call(body, out_shape, places, args, scratch=(), out_places=None, mib=48, aliases=None):
    if out_places is None:
        out_places = jax.tree.map(lambda _: VM, out_shape)
    return pl.pallas_call(
        body,
        out_shape=out_shape,
        in_specs=list(places) + [VM] * (len(args) - len(places)),
        out_specs=out_places,
        scratch_shapes=list(scratch),
        input_output_aliases=aliases or {},
        compiler_params=pltpu.CompilerParams(vmem_limit_bytes=mib * 1024 * 1024),
    )(*args)


def column(row):
    return jnp.broadcast_to(row, (8, row.shape[1])).T[:, 0:1]


def cosine(x):
    k = jnp.round(x * 0.15915494309189535)
    r = x - k * 6.28125
    r = r - k * 0.0019350051879882812
    r = r - k * 3.019916e-07
    u = 1.5707963267948966 - jnp.abs(r)
    u2 = u * u
    p = 2.6083159809786593e-06
    for c in (-0.00019810690719168633, 0.0083330785855650902, -0.16666659712791443, 1.0):
        p = p * u2 + c
    return u * p


def message_kernel(
    pos, mem_h, edge_h, w_h, src_h, times_h, dst_h, listed_h, used_h, freq_h, phase_h, b_h, send_h, hot,
    mem, edge, w, src, times, dst_v, listed, used, freq, phase, b, encs, msgs, out, cols, sems,
):
    loads = [
        pltpu.make_async_copy(h, v, sems.at[i])
        for i, (h, v) in enumerate(
            (
                (src_h, src), (times_h, times), (dst_h, dst_v), (listed_h, listed), (used_h, used),
                (freq_h, freq), (phase_h, phase), (b_h, b), (mem_h, mem), (edge_h, edge), (w_h, w),
            )
        )
    ]
    for c in loads:
        c.start()
    for c in loads[:8]:
        c.wait()
    n_ev, step = 1024, 256
    dst = dst_v[...]
    line = iota((8, n_ev), 0)
    packed = jnp.where(line == 0, src[...], jnp.where(line == 1, times[...], dst))
    cols[...] = packed.T
    slot = iota((32, 32), 0)
    eye = one_hot(slot == iota((32, 32), 1))
    names = listed[...]
    hi = mm(eye, (names >> 5).astype(F32).astype(BF16), ((1,), (1,)))
    lo = mm(eye, (names & 31).astype(F32).astype(BF16), ((1,), (1,)))
    names = jnp.where(slot < used[...], (hi * 32.0 + lo).astype(I32), -1)
    encs[...] = cosine(cols[:, 1:2].astype(F32) * freq[...] + phase[...]).astype(BF16)
    for c in loads[8:]:
        c.wait()
    mem16 = mem[...].astype(BF16)
    for e in range(0, n_ev, step):
        at = cols[e : e + step, :]
        src_mem = mm(one_hot(iota((step, 1024), 1) == at[:, 0:1]), mem16).astype(BF16)
        raw = jnp.concatenate([src_mem, edge[e : e + step, :], encs[e : e + step, :]], axis=1)
        pre = mm(raw, w[...]) + b[...]
        msgs[e : e + step, :] = (pre * jax.nn.sigmoid(pre)).astype(BF16)
    row = dst & 1023
    facts = jnp.where(line == 0, row >> 5, jnp.where(line == 1, row & 31, jnp.where(line == 2, 1, 0)))
    facts = facts.astype(F32).astype(BF16)
    lane = iota((8, 128), 1)
    stores = []
    for t in range(4):
        pick = jnp.concatenate(
            [one_hot(iota((32, n_ev), 1) == names[:, o : o + 1]) for o in range(8 * t, 8 * t + 8)], axis=0
        )
        moved = mm(pick, msgs[...]).astype(BF16)
        tail = mm(facts, pick, ((1,), (1,)))
        for i in range(8):
            o = 8 * t + i
            for q in range(4):
                out[o, 32 * q : 32 * q + 32, :] = moved[32 * i : 32 * i + 32, 128 * q : 128 * q + 128]
            k = o % 4
            own = tail[:, 128 * (i // 4) : 128 * (i // 4) + 128]
            own = jnp.where((lane >> 5) == k, own, 0.0)
            own = pltpu.roll(own, ((pos[0] & 3) + 4 - k) * 32 & 127, 1)
            out[o, 128:144, :] = jnp.concatenate([own, jnp.zeros((8, 128), F32)], axis=0).astype(BF16)
        here = pl.ds(8 * t, 8)
        stores.append(pltpu.make_async_copy(out.at[here], send_h.at[here], sems.at[11 + t]))
        stores[-1].start()
    window = jnp.where(dst >= 32768, (dst - 32768 - 32 * pos[0] + 1024) & 1023, -1)
    q = iota((96, n_ev), 0)
    block = jnp.where(q < 64, 2 * ((q >> 3) & 3) + ((q >> 5) & 1), 8 + 2 * ((q >> 3) & 1) + ((q >> 4) & 1))
    hit = one_hot(4 * block + (q & 3) == window)
    total = mm(hit, msgs[...])
    count = jnp.sum(hit.astype(F32), axis=1, keepdims=True)
    hot[...] = jnp.where((iota((96, 512), 0) & 7) < 4, total, count)
    for c in stores:
        c.wait()


def cold_kernel(pos, own, peer, hot, spill, o0, o1, o2, o3):
    q = iota((512, 128), 0)
    want = (q & 127) + 256 * ((pos[0] + (q >> 7)) & 3) + 128 * pos[1]
    hits = []
    for got in (own, peer):
        for g in range(8):
            tail = got[4 * g, 128:144, :].astype(F32)
            for i in range(1, 4):
                tail = tail + got[4 * g + i, 128:144, :].astype(F32)
            row = jnp.where(tail[2:3, :] > 0.5, tail[0:1, :] * 32.0 + tail[1:2, :], -1.0).astype(I32)
            hits.append(one_hot(want == row))
    hit = jnp.concatenate(hits, axis=1)
    count = mm(jnp.ones((8, 2048), BF16), hit, ((1,), (1,)))
    for n in range(2):
        cols = slice(256 * n, 256 * n + 256)
        msgs = jnp.concatenate(
            [
                jnp.concatenate(
                    [got[:, 32 * k : 32 * k + 32, :].reshape(1024, 128) for k in (2 * n, 2 * n + 1)], axis=1
                )
                for got in (own, peer)
            ],
            axis=0,
        )
        total = mm(hit, msgs)
        for d, to in enumerate((o0, o1, o2, o3)):
            here = slice(128 * d, 128 * d + 128)
            to[0:128, cols] = total[here, :]
            j = (pos[0] + d) & 3
            tile = hot[4 * pos[1] + j, :, cols] + jnp.where(j < 2, 1.0, 0.0) * spill[j & 1, :, cols]
            if n == 0:
                rows = jnp.concatenate([count[:, here], tile[:, 128:256]], axis=1)
                tile = jnp.where((iota((8, 256), 0) >= 4) & (iota((8, 256), 1) < 128), rows, tile)
            to[128:136, cols] = tile


def agg_kernel(p1_h, p2_h, p3_h, p0, out_h, part, out, sems):
    loads = [pltpu.make_async_copy(h, part.at[i], sems.at[i]) for i, h in enumerate((p1_h, p2_h, p3_h))]
    for c in loads:
        c.start()
    for c in loads:
        c.wait()
    total = p0[...] + part[0] + part[1] + part[2]
    count = column(total[132:133, 0:128])
    agg = jnp.where(count > 0.0, total[0:128, :] / jnp.maximum(count, 1.0), DEAD)
    out[0:128, :] = agg.astype(BF16)
    count = total[132:136, 128:129]
    agg = jnp.where(count > 0.0, total[128:132, :] / jnp.maximum(count, 1.0), DEAD)
    out[128:144, :] = jnp.concatenate([agg, jnp.full((12, 512), DEAD, F32)], axis=0).astype(BF16)
    store = pltpu.make_async_copy(out, out_h, sems.at[3])
    store.start()
    store.wait()


def gates(agg, mem, w_in, w_hid):
    gi = mm(agg, w_in)
    gh = mm(mem.astype(BF16), w_hid)
    reset = jax.nn.sigmoid(gi[:, 0:256] + gh[:, 0:256])
    update = jax.nn.sigmoid(gi[:, 256:512] + gh[:, 256:512])
    cand = jnp.tanh(gi[:, 512:768] + reset * gh[:, 512:768])
    return reset, update, cand, gh[:, 512:768]


def hot_place_kernel(pos, ids, a0, a1, a2, a3, b0, b1, b2, b3, out, rows):
    x, core = pos[0], pos[1]
    for group, c in (((a0, a1, a2, a3), core), ((b0, b1, b2, b3), 1 - core)):
        for d, part in enumerate(group):
            block = 2 * ((x - d + 4) & 3) + c
            for n in range(32):
                rows[block, 4 * n : 4 * n + 4, 0:128] = part[n, 0:4, :]
                rows[block, 4 * n : 4 * n + 4, 128:256] = part[n, 4:8, :]
    name = column(ids[...]) - 32768
    at = 128 * ((name >> 2) & 7) + 4 * (name >> 5) + (name & 3)
    full = rows[...].reshape(1024, 256)
    hi = full.astype(BF16)
    rest = full - hi.astype(F32)
    mid = rest.astype(BF16)
    low = (rest - mid.astype(F32)).astype(BF16)
    for h in range(0, 1024, 256):
        pick = one_hot(iota((256, 1024), 1) == at[h : h + 256, :])
        out[h : h + 256, :] = mm(pick, hi) + (mm(pick, mid) + mm(pick, low))


def update_kernel(ds, done, pos, *refs):
    last = len(done) > 0
    parts, refs = refs[: 2 * len(ds)], refs[2 * len(ds) :]
    mem, cot, hot_mem, hot_cot, w_in, w_hid = refs[:6]
    refs = refs[6:]
    if last:
        olds, (own_hot, old_acc, new, grad, acc) = refs[: len(done)], refs[len(done) :]
        for d, old in zip(done, olds):
            chip = (pos[0] - d + 4) & 3
            new[pl.ds(pl.multiple_of(256 * chip, 256), 256), :] = old[...]
    elif 0 in ds:
        new, hot, acc = refs
        old_acc = None
    else:
        old_acc, new, acc = refs
    if old_acc is not None:
        acc[...] = old_acc[...]
    x, core, rep = pos[0], pos[1], pos[2]
    k, q = iota((512, 128), 0), iota((512, 128), 1)
    sel_a = one_hot((k == 64 * rep + q) & (q < 64))
    k, q = iota((256, 128), 0), iota((256, 128), 1)
    sel_m = one_hot((k == 32 * rep + q - 64) & (q >= 64) & (q < 96))
    for i, d in enumerate(ds):
        chip = (x - d + 4) & 3
        at = pl.ds(pl.multiple_of(256 * chip, 256), 256)
        hot_at = pl.ds(pl.multiple_of(32 * chip, 32), 32)
        mine, other = parts[2 * i][...], parts[2 * i + 1][...]
        low = jnp.where(core == 0, mine, other)
        high = jnp.where(core == 0, other, mine)
        wide = jnp.concatenate([low[0:128], high[0:128], low[128:144], high[128:144]], axis=0).astype(F32)
        live = wide[:, 0:1] < DEAD * 0.5
        a = jnp.where(live, wide, 0.0).astype(BF16)
        m = jnp.concatenate([mem[at, :], hot_mem[hot_at, :]], axis=0)
        reset, update, cand, hid_cand = gates(a, m, w_in[...], w_hid[...])
        fresh = jnp.where(live, (1.0 - update) * cand + update * m, m)
        if last:
            new[at, :] = fresh[0:256, :]
        else:
            new[...] = fresh[0:256, :]
            if d == 0:
                own = jnp.where(core == 0, fresh[256:264, :], fresh[272:280, :])
                hot[...] = jnp.concatenate([own[0:4, 0:128], own[0:4, 128:256]], axis=0)
        g = jnp.where(live, jnp.concatenate([cot[at, :], hot_cot[hot_at, :]], axis=0), 0.0)
        d_cand = g * (1.0 - update) * (1.0 - cand * cand)
        d_upd = g * (m - cand) * update * (1.0 - update)
        d_reset = d_cand * hid_cand * reset * (1.0 - reset)
        left = (mm(a, sel_a) + mm(m.astype(BF16), sel_m)).astype(BF16)
        for j, v in enumerate((d_reset, d_upd, d_cand, d_cand * reset)):
            hi = v.astype(BF16)
            low = (v - hi.astype(F32)).astype(BF16)
            part = mm(left, hi, ((0,), (0,))) + mm(left, low, ((0,), (0,)))
            cols = slice(256 * j, 256 * j + 256)
            if i == 0 and old_acc is None:
                acc[:, cols] = part
            else:
                acc[:, cols] += part
    if last:
        total = acc[...] * GRAD_SCALE
        third = jnp.where(iota((128, 256), 0) < 64, total[:, 512:768], total[:, 768:1024])
        total = jnp.concatenate([total[:, 0:512], third], axis=1)
        for p in range(32):
            i, j = p // 2, p % 2
            grad[p, :, 0:384] = total[8 * i : 8 * i + 8, 384 * j : 384 * j + 384]
            grad[p, :, 384:512] = own_hot[...]


def piece_kernel(parts, out, hot):
    total = parts[0, :, 0:384]
    for k in range(1, 32):
        total = total + parts[k, :, 0:384]
    for k in range(32):
        out[k] = total
        hot[k] = parts[k, :, 384:512]


def place_kernel(other, pos, a0, a1, a2, a3, *refs):
    g_in, g_hid, both, sems = refs[-4:]
    x = pos[0]
    core = 1 - pos[1] if other else pos[1]
    stores = []
    for d, part in enumerate((a0, a1, a2, a3)):
        block = 2 * ((x - d + 4) & 3) + core
        for p in range(24):
            i, j = p // 2, p % 2
            both[96 * d + 8 * i : 96 * d + 8 * i + 8, 384 * j : 384 * j + 384] = part[p]
        for rows, at, dst in (
            (64, 96 * d, g_in.at[pl.ds(pl.multiple_of(block * 64, 64), 64)]),
            (32, 96 * d + 64, g_hid.at[pl.ds(pl.multiple_of(block * 32, 32), 32)]),
        ):
            stores.append(pltpu.make_async_copy(both.at[at : at + rows], dst, sems.at[len(stores)]))
            stores[-1].start()
    for c in stores:
        c.wait()


def swap_core(v):
    return lax.ppermute(v, "rep", [(k, k ^ 1) for k in range(8)])


def shift_x(v, d):
    return lax.ppermute(v, "rep", [(k, (k + 2 * d) % 8) for k in range(8)])


def gather_rep(v):
    own = [v] + [shift_x(v, d) for d in (1, 2, 3)]
    return own + [swap_core(u) for u in own]


def on_device(
    memory,
    hot_memory,
    cot_cold,
    cot_hot,
    src_local,
    dst_ids,
    times,
    edge_feat,
    cold_list,
    cold_count,
    hot_ids,
    time_freq,
    time_phase,
    w_msg,
    b_msg,
    w_in,
    w_hid,
):
    node = lax.axis_index("node")
    rep = lax.axis_index("rep")
    pos = jnp.stack([rep // 2, rep % 2, rep]).astype(I32)
    sds = jax.ShapeDtypeStruct

    chip, core = rep // 2, rep % 2
    send, hot = call(
        message_kernel,
        (sds((32, 144, 128), BF16), sds((96, 512), F32)),
        (SM,) + (HB,) * 11,
        (
            node.astype(I32)[None], memory, edge_feat, w_msg, src_local[None, :], times[None, :],
            dst_ids[None, :], cold_list, cold_count[None, :], time_freq[None, :], time_phase[None, :],
            b_msg[None, :],
        ),
        (
            pltpu.VMEM((1024, 256), F32), pltpu.VMEM((1024, 128), BF16), pltpu.VMEM((512, 512), BF16),
            pltpu.VMEM((1, 1024), I32), pltpu.VMEM((1, 1024), I32), pltpu.VMEM((1, 1024), I32),
            pltpu.VMEM((32, 32), I32), pltpu.VMEM((1, 32), I32), pltpu.VMEM((1, 128), F32),
            pltpu.VMEM((1, 128), F32), pltpu.VMEM((1, 512), F32),
            pltpu.VMEM((1024, 128), BF16), pltpu.VMEM((1024, 512), BF16), pltpu.VMEM((32, 144, 128), BF16),
            pltpu.VMEM((1024, 8), I32),
            pltpu.SemaphoreType.DMA((15,)),
        ),
        (ANY, VM),
        63,
    )
    recv = lax.all_to_all(send, "node", split_axis=0, concat_axis=0, tiled=True)

    hot = hot + swap_core(hot)
    spill = lax.dynamic_slice_in_dim(hot, 64 + 16 * core, 16, 0)
    spill = lax.ppermute(spill, "node", [(k, (k + 1) % 32) for k in range(32)])
    k = jnp.arange(128, dtype=I32)
    want = 32768 + 32 * node + 4 * (k // 16) + k % 4
    at = jnp.sum(jnp.where(want[:, None] == hot_ids[None, :], jnp.arange(1024, dtype=I32)[None, :], 0), axis=1)
    hot_mem = jnp.take(hot_memory, at, axis=0, mode="clip")
    hot_cot = jnp.take(cot_hot, at, axis=0, mode="clip")

    recv, hot_mem, hot_cot, _ = lax.optimization_barrier((recv, hot_mem, hot_cot, spill))
    block = sds((136, 512), F32)
    parts = call(
        cold_kernel,
        (block,) * 4,
        (SM,),
        (pos, recv, swap_core(recv), hot.reshape(12, 8, 512), spill.reshape(2, 8, 512)),
    )
    parts = [parts[0]] + [shift_x(parts[d], d) for d in (1, 2, 3)]
    agg = call(
        agg_kernel,
        sds((144, 512), BF16),
        (ANY, ANY, ANY),
        (*parts[1:], parts[0]),
        (pltpu.VMEM((3, 136, 512), F32), pltpu.VMEM((144, 512), BF16), pltpu.SemaphoreType.DMA((4,))),
        ANY,
    )
    near, far, back = [shift_x(agg, d) for d in (1, 2, 3)]
    shared = (memory, cot_cold, hot_mem, hot_cot, w_in, w_hid)
    rows, sums = sds((256, 256), F32), sds((128, 1024), F32)
    new_own, hot_own, acc = call(
        functools.partial(update_kernel, (0,), ()),
        (rows, sds((8, 128), F32), sums),
        (SM,),
        (pos, agg, swap_core(agg), *shared),
    )
    new_near, acc = call(
        functools.partial(update_kernel, (1,), ()),
        (rows, sums),
        (SM,),
        (pos, near, swap_core(near), *shared, acc),
    )
    far, new_near = lax.optimization_barrier((far, new_near))
    new_memory, grad = call(
        functools.partial(update_kernel, (3, 2), (0, 1)),
        (sds((1024, 256), F32), sds((32, 8, 512), F32)),
        (SM,),
        (pos, back, swap_core(back), far, swap_core(far), *shared, new_own, new_near, hot_own, acc),
        (pltpu.VMEM((128, 1024), F32),),
    )

    grad = lax.all_to_all(grad, "node", split_axis=0, concat_axis=0, tiled=True)
    grad, hot_new = call(piece_kernel, (sds((32, 8, 384), F32), sds((32, 8, 128), F32)), (), (grad,))
    grad = lax.all_to_all(grad, "node", split_axis=0, concat_axis=0, tiled=True)
    hot_parts = gather_rep(hot_new)
    grad, hot_parts = lax.optimization_barrier((grad, hot_parts))
    new_hot = call(
        hot_place_kernel,
        sds((1024, 256), F32),
        (SM,),
        (pos, hot_ids[None, :], *hot_parts),
        (pltpu.VMEM((8, 128, 256), F32),),
    )
    own = [grad[0:24]] + [shift_x(grad[0:24], d) for d in (1, 2, 3)]
    own[2], new_hot = lax.optimization_barrier((own[2], new_hot))
    places = (pltpu.VMEM((384, 768), F32), pltpu.SemaphoreType.DMA((8,)))
    grads = (sds((512, 768), F32), sds((256, 768), F32))
    grads = call(
        functools.partial(place_kernel, False), grads, (SM,), (pos, *own), places, (ANY, ANY)
    )
    grad_in, grad_hid = call(
        functools.partial(place_kernel, True),
        tuple(sds(g.shape, F32) for g in grads),
        (SM, VM, VM, VM, VM, ANY, ANY),
        (pos, *[swap_core(v) for v in own], *grads),
        places,
        (ANY, ANY),
        aliases={5: 0, 6: 1},
    )
    return (new_memory, new_hot, grad_in, grad_hid)


def solution(mesh):
    in_specs = (
        P("node", None),
        P(),
        P("node", None),
        P(),
        P(("node", "rep")),
        P(("node", "rep")),
        P(("node", "rep")),
        P(("node", "rep"), None),
        P(("node", "rep"), None),
        P(("node", "rep")),
        P(),
        P(),
        P(),
        P(),
        P(),
        P(),
        P(),
    )
    out_specs = (P("node", None), P(), P(), P())
    return jax.shard_map(
        on_device, mesh=mesh, in_specs=in_specs, out_specs=out_specs, check_vma=False
    )
```

```python
import functools

import jax
import jax.numpy as jnp
from jax import lax
from jax.experimental import pallas as pl
from jax.experimental.pallas import tpu as pltpu
from jax.sharding import PartitionSpec as P

GRAD_SCALE = 1.0 / 64.0
DEAD = 2.0**100
F32, BF16, I32 = jnp.float32, jnp.bfloat16, jnp.int32
VM = pl.BlockSpec(memory_space=pltpu.VMEM)
SM = pl.BlockSpec(memory_space=pltpu.SMEM)
HB = pl.BlockSpec(memory_space=pltpu.HBM)
ANY = pl.BlockSpec(memory_space=pl.ANY)


def iota(shape, dim):
    return lax.broadcasted_iota(I32, shape, dim)


def one_hot(mask):
    return jnp.where(mask, 1.0, 0.0).astype(BF16)


def mm(a, b, dims=((1,), (0,))):
    return lax.dot_general(a, b, (dims, ((), ())), preferred_element_type=F32)


def call(body, out_shape, places, args, scratch=(), out_places=None, mib=48, aliases=None):
    if out_places is None:
        out_places = jax.tree.map(lambda _: VM, out_shape)
    return pl.pallas_call(
        body,
        out_shape=out_shape,
        in_specs=list(places) + [VM] * (len(args) - len(places)),
        out_specs=out_places,
        scratch_shapes=list(scratch),
        input_output_aliases=aliases or {},
        compiler_params=pltpu.CompilerParams(vmem_limit_bytes=mib * 1024 * 1024),
    )(*args)


def column(row):
    return jnp.broadcast_to(row, (8, row.shape[1])).T[:, 0:1]


def cosine(x):
    k = jnp.round(x * 0.15915494309189535)
    r = x - k * 6.28125
    r = r - k * 0.0019350051879882812
    r = r - k * 3.019916e-07
    u = 1.5707963267948966 - jnp.abs(r)
    u2 = u * u
    p = 2.6083159809786593e-06
    for c in (-0.00019810690719168633, 0.0083330785855650902, -0.16666659712791443, 1.0):
        p = p * u2 + c
    return u * p


def message_kernel(
    pos, mem_h, edge_h, w_h, src_h, times_h, dst_h, listed_h, used_h, freq_h, phase_h, b_h, send_h, hot,
    mem, edge, w, src, times, dst_v, listed, used, freq, phase, b, encs, msgs, out, cols, sems,
):
    loads = [
        pltpu.make_async_copy(h, v, sems.at[i])
        for i, (h, v) in enumerate(
            (
                (src_h, src), (times_h, times), (dst_h, dst_v), (listed_h, listed), (used_h, used),
                (freq_h, freq), (phase_h, phase), (b_h, b), (mem_h, mem), (edge_h, edge), (w_h, w),
            )
        )
    ]
    for c in loads:
        c.start()
    for c in loads[:8]:
        c.wait()
    n_ev, step = 1024, 256
    dst = dst_v[...]
    line = iota((8, n_ev), 0)
    packed = jnp.where(line == 0, src[...], jnp.where(line == 1, times[...], dst))
    cols[...] = packed.T
    slot = iota((32, 32), 0)
    eye = one_hot(slot == iota((32, 32), 1))
    names = listed[...]
    hi = mm(eye, (names >> 5).astype(F32).astype(BF16), ((1,), (1,)))
    lo = mm(eye, (names & 31).astype(F32).astype(BF16), ((1,), (1,)))
    names = jnp.where(slot < used[...], (hi * 32.0 + lo).astype(I32), -1)
    encs[...] = cosine(cols[:, 1:2].astype(F32) * freq[...] + phase[...]).astype(BF16)
    for c in loads[8:]:
        c.wait()
    mem16 = mem[...].astype(BF16)
    for e in range(0, n_ev, step):
        at = cols[e : e + step, :]
        src_mem = mm(one_hot(iota((step, 1024), 1) == at[:, 0:1]), mem16).astype(BF16)
        raw = jnp.concatenate([src_mem, edge[e : e + step, :], encs[e : e + step, :]], axis=1)
        pre = mm(raw, w[...]) + b[...]
        msgs[e : e + step, :] = (pre * jax.nn.sigmoid(pre)).astype(BF16)
    row = dst & 1023
    facts = jnp.where(line == 0, row >> 5, jnp.where(line == 1, row & 31, jnp.where(line == 2, 1, 0)))
    facts = facts.astype(F32).astype(BF16)
    lane = iota((8, 128), 1)
    stores = []
    for t in range(4):
        pick = jnp.concatenate(
            [one_hot(iota((32, n_ev), 1) == names[:, o : o + 1]) for o in range(8 * t, 8 * t + 8)], axis=0
        )
        moved = mm(pick, msgs[...]).astype(BF16)
        tail = mm(facts, pick, ((1,), (1,)))
        for i in range(8):
            o = 8 * t + i
            for q in range(4):
                out[o, 32 * q : 32 * q + 32, :] = moved[32 * i : 32 * i + 32, 128 * q : 128 * q + 128]
            k = o % 4
            own = tail[:, 128 * (i // 4) : 128 * (i // 4) + 128]
            own = jnp.where((lane >> 5) == k, own, 0.0)
            own = pltpu.roll(own, ((pos[0] & 3) + 4 - k) * 32 & 127, 1)
            out[o, 128:144, :] = jnp.concatenate([own, jnp.zeros((8, 128), F32)], axis=0).astype(BF16)
        here = pl.ds(8 * t, 8)
        stores.append(pltpu.make_async_copy(out.at[here], send_h.at[here], sems.at[11 + t]))
        stores[-1].start()
    window = jnp.where(dst >= 32768, (dst - 32768 - 32 * pos[0] + 1024) & 1023, -1)
    q = iota((96, n_ev), 0)
    block = jnp.where(q < 64, 2 * ((q >> 3) & 3) + ((q >> 5) & 1), 8 + 2 * ((q >> 3) & 1) + ((q >> 4) & 1))
    hit = one_hot(4 * block + (q & 3) == window)
    total = mm(hit, msgs[...])
    count = jnp.sum(hit.astype(F32), axis=1, keepdims=True)
    hot[...] = jnp.where((iota((96, 512), 0) & 7) < 4, total, count)
    for c in stores:
        c.wait()


def cold_kernel(pos, own, peer, hot, spill, o0, o1, o2, o3):
    q = iota((512, 128), 0)
    want = (q & 127) + 256 * ((pos[0] + (q >> 7)) & 3) + 128 * pos[1]
    hits = []
    for got in (own, peer):
        for g in range(8):
            tail = got[4 * g, 128:144, :].astype(F32)
            for i in range(1, 4):
                tail = tail + got[4 * g + i, 128:144, :].astype(F32)
            row = jnp.where(tail[2:3, :] > 0.5, tail[0:1, :] * 32.0 + tail[1:2, :], -1.0).astype(I32)
            hits.append(one_hot(want == row))
    hit = jnp.concatenate(hits, axis=1)
    count = mm(jnp.ones((8, 2048), BF16), hit, ((1,), (1,)))
    for n in range(2):
        cols = slice(256 * n, 256 * n + 256)
        msgs = jnp.concatenate(
            [
                jnp.concatenate(
                    [got[:, 32 * k : 32 * k + 32, :].reshape(1024, 128) for k in (2 * n, 2 * n + 1)], axis=1
                )
                for got in (own, peer)
            ],
            axis=0,
        )
        total = mm(hit, msgs)
        for d, to in enumerate((o0, o1, o2, o3)):
            here = slice(128 * d, 128 * d + 128)
            to[0:128, cols] = total[here, :]
            j = (pos[0] + d) & 3
            tile = hot[4 * pos[1] + j, :, cols] + jnp.where(j < 2, 1.0, 0.0) * spill[j & 1, :, cols]
            if n == 0:
                rows = jnp.concatenate([count[:, here], tile[:, 128:256]], axis=1)
                tile = jnp.where((iota((8, 256), 0) >= 4) & (iota((8, 256), 1) < 128), rows, tile)
            to[128:136, cols] = tile


def agg_kernel(p1_h, p2_h, p3_h, p0, out_h, part, out, sems):
    loads = [pltpu.make_async_copy(h, part.at[i], sems.at[i]) for i, h in enumerate((p1_h, p2_h, p3_h))]
    for c in loads:
        c.start()
    for c in loads:
        c.wait()
    total = p0[...] + part[0] + part[1] + part[2]
    count = column(total[132:133, 0:128])
    agg = jnp.where(count > 0.0, total[0:128, :] / jnp.maximum(count, 1.0), DEAD)
    out[0:128, :] = agg.astype(BF16)
    count = total[132:136, 128:129]
    agg = jnp.where(count > 0.0, total[128:132, :] / jnp.maximum(count, 1.0), DEAD)
    out[128:144, :] = jnp.concatenate([agg, jnp.full((12, 512), DEAD, F32)], axis=0).astype(BF16)
    store = pltpu.make_async_copy(out, out_h, sems.at[3])
    store.start()
    store.wait()


def gates(agg, mem, w_in, w_hid):
    gi = mm(agg, w_in)
    gh = mm(mem.astype(BF16), w_hid)
    reset = jax.nn.sigmoid(gi[:, 0:256] + gh[:, 0:256])
    update = jax.nn.sigmoid(gi[:, 256:512] + gh[:, 256:512])
    cand = jnp.tanh(gi[:, 512:768] + reset * gh[:, 512:768])
    return reset, update, cand, gh[:, 512:768]


def hot_place_kernel(pos, ids, a0, a1, a2, a3, b0, b1, b2, b3, out, rows):
    x, core = pos[0], pos[1]
    for group, c in (((a0, a1, a2, a3), core), ((b0, b1, b2, b3), 1 - core)):
        for d, part in enumerate(group):
            block = 2 * ((x - d + 4) & 3) + c
            for n in range(32):
                rows[block, 4 * n : 4 * n + 4, 0:128] = part[n, 0:4, :]
                rows[block, 4 * n : 4 * n + 4, 128:256] = part[n, 4:8, :]
    name = column(ids[...]) - 32768
    at = 128 * ((name >> 2) & 7) + 4 * (name >> 5) + (name & 3)
    full = rows[...].reshape(1024, 256)
    hi = full.astype(BF16)
    rest = full - hi.astype(F32)
    mid = rest.astype(BF16)
    low = (rest - mid.astype(F32)).astype(BF16)
    for h in range(0, 1024, 256):
        pick = one_hot(iota((256, 1024), 1) == at[h : h + 256, :])
        out[h : h + 256, :] = mm(pick, hi) + (mm(pick, mid) + mm(pick, low))


def update_kernel(ds, done, pos, *refs):
    last = len(done) > 0
    parts, refs = refs[: 2 * len(ds)], refs[2 * len(ds) :]
    mem, cot, hot_mem, hot_cot, w_in, w_hid = refs[:6]
    refs = refs[6:]
    if last:
        olds, (own_hot, old_acc, new_h, grad, acc, new, sems) = refs[: len(done)], refs[len(done) :]
        stores = []
        for d, old in zip(done, olds):
            at = pl.ds(pl.multiple_of(256 * ((pos[0] - d + 4) & 3), 256), 256)
            stores.append(pltpu.make_async_copy(old, new_h.at[at], sems.at[d]))
            stores[-1].start()
    elif 0 in ds:
        new, hot, acc = refs
        old_acc = None
    else:
        old_acc, new, acc = refs
    if old_acc is not None:
        acc[...] = old_acc[...]
    x, core, rep = pos[0], pos[1], pos[2]
    q, k = iota((128, 512), 0), iota((128, 512), 1)
    sel_a = one_hot((k == 64 * rep + q) & (q < 64))
    q, k = iota((128, 256), 0), iota((128, 256), 1)
    sel_m = one_hot((k == 32 * rep + q - 64) & (q >= 64) & (q < 96))
    chips = [(x - d + 4) & 3 for d in ds]
    ats = [pl.ds(pl.multiple_of(256 * c, 256), 256) for c in chips]
    hot_ats = [pl.ds(pl.multiple_of(32 * c, 32), 32) for c in chips]
    rows = []
    for i in range(len(ds)):
        mine, other = parts[2 * i][...], parts[2 * i + 1][...]
        low = jnp.where(core == 0, mine, other)
        high = jnp.where(core == 0, other, mine)
        rows += [low[0:128], high[0:128], low[128:144], high[128:144]]
    wide = jnp.concatenate(rows, axis=0).astype(F32)
    live = wide[:, 0:1] < DEAD * 0.5
    a = jnp.where(live, wide, 0.0).astype(BF16)
    m = jnp.concatenate([v for h, k in zip(ats, hot_ats) for v in (mem[h, :], hot_mem[k, :])], axis=0)
    g = jnp.concatenate([v for h, k in zip(ats, hot_ats) for v in (cot[h, :], hot_cot[k, :])], axis=0)
    reset, update, cand, hid_cand = gates(a, m, w_in[...], w_hid[...])
    fresh = jnp.where(live, (1.0 - update) * cand + update * m, m)
    for i, d in enumerate(ds):
        part = fresh[288 * i : 288 * i + 256, :]
        if last:
            new[256 * i : 256 * i + 256, :] = part
            stores.append(pltpu.make_async_copy(new.at[256 * i : 256 * i + 256], new_h.at[ats[i]], sems.at[d]))
            stores[-1].start()
        else:
            new[...] = part
            if d == 0:
                own = jnp.where(core == 0, fresh[256:264, :], fresh[272:280, :])
                hot[...] = jnp.concatenate([own[0:4, 0:128], own[0:4, 128:256]], axis=0)
    g = jnp.where(live, g, 0.0)
    d_cand = g * (1.0 - update) * (1.0 - cand * cand)
    d_upd = g * (m - cand) * update * (1.0 - update)
    d_reset = d_cand * hid_cand * reset * (1.0 - reset)
    left = (mm(sel_a, a, ((1,), (1,))) + mm(sel_m, m.astype(BF16), ((1,), (1,)))).astype(BF16)
    for j, v in enumerate((d_reset, d_upd, d_cand, d_cand * reset)):
        hi = v.astype(BF16)
        low = (v - hi.astype(F32)).astype(BF16)
        part = mm(left, hi) + mm(left, low)
        cols = slice(256 * j, 256 * j + 256)
        if old_acc is None:
            acc[:, cols] = part
        else:
            acc[:, cols] += part
    if last:
        total = acc[...] * GRAD_SCALE
        third = jnp.where(iota((128, 256), 0) < 64, total[:, 512:768], total[:, 768:1024])
        total = jnp.concatenate([total[:, 0:512], third], axis=1)
        for p in range(32):
            i, j = p // 2, p % 2
            grad[p, :, 0:384] = total[8 * i : 8 * i + 8, 384 * j : 384 * j + 384]
            grad[p, :, 384:512] = own_hot[...]
        for c in stores:
            c.wait()


def piece_kernel(parts, out, hot):
    total = parts[0, :, 0:384]
    for k in range(1, 32):
        total = total + parts[k, :, 0:384]
    for k in range(32):
        out[k] = total
        hot[k] = parts[k, :, 384:512]


def place_kernel(other, pos, a0, a1, a2, a3, *refs):
    g_in, g_hid, both, sems = refs[-4:]
    x = pos[0]
    core = 1 - pos[1] if other else pos[1]
    stores = []
    for d, part in enumerate((a0, a1, a2, a3)):
        block = 2 * ((x - d + 4) & 3) + core
        for p in range(24):
            i, j = p // 2, p % 2
            both[96 * d + 8 * i : 96 * d + 8 * i + 8, 384 * j : 384 * j + 384] = part[p]
        for rows, at, dst in (
            (64, 96 * d, g_in.at[pl.ds(pl.multiple_of(block * 64, 64), 64)]),
            (32, 96 * d + 64, g_hid.at[pl.ds(pl.multiple_of(block * 32, 32), 32)]),
        ):
            stores.append(pltpu.make_async_copy(both.at[at : at + rows], dst, sems.at[len(stores)]))
            stores[-1].start()
    for c in stores:
        c.wait()


def swap_core(v):
    return lax.ppermute(v, "rep", [(k, k ^ 1) for k in range(8)])


def shift_x(v, d):
    return lax.ppermute(v, "rep", [(k, (k + 2 * d) % 8) for k in range(8)])


def gather_rep(v):
    own = [v] + [shift_x(v, d) for d in (1, 2, 3)]
    return own + [swap_core(u) for u in own]


def message_call(*args):
    sds = jax.ShapeDtypeStruct
    return call(
        message_kernel,
        (sds((32, 144, 128), BF16), sds((96, 512), F32)),
        (SM,) + (HB,) * 11,
        args,
        (
            pltpu.VMEM((1024, 256), F32), pltpu.VMEM((1024, 128), BF16), pltpu.VMEM((512, 512), BF16),
            pltpu.VMEM((1, 1024), I32), pltpu.VMEM((1, 1024), I32), pltpu.VMEM((1, 1024), I32),
            pltpu.VMEM((32, 32), I32), pltpu.VMEM((1, 32), I32), pltpu.VMEM((1, 128), F32),
            pltpu.VMEM((1, 128), F32), pltpu.VMEM((1, 512), F32),
            pltpu.VMEM((1024, 128), BF16), pltpu.VMEM((1024, 512), BF16), pltpu.VMEM((32, 144, 128), BF16),
            pltpu.VMEM((1024, 8), I32),
            pltpu.SemaphoreType.DMA((15,)),
        ),
        (ANY, VM),
        63,
    )


def last_update(pos, parts, shared, olds, hot_own, acc):
    sds = jax.ShapeDtypeStruct
    return call(
        functools.partial(update_kernel, (3, 2, 1), (0,)),
        (sds((1024, 256), F32), sds((32, 8, 512), F32)),
        (SM,),
        (pos, *parts, *shared, *olds, hot_own, acc),
        (pltpu.VMEM((128, 1024), F32), pltpu.VMEM((768, 256), F32), pltpu.SemaphoreType.DMA((4,))),
        (ANY, VM),
    )


def on_device(
    memory,
    hot_memory,
    cot_cold,
    cot_hot,
    src_local,
    dst_ids,
    times,
    edge_feat,
    cold_list,
    cold_count,
    hot_ids,
    time_freq,
    time_phase,
    w_msg,
    b_msg,
    w_in,
    w_hid,
):
    node = lax.axis_index("node")
    rep = lax.axis_index("rep")
    pos = jnp.stack([rep // 2, rep % 2, rep]).astype(I32)
    sds = jax.ShapeDtypeStruct

    chip, core = rep // 2, rep % 2
    send, hot = message_call(
        node.astype(I32)[None], memory, edge_feat, w_msg, src_local[None, :], times[None, :],
        dst_ids[None, :], cold_list, cold_count[None, :], time_freq[None, :], time_phase[None, :],
        b_msg[None, :],
    )
    recv = lax.all_to_all(send, "node", split_axis=0, concat_axis=0, tiled=True)

    hot = hot + swap_core(hot)
    spill = lax.dynamic_slice_in_dim(hot, 64 + 16 * core, 16, 0)
    spill = lax.ppermute(spill, "node", [(k, (k + 1) % 32) for k in range(32)])
    k = jnp.arange(128, dtype=I32)
    want = 32768 + 32 * node + 4 * (k // 16) + k % 4
    at = jnp.sum(jnp.where(want[:, None] == hot_ids[None, :], jnp.arange(1024, dtype=I32)[None, :], 0), axis=1)
    hot_mem = jnp.take(hot_memory, at, axis=0, mode="clip")
    hot_cot = jnp.take(cot_hot, at, axis=0, mode="clip")

    recv, hot_mem, hot_cot, _ = lax.optimization_barrier((recv, hot_mem, hot_cot, spill))
    block = sds((136, 512), F32)
    parts = call(
        cold_kernel,
        (block,) * 4,
        (SM,),
        (pos, recv, swap_core(recv), hot.reshape(12, 8, 512), spill.reshape(2, 8, 512)),
    )
    parts = [parts[0]] + [shift_x(parts[d], d) for d in (1, 2, 3)]
    agg = call(
        agg_kernel,
        sds((144, 512), BF16),
        (ANY, ANY, ANY),
        (*parts[1:], parts[0]),
        (pltpu.VMEM((3, 136, 512), F32), pltpu.VMEM((144, 512), BF16), pltpu.SemaphoreType.DMA((4,))),
        ANY,
    )
    near, far, back = [shift_x(agg, d) for d in (1, 2, 3)]
    shared = (memory, cot_cold, hot_mem, hot_cot, w_in, w_hid)
    rows, sums = sds((256, 256), F32), sds((128, 1024), F32)
    new_own, hot_own, acc = call(
        functools.partial(update_kernel, (0,), ()),
        (rows, sds((8, 128), F32), sums),
        (SM,),
        (pos, agg, swap_core(agg), *shared),
    )
    near, far, back, new_own = lax.optimization_barrier((near, far, back, new_own))
    parts = (back, swap_core(back), far, swap_core(far), near, swap_core(near))
    new_memory, grad = last_update(pos, parts, shared, (new_own,), hot_own, acc)

    grad = lax.all_to_all(grad, "node", split_axis=0, concat_axis=0, tiled=True)
    grad, hot_new = call(piece_kernel, (sds((32, 8, 384), F32), sds((32, 8, 128), F32)), (), (grad,))
    grad = lax.all_to_all(grad, "node", split_axis=0, concat_axis=0, tiled=True)
    hot_parts = gather_rep(hot_new)
    grad, hot_parts = lax.optimization_barrier((grad, hot_parts))
    new_hot = call(
        hot_place_kernel,
        sds((1024, 256), F32),
        (SM,),
        (pos, hot_ids[None, :], *hot_parts),
        (pltpu.VMEM((8, 128, 256), F32),),
    )
    own = [grad[0:24]] + [shift_x(grad[0:24], d) for d in (1, 2, 3)]
    own[2], new_hot = lax.optimization_barrier((own[2], new_hot))
    places = (pltpu.VMEM((384, 768), F32), pltpu.SemaphoreType.DMA((8,)))
    grads = (sds((512, 768), F32), sds((256, 768), F32))
    grads = call(
        functools.partial(place_kernel, False), grads, (SM,), (pos, *own), places, (ANY, ANY)
    )
    grad_in, grad_hid = call(
        functools.partial(place_kernel, True),
        tuple(sds(g.shape, F32) for g in grads),
        (SM, VM, VM, VM, VM, ANY, ANY),
        (pos, *[swap_core(v) for v in own], *grads),
        places,
        (ANY, ANY),
        aliases={5: 0, 6: 1},
    )
    return (new_memory, new_hot, grad_in, grad_hid)


def solution(mesh):
    in_specs = (
        P("node", None),
        P(),
        P("node", None),
        P(),
        P(("node", "rep")),
        P(("node", "rep")),
        P(("node", "rep")),
        P(("node", "rep"), None),
        P(("node", "rep"), None),
        P(("node", "rep")),
        P(),
        P(),
        P(),
        P(),
        P(),
        P(),
        P(),
    )
    out_specs = (P("node", None), P(), P(), P())
    return jax.shard_map(
        on_device, mesh=mesh, in_specs=in_specs, out_specs=out_specs, check_vma=False
    )
```

```python
import functools

import jax
import jax.numpy as jnp
from jax import lax
from jax.experimental import pallas as pl
from jax.experimental.pallas import tpu as pltpu
from jax.sharding import PartitionSpec as P

GRAD_SCALE = 1.0 / 64.0
DEAD = 2.0**100
F32, BF16, I32 = jnp.float32, jnp.bfloat16, jnp.int32
VM = pl.BlockSpec(memory_space=pltpu.VMEM)
SM = pl.BlockSpec(memory_space=pltpu.SMEM)
HB = pl.BlockSpec(memory_space=pltpu.HBM)
ANY = pl.BlockSpec(memory_space=pl.ANY)


def iota(shape, dim):
    return lax.broadcasted_iota(I32, shape, dim)


def one_hot(mask):
    return jnp.where(mask, 1.0, 0.0).astype(BF16)


def mm(a, b, dims=((1,), (0,))):
    return lax.dot_general(a, b, (dims, ((), ())), preferred_element_type=F32)


def call(body, out_shape, places, args, scratch=(), out_places=None, mib=48, aliases=None):
    if out_places is None:
        out_places = jax.tree.map(lambda _: VM, out_shape)
    return pl.pallas_call(
        body,
        out_shape=out_shape,
        in_specs=list(places) + [VM] * (len(args) - len(places)),
        out_specs=out_places,
        scratch_shapes=list(scratch),
        input_output_aliases=aliases or {},
        compiler_params=pltpu.CompilerParams(vmem_limit_bytes=mib * 1024 * 1024),
    )(*args)


def column(row):
    return jnp.broadcast_to(row, (8, row.shape[1])).T[:, 0:1]


def cosine(x):
    k = jnp.round(x * 0.15915494309189535)
    r = x - k * 6.28125
    r = r - k * 0.0019350051879882812
    r = r - k * 3.019916e-07
    u = 1.5707963267948966 - jnp.abs(r)
    u2 = u * u
    p = 2.6083159809786593e-06
    for c in (-0.00019810690719168633, 0.0083330785855650902, -0.16666659712791443, 1.0):
        p = p * u2 + c
    return u * p


def message_kernel(
    pos, mem_h, edge_h, w_h, src_h, times_h, dst_h, listed_h, used_h, freq_h, phase_h, b_h, send_h, hot,
    mem, edge, w, src, times, dst_v, listed, used, freq, phase, b, encs, msgs, out, cols, sems,
):
    loads = [
        pltpu.make_async_copy(h, v, sems.at[i])
        for i, (h, v) in enumerate(
            (
                (src_h, src), (times_h, times), (dst_h, dst_v), (listed_h, listed), (used_h, used),
                (freq_h, freq), (phase_h, phase), (b_h, b), (mem_h, mem), (edge_h, edge), (w_h, w),
            )
        )
    ]
    for c in loads:
        c.start()
    for c in loads[:8]:
        c.wait()
    n_ev, step = 1024, 256
    dst = dst_v[...]
    line = iota((8, n_ev), 0)
    packed = jnp.where(line == 0, src[...], jnp.where(line == 1, times[...], dst))
    cols[...] = packed.T
    slot = iota((32, 32), 0)
    eye = one_hot(slot == iota((32, 32), 1))
    names = listed[...]
    hi = mm(eye, (names >> 5).astype(F32).astype(BF16), ((1,), (1,)))
    lo = mm(eye, (names & 31).astype(F32).astype(BF16), ((1,), (1,)))
    names = jnp.where(slot < used[...], (hi * 32.0 + lo).astype(I32), -1)
    encs[...] = cosine(cols[:, 1:2].astype(F32) * freq[...] + phase[...]).astype(BF16)
    for c in loads[8:]:
        c.wait()
    mem16 = mem[...].astype(BF16)
    for e in range(0, n_ev, step):
        at = cols[e : e + step, :]
        src_mem = mm(one_hot(iota((step, 1024), 1) == at[:, 0:1]), mem16).astype(BF16)
        raw = jnp.concatenate([src_mem, edge[e : e + step, :], encs[e : e + step, :]], axis=1)
        pre = mm(raw, w[...]) + b[...]
        msgs[e : e + step, :] = (pre * jax.nn.sigmoid(pre)).astype(BF16)
    row = dst & 1023
    facts = jnp.where(line == 0, row >> 5, jnp.where(line == 1, row & 31, jnp.where(line == 2, 1, 0)))
    facts = facts.astype(F32).astype(BF16)
    lane = iota((8, 128), 1)
    stores = []
    for t in range(4):
        pick = jnp.concatenate(
            [one_hot(iota((32, n_ev), 1) == names[:, o : o + 1]) for o in range(8 * t, 8 * t + 8)], axis=0
        )
        moved = mm(pick, msgs[...]).astype(BF16)
        tail = mm(facts, pick, ((1,), (1,)))
        for i in range(8):
            o = 8 * t + i
            for q in range(4):
                out[o, 32 * q : 32 * q + 32, :] = moved[32 * i : 32 * i + 32, 128 * q : 128 * q + 128]
            k = o % 4
            own = tail[:, 128 * (i // 4) : 128 * (i // 4) + 128]
            own = jnp.where((lane >> 5) == k, own, 0.0)
            own = pltpu.roll(own, ((pos[0] & 3) + 4 - k) * 32 & 127, 1)
            out[o, 128:144, :] = jnp.concatenate([own, jnp.zeros((8, 128), F32)], axis=0).astype(BF16)
        here = pl.ds(8 * t, 8)
        stores.append(pltpu.make_async_copy(out.at[here], send_h.at[here], sems.at[11 + t]))
        stores[-1].start()
    window = jnp.where(dst >= 32768, (dst - 32768 - 32 * pos[0] + 1024) & 1023, -1)
    q = iota((96, n_ev), 0)
    block = jnp.where(q < 64, 2 * ((q >> 3) & 3) + ((q >> 5) & 1), 8 + 2 * ((q >> 3) & 1) + ((q >> 4) & 1))
    hit = one_hot(4 * block + (q & 3) == window)
    total = mm(hit, msgs[...])
    count = jnp.sum(hit.astype(F32), axis=1, keepdims=True)
    hot[...] = jnp.where((iota((96, 512), 0) & 7) < 4, total, count)
    for c in stores:
        c.wait()


def cold_kernel(pos, own, peer, hot, spill, o0, o1, o2, o3):
    q = iota((512, 128), 0)
    want = (q & 127) + 256 * ((pos[0] + (q >> 7)) & 3) + 128 * pos[1]
    hits = []
    for got in (own, peer):
        for g in range(8):
            tail = got[4 * g, 128:144, :].astype(F32)
            for i in range(1, 4):
                tail = tail + got[4 * g + i, 128:144, :].astype(F32)
            row = jnp.where(tail[2:3, :] > 0.5, tail[0:1, :] * 32.0 + tail[1:2, :], -1.0).astype(I32)
            hits.append(one_hot(want == row))
    hit = jnp.concatenate(hits, axis=1)
    count = mm(jnp.ones((8, 2048), BF16), hit, ((1,), (1,)))
    for n in range(2):
        cols = slice(256 * n, 256 * n + 256)
        msgs = jnp.concatenate(
            [
                jnp.concatenate(
                    [got[:, 32 * k : 32 * k + 32, :].reshape(1024, 128) for k in (2 * n, 2 * n + 1)], axis=1
                )
                for got in (own, peer)
            ],
            axis=0,
        )
        total = mm(hit, msgs)
        for d, to in enumerate((o0, o1, o2, o3)):
            here = slice(128 * d, 128 * d + 128)
            to[0:128, cols] = total[here, :]
            j = (pos[0] + d) & 3
            tile = hot[4 * pos[1] + j, :, cols] + jnp.where(j < 2, 1.0, 0.0) * spill[j & 1, :, cols]
            if n == 0:
                rows = jnp.concatenate([count[:, here], tile[:, 128:256]], axis=1)
                tile = jnp.where((iota((8, 256), 0) >= 4) & (iota((8, 256), 1) < 128), rows, tile)
            to[128:136, cols] = tile


def agg_kernel(p1_h, p2_h, p3_h, p0, out_h, part, out, sems):
    loads = [pltpu.make_async_copy(h, part.at[i], sems.at[i]) for i, h in enumerate((p1_h, p2_h, p3_h))]
    for c in loads:
        c.start()
    for c in loads:
        c.wait()
    total = p0[...] + part[0] + part[1] + part[2]
    count = column(total[132:133, 0:128])
    agg = jnp.where(count > 0.0, total[0:128, :] / jnp.maximum(count, 1.0), DEAD)
    out[0:128, :] = agg.astype(BF16)
    count = total[132:136, 128:129]
    agg = jnp.where(count > 0.0, total[128:132, :] / jnp.maximum(count, 1.0), DEAD)
    out[128:144, :] = jnp.concatenate([agg, jnp.full((12, 512), DEAD, F32)], axis=0).astype(BF16)
    store = pltpu.make_async_copy(out, out_h, sems.at[3])
    store.start()
    store.wait()


def gates(agg, mem, w_in, w_hid):
    gi = mm(agg, w_in)
    gh = mm(mem.astype(BF16), w_hid)
    reset = jax.nn.sigmoid(gi[:, 0:256] + gh[:, 0:256])
    update = jax.nn.sigmoid(gi[:, 256:512] + gh[:, 256:512])
    cand = jnp.tanh(gi[:, 512:768] + reset * gh[:, 512:768])
    return reset, update, cand, gh[:, 512:768]


def hot_place_kernel(pos, ids, a0, a1, a2, a3, b0, b1, b2, b3, out, rows):
    x, core = pos[0], pos[1]
    for group, c in (((a0, a1, a2, a3), core), ((b0, b1, b2, b3), 1 - core)):
        for d, part in enumerate(group):
            block = 2 * ((x - d + 4) & 3) + c
            for n in range(32):
                rows[block, 4 * n : 4 * n + 4, 0:128] = part[n, 0]
                rows[block, 4 * n : 4 * n + 4, 128:256] = part[n, 1]
    name = column(ids[...]) - 32768
    at = 128 * ((name >> 2) & 7) + 4 * (name >> 5) + (name & 3)
    full = rows[...].reshape(1024, 256)
    hi = full.astype(BF16)
    rest = full - hi.astype(F32)
    mid = rest.astype(BF16)
    low = (rest - mid.astype(F32)).astype(BF16)
    for h in range(0, 1024, 256):
        pick = one_hot(iota((256, 1024), 1) == at[h : h + 256, :])
        out[h : h + 256, :] = mm(pick, hi) + (mm(pick, mid) + mm(pick, low))


def update_kernel(ds, done, pos, *refs):
    last = len(done) > 0
    parts, refs = refs[: 2 * len(ds)], refs[2 * len(ds) :]
    mem, cot, hot_mem, hot_cot, w_in, w_hid = refs[:6]
    refs = refs[6:]
    if last:
        olds, (own_hot, old_acc, new_h, grad, acc, new, flat, sems) = refs[: len(done)], refs[len(done) :]
        stores = []
        for d, old in zip(done, olds):
            at = pl.ds(pl.multiple_of(256 * ((pos[0] - d + 4) & 3), 256), 256)
            stores.append(pltpu.make_async_copy(old, new_h.at[at], sems.at[d]))
            stores[-1].start()
    elif 0 in ds:
        new, hot, acc = refs
        old_acc = None
    else:
        old_acc, new, acc = refs
    if old_acc is not None:
        acc[...] = old_acc[...]
    x, core, rep = pos[0], pos[1], pos[2]
    q, k = iota((128, 512), 0), iota((128, 512), 1)
    sel_a = one_hot((k == 64 * rep + q) & (q < 64))
    q, k = iota((128, 256), 0), iota((128, 256), 1)
    sel_m = one_hot((k == 32 * rep + q - 64) & (q >= 64) & (q < 96))
    chips = [(x - d + 4) & 3 for d in ds]
    ats = [pl.ds(pl.multiple_of(256 * c, 256), 256) for c in chips]
    hot_ats = [pl.ds(pl.multiple_of(32 * c, 32), 32) for c in chips]
    rows = []
    for i in range(len(ds)):
        mine, other = parts[2 * i][...], parts[2 * i + 1][...]
        low = jnp.where(core == 0, mine, other)
        high = jnp.where(core == 0, other, mine)
        rows += [low[0:128], high[0:128], low[128:144], high[128:144]]
    wide = jnp.concatenate(rows, axis=0).astype(F32)
    live = wide[:, 0:1] < DEAD * 0.5
    a = jnp.where(live, wide, 0.0).astype(BF16)
    m = jnp.concatenate([v for h, k in zip(ats, hot_ats) for v in (mem[h, :], hot_mem[k, :])], axis=0)
    g = jnp.concatenate([v for h, k in zip(ats, hot_ats) for v in (cot[h, :], hot_cot[k, :])], axis=0)
    reset, update, cand, hid_cand = gates(a, m, w_in[...], w_hid[...])
    fresh = jnp.where(live, (1.0 - update) * cand + update * m, m)
    for i, d in enumerate(ds):
        part = fresh[288 * i : 288 * i + 256, :]
        if last:
            new[256 * i : 256 * i + 256, :] = part
            stores.append(pltpu.make_async_copy(new.at[256 * i : 256 * i + 256], new_h.at[ats[i]], sems.at[d]))
            stores[-1].start()
        else:
            new[...] = part
            if d == 0:
                own = jnp.where(core == 0, fresh[256:264, :], fresh[272:280, :])
                hot[...] = jnp.concatenate([own[0:4, 0:128], own[0:4, 128:256]], axis=0)
    g = jnp.where(live, g, 0.0)
    d_cand = g * (1.0 - update) * (1.0 - cand * cand)
    d_upd = g * (m - cand) * update * (1.0 - update)
    d_reset = d_cand * hid_cand * reset * (1.0 - reset)
    left = (mm(sel_a, a, ((1,), (1,))) + mm(sel_m, m.astype(BF16), ((1,), (1,)))).astype(BF16)
    for j, v in enumerate((d_reset, d_upd, d_cand, d_cand * reset)):
        hi = v.astype(BF16)
        low = (v - hi.astype(F32)).astype(BF16)
        part = mm(left, hi) + mm(left, low)
        cols = slice(256 * j, 256 * j + 256)
        if old_acc is None:
            acc[:, cols] = part
        else:
            acc[:, cols] += part
    if last:
        total = acc[...] * GRAD_SCALE
        third = jnp.where(iota((128, 256), 0) < 64, total[:, 512:768], total[:, 768:1024])
        total = jnp.concatenate([total[:, 0:512], third], axis=1)
        for c in range(6):
            flat[96 * c : 96 * c + 96, :] = total[0:96, 128 * c : 128 * c + 128]
        flat[576:640, :] = jnp.zeros((64, 128), F32)
        for p in range(32):
            for j in range(5):
                grad[p, j] = flat[20 * p + 4 * j : 20 * p + 4 * j + 4, :]
            for j in range(2):
                grad[p, 5 + j] = own_hot[4 * j : 4 * j + 4, :]
        for c in stores:
            c.wait()


def piece_kernel(parts, out, hot):
    for j in range(5):
        total = parts[0, j]
        for k in range(1, 32):
            total = total + parts[k, j]
        for k in range(32):
            out[k, j] = total
    for k in range(32):
        hot[k] = parts[k, 5:7]


def place_kernel(other, pos, a0, a1, a2, a3, *refs):
    g_in, g_hid, both, sems = refs[-4:]
    x = pos[0]
    core = 1 - pos[1] if other else pos[1]
    stores = []
    for d, part in enumerate((a0, a1, a2, a3)):
        block = 2 * ((x - d + 4) & 3) + core
        for k in range(144):
            i, c = 4 * k % 96, 4 * k // 96
            both[96 * d + i : 96 * d + i + 4, 128 * c : 128 * c + 128] = part[k // 5, k % 5]
        for rows, at, dst in (
            (64, 96 * d, g_in.at[pl.ds(pl.multiple_of(block * 64, 64), 64)]),
            (32, 96 * d + 64, g_hid.at[pl.ds(pl.multiple_of(block * 32, 32), 32)]),
        ):
            stores.append(pltpu.make_async_copy(both.at[at : at + rows], dst, sems.at[len(stores)]))
            stores[-1].start()
    for c in stores:
        c.wait()


def swap_core(v):
    return lax.ppermute(v, "rep", [(k, k ^ 1) for k in range(8)])


def shift_x(v, d):
    return lax.ppermute(v, "rep", [(k, (k + 2 * d) % 8) for k in range(8)])


def gather_rep(v):
    own = [v] + [shift_x(v, d) for d in (1, 2, 3)]
    return own + [swap_core(u) for u in own]


def message_call(*args):
    sds = jax.ShapeDtypeStruct
    return call(
        message_kernel,
        (sds((32, 144, 128), BF16), sds((96, 512), F32)),
        (SM,) + (HB,) * 11,
        args,
        (
            pltpu.VMEM((1024, 256), F32), pltpu.VMEM((1024, 128), BF16), pltpu.VMEM((512, 512), BF16),
            pltpu.VMEM((1, 1024), I32), pltpu.VMEM((1, 1024), I32), pltpu.VMEM((1, 1024), I32),
            pltpu.VMEM((32, 32), I32), pltpu.VMEM((1, 32), I32), pltpu.VMEM((1, 128), F32),
            pltpu.VMEM((1, 128), F32), pltpu.VMEM((1, 512), F32),
            pltpu.VMEM((1024, 128), BF16), pltpu.VMEM((1024, 512), BF16), pltpu.VMEM((32, 144, 128), BF16),
            pltpu.VMEM((1024, 8), I32),
            pltpu.SemaphoreType.DMA((15,)),
        ),
        (ANY, VM),
        63,
    )


def last_update(pos, parts, shared, olds, hot_own, acc):
    sds = jax.ShapeDtypeStruct
    return call(
        functools.partial(update_kernel, (3, 2, 1), (0,)),
        (sds((1024, 256), F32), sds((32, 7, 4, 128), F32)),
        (SM,),
        (pos, *parts, *shared, *olds, hot_own, acc),
        (
            pltpu.VMEM((128, 1024), F32), pltpu.VMEM((768, 256), F32), pltpu.VMEM((640, 128), F32),
            pltpu.SemaphoreType.DMA((4,)),
        ),
        (ANY, VM),
    )


def on_device(
    memory,
    hot_memory,
    cot_cold,
    cot_hot,
    src_local,
    dst_ids,
    times,
    edge_feat,
    cold_list,
    cold_count,
    hot_ids,
    time_freq,
    time_phase,
    w_msg,
    b_msg,
    w_in,
    w_hid,
):
    node = lax.axis_index("node")
    rep = lax.axis_index("rep")
    pos = jnp.stack([rep // 2, rep % 2, rep]).astype(I32)
    sds = jax.ShapeDtypeStruct

    chip, core = rep // 2, rep % 2
    send, hot = message_call(
        node.astype(I32)[None], memory, edge_feat, w_msg, src_local[None, :], times[None, :],
        dst_ids[None, :], cold_list, cold_count[None, :], time_freq[None, :], time_phase[None, :],
        b_msg[None, :],
    )
    recv = lax.all_to_all(send, "node", split_axis=0, concat_axis=0, tiled=True)

    hot = hot + swap_core(hot)
    spill = lax.dynamic_slice_in_dim(hot, 64 + 16 * core, 16, 0)
    spill = lax.ppermute(spill, "node", [(k, (k + 1) % 32) for k in range(32)])
    k = jnp.arange(128, dtype=I32)
    want = 32768 + 32 * node + 4 * (k // 16) + k % 4
    at = jnp.sum(jnp.where(want[:, None] == hot_ids[None, :], jnp.arange(1024, dtype=I32)[None, :], 0), axis=1)
    hot_mem = jnp.take(hot_memory, at, axis=0, mode="clip")
    hot_cot = jnp.take(cot_hot, at, axis=0, mode="clip")

    recv, hot_mem, hot_cot, _ = lax.optimization_barrier((recv, hot_mem, hot_cot, spill))
    block = sds((136, 512), F32)
    parts = call(
        cold_kernel,
        (block,) * 4,
        (SM,),
        (pos, recv, swap_core(recv), hot.reshape(12, 8, 512), spill.reshape(2, 8, 512)),
    )
    parts = [parts[0]] + [shift_x(parts[d], d) for d in (1, 2, 3)]
    agg = call(
        agg_kernel,
        sds((144, 512), BF16),
        (ANY, ANY, ANY),
        (parts[2], parts[3], parts[1], parts[0]),
        (pltpu.VMEM((3, 136, 512), F32), pltpu.VMEM((144, 512), BF16), pltpu.SemaphoreType.DMA((4,))),
        ANY,
    )
    near, far, back = [shift_x(agg, d) for d in (1, 2, 3)]
    shared = (memory, cot_cold, hot_mem, hot_cot, w_in, w_hid)
    rows, sums = sds((256, 256), F32), sds((128, 1024), F32)
    new_own, hot_own, acc = call(
        functools.partial(update_kernel, (0,), ()),
        (rows, sds((8, 128), F32), sums),
        (SM,),
        (pos, agg, swap_core(agg), *shared),
    )
    far, back, near, new_own = lax.optimization_barrier((far, back, near, new_own))
    parts = (back, swap_core(back), far, swap_core(far), near, swap_core(near))
    new_memory, grad = last_update(pos, parts, shared, (new_own,), hot_own, acc)

    grad = lax.all_to_all(grad, "node", split_axis=0, concat_axis=0, tiled=True)
    grad, hot_new = call(piece_kernel, (sds((32, 5, 4, 128), F32), sds((32, 2, 4, 128), F32)), (), (grad,))
    grad = lax.all_to_all(grad, "node", split_axis=0, concat_axis=0, tiled=True)
    hot_parts = gather_rep(hot_new)
    grad, hot_parts = lax.optimization_barrier((grad, hot_parts))
    new_hot = call(
        hot_place_kernel,
        sds((1024, 256), F32),
        (SM,),
        (pos, hot_ids[None, :], *hot_parts),
        (pltpu.VMEM((8, 128, 256), F32),),
    )
    own = [grad[0:29]] + [shift_x(grad[0:29], d) for d in (1, 2, 3)]
    own[2], new_hot = lax.optimization_barrier((own[2], new_hot))
    places = (pltpu.VMEM((384, 768), F32), pltpu.SemaphoreType.DMA((8,)))
    grads = (sds((512, 768), F32), sds((256, 768), F32))
    grads = call(
        functools.partial(place_kernel, False), grads, (SM,), (pos, *own), places, (ANY, ANY)
    )
    grad_in, grad_hid = call(
        functools.partial(place_kernel, True),
        tuple(sds(g.shape, F32) for g in grads),
        (SM, VM, VM, VM, VM, ANY, ANY),
        (pos, *[swap_core(v) for v in own], *grads),
        places,
        (ANY, ANY),
        aliases={5: 0, 6: 1},
    )
    return (new_memory, new_hot, grad_in, grad_hid)


def solution(mesh):
    in_specs = (
        P("node", None),
        P(),
        P("node", None),
        P(),
        P(("node", "rep")),
        P(("node", "rep")),
        P(("node", "rep")),
        P(("node", "rep"), None),
        P(("node", "rep"), None),
        P(("node", "rep")),
        P(),
        P(),
        P(),
        P(),
        P(),
        P(),
        P(),
    )
    out_specs = (P("node", None), P(), P(), P())
    return jax.shard_map(
        on_device, mesh=mesh, in_specs=in_specs, out_specs=out_specs, check_vma=False
    )
```

```python
import functools

import jax
import jax.numpy as jnp
from jax import lax
from jax.experimental import pallas as pl
from jax.experimental.pallas import tpu as pltpu
from jax.sharding import PartitionSpec as P

GRAD_SCALE = 1.0 / 64.0
DEAD = 2.0**100
F32, BF16, I32 = jnp.float32, jnp.bfloat16, jnp.int32
VM = pl.BlockSpec(memory_space=pltpu.VMEM)
SM = pl.BlockSpec(memory_space=pltpu.SMEM)
HB = pl.BlockSpec(memory_space=pltpu.HBM)
ANY = pl.BlockSpec(memory_space=pl.ANY)


def iota(shape, dim):
    return lax.broadcasted_iota(I32, shape, dim)


def one_hot(mask):
    return jnp.where(mask, 1.0, 0.0).astype(BF16)


def mm(a, b, dims=((1,), (0,))):
    return lax.dot_general(a, b, (dims, ((), ())), preferred_element_type=F32)


def call(body, out_shape, places, args, scratch=(), out_places=None, mib=48, aliases=None):
    if out_places is None:
        out_places = jax.tree.map(lambda _: VM, out_shape)
    return pl.pallas_call(
        body,
        out_shape=out_shape,
        in_specs=list(places) + [VM] * (len(args) - len(places)),
        out_specs=out_places,
        scratch_shapes=list(scratch),
        input_output_aliases=aliases or {},
        compiler_params=pltpu.CompilerParams(vmem_limit_bytes=mib * 1024 * 1024),
    )(*args)


def column(row):
    return jnp.broadcast_to(row, (8, row.shape[1])).T[:, 0:1]


def cosine(x):
    k = jnp.round(x * 0.15915494309189535)
    r = x - k * 6.28125
    r = r - k * 0.0019350051879882812
    r = r - k * 3.019916e-07
    u = 1.5707963267948966 - jnp.abs(r)
    u2 = u * u
    p = 2.6083159809786593e-06
    for c in (-0.00019810690719168633, 0.0083330785855650902, -0.16666659712791443, 1.0):
        p = p * u2 + c
    return u * p


def message_kernel(
    pos, mem_h, edge_h, w_h, src_h, times_h, dst_h, listed_h, used_h, freq_h, phase_h, b_h, send_h, hot,
    mem, edge, w, src, times, dst_v, listed, used, freq, phase, b, encs, msgs, out, cols, sems,
):
    loads = [
        pltpu.make_async_copy(h, v, sems.at[i])
        for i, (h, v) in enumerate(
            (
                (src_h, src), (times_h, times), (dst_h, dst_v), (listed_h, listed), (used_h, used),
                (freq_h, freq), (phase_h, phase), (b_h, b), (mem_h, mem), (edge_h, edge), (w_h, w),
            )
        )
    ]
    for c in loads:
        c.start()
    for c in loads[:8]:
        c.wait()
    n_ev, step = 1024, 256
    dst = dst_v[...]
    line = iota((8, n_ev), 0)
    packed = jnp.where(line == 0, src[...], jnp.where(line == 1, times[...], dst))
    cols[...] = packed.T
    slot = iota((32, 32), 0)
    eye = one_hot(slot == iota((32, 32), 1))
    names = listed[...]
    hi = mm(eye, (names >> 5).astype(F32).astype(BF16), ((1,), (1,)))
    lo = mm(eye, (names & 31).astype(F32).astype(BF16), ((1,), (1,)))
    names = jnp.where(slot < used[...], (hi * 32.0 + lo).astype(I32), -1)
    encs[...] = cosine(cols[:, 1:2].astype(F32) * freq[...] + phase[...]).astype(BF16)
    for c in loads[8:]:
        c.wait()
    mem16 = mem[...].astype(BF16)
    for e in range(0, n_ev, step):
        at = cols[e : e + step, :]
        src_mem = mm(one_hot(iota((step, 1024), 1) == at[:, 0:1]), mem16).astype(BF16)
        raw = jnp.concatenate([src_mem, edge[e : e + step, :], encs[e : e + step, :]], axis=1)
        pre = mm(raw, w[...]) + b[...]
        msgs[e : e + step, :] = (pre * jax.nn.sigmoid(pre)).astype(BF16)
    row = dst & 1023
    facts = jnp.where(line == 0, row >> 5, jnp.where(line == 1, row & 31, jnp.where(line == 2, 1, 0)))
    facts = facts.astype(F32).astype(BF16)
    lane = iota((8, 128), 1)
    stores = []
    for t in range(4):
        pick = jnp.concatenate(
            [one_hot(iota((32, n_ev), 1) == names[:, o : o + 1]) for o in range(8 * t, 8 * t + 8)], axis=0
        )
        moved = mm(pick, msgs[...]).astype(BF16)
        tail = mm(facts, pick, ((1,), (1,)))
        for i in range(8):
            o = 8 * t + i
            for q in range(4):
                out[o, 32 * q : 32 * q + 32, :] = moved[32 * i : 32 * i + 32, 128 * q : 128 * q + 128]
            k = o % 4
            own = tail[:, 128 * (i // 4) : 128 * (i // 4) + 128]
            own = jnp.where((lane >> 5) == k, own, 0.0)
            own = pltpu.roll(own, ((pos[0] & 3) + 4 - k) * 32 & 127, 1)
            out[o, 128:144, :] = jnp.concatenate([own, jnp.zeros((8, 128), F32)], axis=0).astype(BF16)
        here = pl.ds(8 * t, 8)
        stores.append(pltpu.make_async_copy(out.at[here], send_h.at[here], sems.at[11 + t]))
        stores[-1].start()
    window = jnp.where(dst >= 32768, (dst - 32768 - 32 * pos[0] + 1024) & 1023, -1)
    q = iota((96, n_ev), 0)
    block = jnp.where(q < 64, 2 * ((q >> 3) & 3) + ((q >> 5) & 1), 8 + 2 * ((q >> 3) & 1) + ((q >> 4) & 1))
    hit = one_hot(4 * block + (q & 3) == window)
    total = mm(hit, msgs[...])
    count = jnp.sum(hit.astype(F32), axis=1, keepdims=True)
    hot[...] = jnp.where((iota((96, 512), 0) & 7) < 4, total, count)
    for c in stores:
        c.wait()


def cold_hits(pos, got):
    q = iota((512, 128), 0)
    want = (q & 127) + 256 * ((pos[0] + (q >> 7)) & 3) + 128 * pos[1]
    hits = []
    for g in range(8):
        tail = got[4 * g, 128:144, :].astype(F32)
        for i in range(1, 4):
            tail = tail + got[4 * g + i, 128:144, :].astype(F32)
        row = jnp.where(tail[2:3, :] > 0.5, tail[0:1, :] * 32.0 + tail[1:2, :], -1.0).astype(I32)
        hits.append(one_hot(want == row))
    return jnp.concatenate(hits, axis=1)


def cold_sums(hit, got, n):
    msgs = [got[:, 32 * k : 32 * k + 32, :].reshape(1024, 128) for k in (2 * n, 2 * n + 1)]
    return mm(hit, jnp.concatenate(msgs, axis=1))


def own_cold_kernel(pos, own, sums, counts):
    hit = cold_hits(pos, own)
    counts[...] = mm(jnp.ones((8, 1024), BF16), hit, ((1,), (1,)))
    for n in range(2):
        sums[:, 256 * n : 256 * n + 256] = cold_sums(hit, own, n)


def cold_kernel(pos, peer, sums, counts, hot, spill, o0, o1, o2, o3):
    hit = cold_hits(pos, peer)
    count = counts[...] + mm(jnp.ones((8, 1024), BF16), hit, ((1,), (1,)))
    for n in range(2):
        cols = slice(256 * n, 256 * n + 256)
        total = sums[:, cols] + cold_sums(hit, peer, n)
        for d, to in enumerate((o0, o1, o2, o3)):
            here = slice(128 * d, 128 * d + 128)
            to[0:128, cols] = total[here, :]
            j = (pos[0] + d) & 3
            tile = hot[4 * pos[1] + j, :, cols] + jnp.where(j < 2, 1.0, 0.0) * spill[j & 1, :, cols]
            if n == 0:
                rows = jnp.concatenate([count[:, here], tile[:, 128:256]], axis=1)
                tile = jnp.where((iota((8, 256), 0) >= 4) & (iota((8, 256), 1) < 128), rows, tile)
            to[128:136, cols] = tile


def agg_kernel(p1_h, p2_h, p3_h, p0, out_h, part, out, sems):
    loads = [pltpu.make_async_copy(h, part.at[i], sems.at[i]) for i, h in enumerate((p1_h, p2_h, p3_h))]
    for c in loads:
        c.start()
    for c in loads:
        c.wait()
    total = p0[...] + part[0] + part[1] + part[2]
    count = column(total[132:133, 0:128])
    agg = jnp.where(count > 0.0, total[0:128, :] / jnp.maximum(count, 1.0), DEAD)
    out[0:128, :] = agg.astype(BF16)
    count = total[132:136, 128:129]
    agg = jnp.where(count > 0.0, total[128:132, :] / jnp.maximum(count, 1.0), DEAD)
    out[128:144, :] = jnp.concatenate([agg, jnp.full((12, 512), DEAD, F32)], axis=0).astype(BF16)
    store = pltpu.make_async_copy(out, out_h, sems.at[3])
    store.start()
    store.wait()


def gates(agg, mem, w_in, w_hid):
    gi = mm(agg, w_in)
    gh = mm(mem.astype(BF16), w_hid)
    reset = jax.nn.sigmoid(gi[:, 0:256] + gh[:, 0:256])
    update = jax.nn.sigmoid(gi[:, 256:512] + gh[:, 256:512])
    cand = jnp.tanh(gi[:, 512:768] + reset * gh[:, 512:768])
    return reset, update, cand, gh[:, 512:768]


def hot_place_kernel(pos, ids, a0, a1, a2, a3, b0, b1, b2, b3, out, rows):
    x, core = pos[0], pos[1]
    for group, c in (((a0, a1, a2, a3), core), ((b0, b1, b2, b3), 1 - core)):
        for d, part in enumerate(group):
            block = 2 * ((x - d + 4) & 3) + c
            for n in range(32):
                rows[block, 4 * n : 4 * n + 4, 0:128] = part[n, 0]
                rows[block, 4 * n : 4 * n + 4, 128:256] = part[n, 1]
    name = column(ids[...]) - 32768
    at = 128 * ((name >> 2) & 7) + 4 * (name >> 5) + (name & 3)
    full = rows[...].reshape(1024, 256)
    hi = full.astype(BF16)
    rest = full - hi.astype(F32)
    mid = rest.astype(BF16)
    low = (rest - mid.astype(F32)).astype(BF16)
    for h in range(0, 1024, 256):
        pick = one_hot(iota((256, 1024), 1) == at[h : h + 256, :])
        out[h : h + 256, :] = mm(pick, hi) + (mm(pick, mid) + mm(pick, low))


def update_kernel(ds, done, pos, *refs):
    last = len(done) > 0
    parts, refs = refs[: 2 * len(ds)], refs[2 * len(ds) :]
    mem, cot, hot_mem, hot_cot, w_in, w_hid = refs[:6]
    refs = refs[6:]
    if last:
        olds, (own_hot, old_acc, new_h, grad, acc, new, flat, sems) = refs[: len(done)], refs[len(done) :]
        stores = []
        for d, old in zip(done, olds):
            at = pl.ds(pl.multiple_of(256 * ((pos[0] - d + 4) & 3), 256), 256)
            stores.append(pltpu.make_async_copy(old, new_h.at[at], sems.at[d]))
            stores[-1].start()
    elif 0 in ds:
        new, hot, acc = refs
        old_acc = None
    else:
        old_acc, new, acc = refs
    if old_acc is not None:
        acc[...] = old_acc[...]
    x, core, rep = pos[0], pos[1], pos[2]
    q, k = iota((128, 512), 0), iota((128, 512), 1)
    sel_a = one_hot((k == 64 * rep + q) & (q < 64))
    q, k = iota((128, 256), 0), iota((128, 256), 1)
    sel_m = one_hot((k == 32 * rep + q - 64) & (q >= 64) & (q < 96))
    chips = [(x - d + 4) & 3 for d in ds]
    ats = [pl.ds(pl.multiple_of(256 * c, 256), 256) for c in chips]
    hot_ats = [pl.ds(pl.multiple_of(32 * c, 32), 32) for c in chips]
    rows = []
    for i in range(len(ds)):
        mine, other = parts[2 * i][...], parts[2 * i + 1][...]
        low = jnp.where(core == 0, mine, other)
        high = jnp.where(core == 0, other, mine)
        rows += [low[0:128], high[0:128], low[128:144], high[128:144]]
    wide = jnp.concatenate(rows, axis=0).astype(F32)
    live = wide[:, 0:1] < DEAD * 0.5
    a = jnp.where(live, wide, 0.0).astype(BF16)
    m = jnp.concatenate([v for h, k in zip(ats, hot_ats) for v in (mem[h, :], hot_mem[k, :])], axis=0)
    g = jnp.concatenate([v for h, k in zip(ats, hot_ats) for v in (cot[h, :], hot_cot[k, :])], axis=0)
    reset, update, cand, hid_cand = gates(a, m, w_in[...], w_hid[...])
    fresh = jnp.where(live, (1.0 - update) * cand + update * m, m)
    for i, d in enumerate(ds):
        part = fresh[288 * i : 288 * i + 256, :]
        if last:
            new[256 * i : 256 * i + 256, :] = part
            stores.append(pltpu.make_async_copy(new.at[256 * i : 256 * i + 256], new_h.at[ats[i]], sems.at[d]))
            stores[-1].start()
        else:
            new[...] = part
            if d == 0:
                own = jnp.where(core == 0, fresh[256:264, :], fresh[272:280, :])
                hot[...] = jnp.concatenate([own[0:4, 0:128], own[0:4, 128:256]], axis=0)
    g = jnp.where(live, g, 0.0)
    d_cand = g * (1.0 - update) * (1.0 - cand * cand)
    d_upd = g * (m - cand) * update * (1.0 - update)
    d_reset = d_cand * hid_cand * reset * (1.0 - reset)
    left = (mm(sel_a, a, ((1,), (1,))) + mm(sel_m, m.astype(BF16), ((1,), (1,)))).astype(BF16)
    for j, v in enumerate((d_reset, d_upd, d_cand, d_cand * reset)):
        hi = v.astype(BF16)
        low = (v - hi.astype(F32)).astype(BF16)
        part = mm(left, hi) + mm(left, low)
        cols = slice(256 * j, 256 * j + 256)
        if old_acc is None:
            acc[:, cols] = part
        else:
            acc[:, cols] += part
    if last:
        total = acc[...] * GRAD_SCALE
        third = jnp.where(iota((128, 256), 0) < 64, total[:, 512:768], total[:, 768:1024])
        total = jnp.concatenate([total[:, 0:512], third], axis=1)
        for c in range(6):
            flat[96 * c : 96 * c + 96, :] = total[0:96, 128 * c : 128 * c + 128]
        flat[576:640, :] = jnp.zeros((64, 128), F32)
        for p in range(32):
            for j in range(5):
                grad[p, j] = flat[20 * p + 4 * j : 20 * p + 4 * j + 4, :]
            for j in range(2):
                grad[p, 5 + j] = own_hot[4 * j : 4 * j + 4, :]
        for c in stores:
            c.wait()


def piece_kernel(parts, out, hot):
    for j in range(5):
        total = parts[0, j]
        for k in range(1, 32):
            total = total + parts[k, j]
        for k in range(32):
            out[k, j] = total
    for k in range(32):
        hot[k] = parts[k, 5:7]


def place_kernel(blocks, pos, *refs):
    parts, (g_in, g_hid, both, sems) = refs[: len(blocks)], refs[-4:]
    stores = []
    for n, ((d, other), part) in enumerate(zip(blocks, parts)):
        block = 2 * ((pos[0] - d + 4) & 3) + (1 - pos[1] if other else pos[1])
        for k in range(144):
            i, c = 4 * k % 96, 4 * k // 96
            both[96 * n + i : 96 * n + i + 4, 128 * c : 128 * c + 128] = part[k // 5, k % 5]
        for rows, at, dst in (
            (64, 96 * n, g_in.at[pl.ds(pl.multiple_of(block * 64, 64), 64)]),
            (32, 96 * n + 64, g_hid.at[pl.ds(pl.multiple_of(block * 32, 32), 32)]),
        ):
            stores.append(pltpu.make_async_copy(both.at[at : at + rows], dst, sems.at[len(stores)]))
            stores[-1].start()
    for c in stores:
        c.wait()


def swap_core(v):
    return lax.ppermute(v, "rep", [(k, k ^ 1) for k in range(8)])


def shift_x(v, d):
    return lax.ppermute(v, "rep", [(k, (k + 2 * d) % 8) for k in range(8)])


def gather_rep(v):
    own = [v] + [shift_x(v, d) for d in (1, 2, 3)]
    return own + [swap_core(u) for u in own]


def message_call(*args):
    sds = jax.ShapeDtypeStruct
    return call(
        message_kernel,
        (sds((32, 144, 128), BF16), sds((96, 512), F32)),
        (SM,) + (HB,) * 11,
        args,
        (
            pltpu.VMEM((1024, 256), F32), pltpu.VMEM((1024, 128), BF16), pltpu.VMEM((512, 512), BF16),
            pltpu.VMEM((1, 1024), I32), pltpu.VMEM((1, 1024), I32), pltpu.VMEM((1, 1024), I32),
            pltpu.VMEM((32, 32), I32), pltpu.VMEM((1, 32), I32), pltpu.VMEM((1, 128), F32),
            pltpu.VMEM((1, 128), F32), pltpu.VMEM((1, 512), F32),
            pltpu.VMEM((1024, 128), BF16), pltpu.VMEM((1024, 512), BF16), pltpu.VMEM((32, 144, 128), BF16),
            pltpu.VMEM((1024, 8), I32),
            pltpu.SemaphoreType.DMA((15,)),
        ),
        (ANY, VM),
        63,
    )


def last_update(pos, parts, shared, olds, hot_own, acc):
    sds = jax.ShapeDtypeStruct
    return call(
        functools.partial(update_kernel, (3, 2, 1), (0,)),
        (sds((1024, 256), F32), sds((32, 7, 4, 128), F32)),
        (SM,),
        (pos, *parts, *shared, *olds, hot_own, acc),
        (
            pltpu.VMEM((128, 1024), F32), pltpu.VMEM((768, 256), F32), pltpu.VMEM((640, 128), F32),
            pltpu.SemaphoreType.DMA((4,)),
        ),
        (ANY, VM),
    )


def on_device(
    memory,
    hot_memory,
    cot_cold,
    cot_hot,
    src_local,
    dst_ids,
    times,
    edge_feat,
    cold_list,
    cold_count,
    hot_ids,
    time_freq,
    time_phase,
    w_msg,
    b_msg,
    w_in,
    w_hid,
):
    node = lax.axis_index("node")
    rep = lax.axis_index("rep")
    pos = jnp.stack([rep // 2, rep % 2, rep]).astype(I32)
    sds = jax.ShapeDtypeStruct

    chip, core = rep // 2, rep % 2
    send, hot = message_call(
        node.astype(I32)[None], memory, edge_feat, w_msg, src_local[None, :], times[None, :],
        dst_ids[None, :], cold_list, cold_count[None, :], time_freq[None, :], time_phase[None, :],
        b_msg[None, :],
    )
    recv = lax.all_to_all(send, "node", split_axis=0, concat_axis=0, tiled=True)

    hot = hot + swap_core(hot)
    spill = lax.dynamic_slice_in_dim(hot, 64 + 16 * core, 16, 0)
    spill = lax.ppermute(spill, "node", [(k, (k + 1) % 32) for k in range(32)])
    k = jnp.arange(128, dtype=I32)
    want = 32768 + 32 * node + 4 * (k // 16) + k % 4
    at = jnp.sum(jnp.where(want[:, None] == hot_ids[None, :], jnp.arange(1024, dtype=I32)[None, :], 0), axis=1)
    hot_mem = jnp.take(hot_memory, at, axis=0, mode="clip")
    hot_cot = jnp.take(cot_hot, at, axis=0, mode="clip")

    recv, hot_mem, hot_cot, _ = lax.optimization_barrier((recv, hot_mem, hot_cot, spill))
    block = sds((136, 512), F32)
    peer = swap_core(recv)
    sums = call(own_cold_kernel, (sds((512, 512), F32), sds((8, 512), F32)), (SM,), (pos, recv))
    parts = call(
        cold_kernel,
        (block,) * 4,
        (SM,),
        (pos, peer, *sums, hot.reshape(12, 8, 512), spill.reshape(2, 8, 512)),
    )
    parts = [parts[0]] + [shift_x(parts[d], d) for d in (1, 2, 3)]
    agg = call(
        agg_kernel,
        sds((144, 512), BF16),
        (ANY, ANY, ANY),
        (parts[2], parts[3], parts[1], parts[0]),
        (pltpu.VMEM((3, 136, 512), F32), pltpu.VMEM((144, 512), BF16), pltpu.SemaphoreType.DMA((4,))),
        ANY,
    )
    near, far, back = [shift_x(agg, d) for d in (1, 2, 3)]
    shared = (memory, cot_cold, hot_mem, hot_cot, w_in, w_hid)
    rows, sums = sds((256, 256), F32), sds((128, 1024), F32)
    new_own, hot_own, acc = call(
        functools.partial(update_kernel, (0,), ()),
        (rows, sds((8, 128), F32), sums),
        (SM,),
        (pos, agg, swap_core(agg), *shared),
    )
    near, back, far, new_own = lax.optimization_barrier((near, back, far, new_own))
    parts = (back, swap_core(back), far, swap_core(far), near, swap_core(near))
    new_memory, grad = last_update(pos, parts, shared, (new_own,), hot_own, acc)

    grad = lax.all_to_all(grad, "node", split_axis=0, concat_axis=0, tiled=True)
    grad, hot_new = call(piece_kernel, (sds((32, 5, 4, 128), F32), sds((32, 2, 4, 128), F32)), (), (grad,))
    grad = lax.all_to_all(grad, "node", split_axis=0, concat_axis=0, tiled=True)
    hot_parts = gather_rep(hot_new)
    grad, hot_parts = lax.optimization_barrier((grad, hot_parts))
    new_hot = call(
        hot_place_kernel,
        sds((1024, 256), F32),
        (SM,),
        (pos, hot_ids[None, :], *hot_parts),
        (pltpu.VMEM((8, 128, 256), F32),),
    )
    own = [grad[0:29]] + [shift_x(grad[0:29], d) for d in (1, 2, 3)]
    grads = ()
    for blocks in (((0, False), (0, True)), tuple((d, False) for d in (2, 3, 1)), tuple((d, True) for d in (2, 3, 1))):
        parts = [swap_core(own[d]) if other else own[d] for d, other in blocks]
        n = len(parts)
        grads = call(
            functools.partial(place_kernel, blocks),
            (sds((512, 768), F32), sds((256, 768), F32)),
            (SM,) + (VM,) * n + (ANY,) * len(grads),
            (pos, *parts, *grads),
            (pltpu.VMEM((96 * n, 768), F32), pltpu.SemaphoreType.DMA((2 * n,))),
            (ANY, ANY),
            aliases={n + 1: 0, n + 2: 1} if grads else {},
        )
        if n == 2:
            own[2], own[3], own[1], new_hot, *grads = lax.optimization_barrier(
                (own[2], own[3], own[1], new_hot, *grads)
            )
    grad_in, grad_hid = grads
    return (new_memory, new_hot, grad_in, grad_hid)


def solution(mesh):
    in_specs = (
        P("node", None),
        P(),
        P("node", None),
        P(),
        P(("node", "rep")),
        P(("node", "rep")),
        P(("node", "rep")),
        P(("node", "rep"), None),
        P(("node", "rep"), None),
        P(("node", "rep")),
        P(),
        P(),
        P(),
        P(),
        P(),
        P(),
        P(),
    )
    out_specs = (P("node", None), P(), P(), P())
    return jax.shard_map(
        on_device, mesh=mesh, in_specs=in_specs, out_specs=out_specs, check_vma=False
    )
```

```python
import functools

import jax
import jax.numpy as jnp
from jax import lax
from jax.experimental import pallas as pl
from jax.experimental.pallas import tpu as pltpu
from jax.sharding import PartitionSpec as P

GRAD_SCALE = 1.0 / 64.0
DEAD = 2.0**100
F32, BF16, I32 = jnp.float32, jnp.bfloat16, jnp.int32
VM = pl.BlockSpec(memory_space=pltpu.VMEM)
SM = pl.BlockSpec(memory_space=pltpu.SMEM)
HB = pl.BlockSpec(memory_space=pltpu.HBM)
ANY = pl.BlockSpec(memory_space=pl.ANY)


def iota(shape, dim):
    return lax.broadcasted_iota(I32, shape, dim)


def one_hot(mask):
    return jnp.where(mask, 1.0, 0.0).astype(BF16)


def mm(a, b, dims=((1,), (0,))):
    return lax.dot_general(a, b, (dims, ((), ())), preferred_element_type=F32)


def call(body, out_shape, places, args, scratch=(), out_places=None, mib=48, aliases=None):
    if out_places is None:
        out_places = jax.tree.map(lambda _: VM, out_shape)
    return pl.pallas_call(
        body,
        out_shape=out_shape,
        in_specs=list(places) + [VM] * (len(args) - len(places)),
        out_specs=out_places,
        scratch_shapes=list(scratch),
        input_output_aliases=aliases or {},
        compiler_params=pltpu.CompilerParams(vmem_limit_bytes=mib * 1024 * 1024),
    )(*args)


def column(row):
    return jnp.broadcast_to(row, (8, row.shape[1])).T[:, 0:1]


def cosine(x):
    k = jnp.round(x * 0.15915494309189535)
    r = x - k * 6.28125
    r = r - k * 0.0019350051879882812
    r = r - k * 3.019916e-07
    u = 1.5707963267948966 - jnp.abs(r)
    u2 = u * u
    p = 2.6083159809786593e-06
    for c in (-0.00019810690719168633, 0.0083330785855650902, -0.16666659712791443, 1.0):
        p = p * u2 + c
    return u * p


def message_kernel(
    pos, mem_h, edge_h, w_h, src_h, times_h, dst_h, listed_h, used_h, freq_h, phase_h, b_h, send_h, hot,
    mem, edge, w, src, times, dst_v, listed, used, freq, phase, b, encs, msgs, out, cols, sems,
):
    loads = [
        pltpu.make_async_copy(h, v, sems.at[i])
        for i, (h, v) in enumerate(
            (
                (src_h, src), (times_h, times), (dst_h, dst_v), (listed_h, listed), (used_h, used),
                (freq_h, freq), (phase_h, phase), (b_h, b), (mem_h, mem), (edge_h, edge), (w_h, w),
            )
        )
    ]
    for c in loads:
        c.start()
    for c in loads[:8]:
        c.wait()
    n_ev, step = 1024, 256
    dst = dst_v[...]
    line = iota((8, n_ev), 0)
    packed = jnp.where(line == 0, src[...], jnp.where(line == 1, times[...], dst))
    cols[...] = packed.T
    slot = iota((32, 32), 0)
    eye = one_hot(slot == iota((32, 32), 1))
    names = listed[...]
    hi = mm(eye, (names >> 5).astype(F32).astype(BF16), ((1,), (1,)))
    lo = mm(eye, (names & 31).astype(F32).astype(BF16), ((1,), (1,)))
    names = jnp.where(slot < used[...], (hi * 32.0 + lo).astype(I32), -1)
    encs[...] = cosine(cols[:, 1:2].astype(F32) * freq[...] + phase[...]).astype(BF16)
    for c in loads[8:]:
        c.wait()
    mem16 = mem[...].astype(BF16)
    for e in range(0, n_ev, step):
        at = cols[e : e + step, :]
        src_mem = mm(one_hot(iota((step, 1024), 1) == at[:, 0:1]), mem16).astype(BF16)
        raw = jnp.concatenate([src_mem, edge[e : e + step, :], encs[e : e + step, :]], axis=1)
        pre = mm(raw, w[...]) + b[...]
        msgs[e : e + step, :] = (pre * jax.nn.sigmoid(pre)).astype(BF16)
    row = dst & 1023
    facts = jnp.where(line == 0, row >> 5, jnp.where(line == 1, row & 31, jnp.where(line == 2, 1, 0)))
    facts = facts.astype(F32).astype(BF16)
    lane = iota((8, 128), 1)
    stores = []
    for t in range(4):
        pick = jnp.concatenate(
            [one_hot(iota((32, n_ev), 1) == names[:, o : o + 1]) for o in range(8 * t, 8 * t + 8)], axis=0
        )
        moved = mm(pick, msgs[...]).astype(BF16)
        tail = mm(facts, pick, ((1,), (1,)))
        for i in range(8):
            o = 8 * t + i
            for q in range(4):
                out[o, 32 * q : 32 * q + 32, :] = moved[32 * i : 32 * i + 32, 128 * q : 128 * q + 128]
            k = o % 4
            own = tail[:, 128 * (i // 4) : 128 * (i // 4) + 128]
            own = jnp.where((lane >> 5) == k, own, 0.0)
            own = pltpu.roll(own, ((pos[0] & 3) + 4 - k) * 32 & 127, 1)
            out[o, 128:144, :] = jnp.concatenate([own, jnp.zeros((8, 128), F32)], axis=0).astype(BF16)
        here = pl.ds(8 * t, 8)
        stores.append(pltpu.make_async_copy(out.at[here], send_h.at[here], sems.at[11 + t]))
        stores[-1].start()
    window = jnp.where(dst >= 32768, (dst - 32768 - 32 * pos[0] + 1024) & 1023, -1)
    q = iota((96, n_ev), 0)
    block = jnp.where(q < 64, 2 * ((q >> 3) & 3) + ((q >> 5) & 1), 8 + 2 * ((q >> 3) & 1) + ((q >> 4) & 1))
    hit = one_hot(4 * block + (q & 3) == window)
    total = mm(hit, msgs[...])
    count = jnp.sum(hit.astype(F32), axis=1, keepdims=True)
    hot[...] = jnp.where((iota((96, 512), 0) & 7) < 4, total, count)
    for c in stores:
        c.wait()


def cold_hits(pos, got):
    q = iota((512, 128), 0)
    want = (q & 127) + 256 * ((pos[0] + (q >> 7)) & 3) + 128 * pos[1]
    hits = []
    for g in range(8):
        tail = got[4 * g, 128:144, :].astype(F32)
        for i in range(1, 4):
            tail = tail + got[4 * g + i, 128:144, :].astype(F32)
        row = jnp.where(tail[2:3, :] > 0.5, tail[0:1, :] * 32.0 + tail[1:2, :], -1.0).astype(I32)
        hits.append(one_hot(want == row))
    return jnp.concatenate(hits, axis=1)


def cold_sums(hit, got, n):
    msgs = [got[:, 32 * k : 32 * k + 32, :].reshape(1024, 128) for k in (2 * n, 2 * n + 1)]
    return mm(hit, jnp.concatenate(msgs, axis=1))


def own_cold_kernel(pos, own, sums, counts):
    hit = cold_hits(pos, own)
    counts[...] = mm(jnp.ones((8, 1024), BF16), hit, ((1,), (1,)))
    for n in range(2):
        sums[:, 256 * n : 256 * n + 256] = cold_sums(hit, own, n)


def cold_kernel(pos, peer, sums, counts, hot, spill, o0, o1, o2, o3):
    hit = cold_hits(pos, peer)
    count = counts[...] + mm(jnp.ones((8, 1024), BF16), hit, ((1,), (1,)))
    for n in range(2):
        cols = slice(256 * n, 256 * n + 256)
        total = sums[:, cols] + cold_sums(hit, peer, n)
        for d, to in enumerate((o0, o1, o2, o3)):
            here = slice(128 * d, 128 * d + 128)
            to[0:128, cols] = total[here, :]
            j = (pos[0] + d) & 3
            tile = hot[4 * pos[1] + j, :, cols] + jnp.where(j < 2, 1.0, 0.0) * spill[j & 1, :, cols]
            if n == 0:
                rows = jnp.concatenate([count[:, here], tile[:, 128:256]], axis=1)
                tile = jnp.where((iota((8, 256), 0) >= 4) & (iota((8, 256), 1) < 128), rows, tile)
            to[128:136, cols] = tile


def agg_kernel(p1_h, p2_h, p3_h, p0, out_h, part, out, sems):
    loads = [pltpu.make_async_copy(h, part.at[i], sems.at[i]) for i, h in enumerate((p1_h, p2_h, p3_h))]
    for c in loads:
        c.start()
    for c in loads:
        c.wait()
    total = p0[...] + part[0] + part[1] + part[2]
    count = column(total[132:133, 0:128])
    agg = jnp.where(count > 0.0, total[0:128, :] / jnp.maximum(count, 1.0), DEAD)
    out[0:128, :] = agg.astype(BF16)
    count = total[132:136, 128:129]
    agg = jnp.where(count > 0.0, total[128:132, :] / jnp.maximum(count, 1.0), DEAD)
    out[128:144, :] = jnp.concatenate([agg, jnp.full((12, 512), DEAD, F32)], axis=0).astype(BF16)
    store = pltpu.make_async_copy(out, out_h, sems.at[3])
    store.start()
    store.wait()


def gates(agg, mem, w_in, w_hid):
    gi = mm(agg, w_in)
    gh = mm(mem.astype(BF16), w_hid)
    reset = jax.nn.sigmoid(gi[:, 0:256] + gh[:, 0:256])
    update = jax.nn.sigmoid(gi[:, 256:512] + gh[:, 256:512])
    cand = jnp.tanh(gi[:, 512:768] + reset * gh[:, 512:768])
    return reset, update, cand, gh[:, 512:768]


def hot_place_kernel(pos, ids, a0, a1, a2, a3, b0, b1, b2, b3, out, rows):
    x, core = pos[0], pos[1]
    for group, c in (((a0, a1, a2, a3), core), ((b0, b1, b2, b3), 1 - core)):
        for d, part in enumerate(group):
            block = 2 * ((x - d + 4) & 3) + c
            for n in range(32):
                rows[block, 4 * n : 4 * n + 4, 0:128] = part[n, 0]
                rows[block, 4 * n : 4 * n + 4, 128:256] = part[n, 1]
    name = column(ids[...]) - 32768
    at = 128 * ((name >> 2) & 7) + 4 * (name >> 5) + (name & 3)
    full = rows[...].reshape(1024, 256)
    hi = full.astype(BF16)
    rest = full - hi.astype(F32)
    mid = rest.astype(BF16)
    low = (rest - mid.astype(F32)).astype(BF16)
    for h in range(0, 1024, 256):
        pick = one_hot(iota((256, 1024), 1) == at[h : h + 256, :])
        out[h : h + 256, :] = mm(pick, hi) + (mm(pick, mid) + mm(pick, low))


def update_kernel(ds, done, pos, *refs):
    last = len(done) > 0
    parts, refs = refs[: 2 * len(ds)], refs[2 * len(ds) :]
    mem, cot, hot_mem, hot_cot, w_in, w_hid = refs[:6]
    refs = refs[6:]
    if last:
        olds, (own_hot, old_acc, new_h, grad, acc, new, flat, sems) = refs[: len(done)], refs[len(done) :]
        stores = []
        for d, old in zip(done, olds):
            at = pl.ds(pl.multiple_of(256 * ((pos[0] - d + 4) & 3), 256), 256)
            stores.append(pltpu.make_async_copy(old, new_h.at[at], sems.at[d]))
            stores[-1].start()
    elif 0 in ds:
        new, hot, acc = refs
        old_acc = None
    else:
        old_acc, new, acc = refs
    if old_acc is not None:
        acc[...] = old_acc[...]
    x, core, rep = pos[0], pos[1], pos[2]
    q, k = iota((128, 512), 0), iota((128, 512), 1)
    sel_a = one_hot((k == 64 * rep + q) & (q < 64))
    q, k = iota((128, 256), 0), iota((128, 256), 1)
    sel_m = one_hot((k == 32 * rep + q - 64) & (q >= 64) & (q < 96))
    chips = [(x - d + 4) & 3 for d in ds]
    ats = [pl.ds(pl.multiple_of(256 * c, 256), 256) for c in chips]
    hot_ats = [pl.ds(pl.multiple_of(32 * c, 32), 32) for c in chips]
    rows = []
    for i in range(len(ds)):
        mine, other = parts[2 * i][...], parts[2 * i + 1][...]
        low = jnp.where(core == 0, mine, other)
        high = jnp.where(core == 0, other, mine)
        rows += [low[0:128], high[0:128], low[128:144], high[128:144]]
    wide = jnp.concatenate(rows, axis=0).astype(F32)
    live = wide[:, 0:1] < DEAD * 0.5
    a = jnp.where(live, wide, 0.0).astype(BF16)
    m = jnp.concatenate([v for h, k in zip(ats, hot_ats) for v in (mem[h, :], hot_mem[k, :])], axis=0)
    g = jnp.concatenate([v for h, k in zip(ats, hot_ats) for v in (cot[h, :], hot_cot[k, :])], axis=0)
    reset, update, cand, hid_cand = gates(a, m, w_in[...], w_hid[...])
    fresh = jnp.where(live, (1.0 - update) * cand + update * m, m)
    for i, d in enumerate(ds):
        part = fresh[288 * i : 288 * i + 256, :]
        if last:
            new[256 * i : 256 * i + 256, :] = part
            stores.append(pltpu.make_async_copy(new.at[256 * i : 256 * i + 256], new_h.at[ats[i]], sems.at[d]))
            stores[-1].start()
        else:
            new[...] = part
            if d == 0:
                own = jnp.where(core == 0, fresh[256:264, :], fresh[272:280, :])
                hot[...] = jnp.concatenate([own[0:4, 0:128], own[0:4, 128:256]], axis=0)
    g = jnp.where(live, g, 0.0)
    d_cand = g * (1.0 - update) * (1.0 - cand * cand)
    d_upd = g * (m - cand) * update * (1.0 - update)
    d_reset = d_cand * hid_cand * reset * (1.0 - reset)
    left = (mm(sel_a, a, ((1,), (1,))) + mm(sel_m, m.astype(BF16), ((1,), (1,)))).astype(BF16)
    for j, v in enumerate((d_reset, d_upd, d_cand, d_cand * reset)):
        hi = v.astype(BF16)
        low = (v - hi.astype(F32)).astype(BF16)
        part = mm(left, hi) + mm(left, low)
        cols = slice(256 * j, 256 * j + 256)
        if old_acc is None:
            acc[:, cols] = part
        else:
            acc[:, cols] += part
    if last:
        total = acc[...] * GRAD_SCALE
        third = jnp.where(iota((128, 256), 0) < 64, total[:, 512:768], total[:, 768:1024])
        total = jnp.concatenate([total[:, 0:512], third], axis=1)
        for c in range(6):
            flat[96 * c : 96 * c + 96, :] = total[0:96, 128 * c : 128 * c + 128]
        flat[576:640, :] = jnp.zeros((64, 128), F32)
        for p in range(32):
            for j in range(5):
                grad[p, j] = flat[20 * p + 4 * j : 20 * p + 4 * j + 4, :]
            for j in range(2):
                grad[p, 5 + j] = own_hot[4 * j : 4 * j + 4, :]
        for c in stores:
            c.wait()


def piece_kernel(parts, out, hot):
    for j in range(5):
        total = parts[0, j]
        for k in range(1, 32):
            total = total + parts[k, j]
        for k in range(32):
            out[k, j] = total
    for k in range(32):
        hot[k] = parts[k, 5:7]


def place_kernel(blocks, pos, *refs):
    parts, (g_in, g_hid, both, sems) = refs[: len(blocks)], refs[-4:]
    stores = []
    for n, ((d, other), part) in enumerate(zip(blocks, parts)):
        block = 2 * ((pos[0] - d + 4) & 3) + (1 - pos[1] if other else pos[1])
        for k in range(144):
            i, c = 4 * k % 96, 4 * k // 96
            both[96 * n + i : 96 * n + i + 4, 128 * c : 128 * c + 128] = part[k // 5, k % 5]
        for rows, at, dst in (
            (64, 96 * n, g_in.at[pl.ds(pl.multiple_of(block * 64, 64), 64)]),
            (32, 96 * n + 64, g_hid.at[pl.ds(pl.multiple_of(block * 32, 32), 32)]),
        ):
            stores.append(pltpu.make_async_copy(both.at[at : at + rows], dst, sems.at[len(stores)]))
            stores[-1].start()
    for c in stores:
        c.wait()


def swap_core(v):
    return lax.ppermute(v, "rep", [(k, k ^ 1) for k in range(8)])


def shift_x(v, d):
    return lax.ppermute(v, "rep", [(k, (k + 2 * d) % 8) for k in range(8)])


def gather_rep(v):
    own = [v] + [shift_x(v, d) for d in (1, 2, 3)]
    return own + [swap_core(u) for u in own]


def message_call(*args):
    sds = jax.ShapeDtypeStruct
    return call(
        message_kernel,
        (sds((32, 144, 128), BF16), sds((96, 512), F32)),
        (SM,) + (HB,) * 11,
        args,
        (
            pltpu.VMEM((1024, 256), F32), pltpu.VMEM((1024, 128), BF16), pltpu.VMEM((512, 512), BF16),
            pltpu.VMEM((1, 1024), I32), pltpu.VMEM((1, 1024), I32), pltpu.VMEM((1, 1024), I32),
            pltpu.VMEM((32, 32), I32), pltpu.VMEM((1, 32), I32), pltpu.VMEM((1, 128), F32),
            pltpu.VMEM((1, 128), F32), pltpu.VMEM((1, 512), F32),
            pltpu.VMEM((1024, 128), BF16), pltpu.VMEM((1024, 512), BF16), pltpu.VMEM((32, 144, 128), BF16),
            pltpu.VMEM((1024, 8), I32),
            pltpu.SemaphoreType.DMA((15,)),
        ),
        (ANY, VM),
        63,
    )


def last_update(pos, parts, shared, olds, hot_own, acc):
    sds = jax.ShapeDtypeStruct
    return call(
        functools.partial(update_kernel, (3, 2, 1), (0,)),
        (sds((1024, 256), F32), sds((32, 7, 4, 128), F32)),
        (SM,),
        (pos, *parts, *shared, *olds, hot_own, acc),
        (
            pltpu.VMEM((128, 1024), F32), pltpu.VMEM((768, 256), F32), pltpu.VMEM((640, 128), F32),
            pltpu.SemaphoreType.DMA((4,)),
        ),
        (ANY, VM),
    )


def on_device(
    memory,
    hot_memory,
    cot_cold,
    cot_hot,
    src_local,
    dst_ids,
    times,
    edge_feat,
    cold_list,
    cold_count,
    hot_ids,
    time_freq,
    time_phase,
    w_msg,
    b_msg,
    w_in,
    w_hid,
):
    node = lax.axis_index("node")
    rep = lax.axis_index("rep")
    pos = jnp.stack([rep // 2, rep % 2, rep]).astype(I32)
    sds = jax.ShapeDtypeStruct

    chip, core = rep // 2, rep % 2
    send, hot = message_call(
        node.astype(I32)[None], memory, edge_feat, w_msg, src_local[None, :], times[None, :],
        dst_ids[None, :], cold_list, cold_count[None, :], time_freq[None, :], time_phase[None, :],
        b_msg[None, :],
    )
    recv = lax.all_to_all(send, "node", split_axis=0, concat_axis=0, tiled=True)

    hot = hot + swap_core(hot)
    spill = lax.dynamic_slice_in_dim(hot, 64 + 16 * core, 16, 0)
    spill = lax.ppermute(spill, "node", [(k, (k + 1) % 32) for k in range(32)])
    k = jnp.arange(128, dtype=I32)
    want = 32768 + 32 * node + 4 * (k // 16) + k % 4
    at = jnp.sum(jnp.where(want[:, None] == hot_ids[None, :], jnp.arange(1024, dtype=I32)[None, :], 0), axis=1)
    hot_mem = jnp.take(hot_memory, at, axis=0, mode="clip")
    hot_cot = jnp.take(cot_hot, at, axis=0, mode="clip")

    recv, hot_mem, hot_cot, _ = lax.optimization_barrier((recv, hot_mem, hot_cot, spill))
    block = sds((136, 512), F32)
    peer = swap_core(recv)
    sums = call(own_cold_kernel, (sds((512, 512), F32), sds((8, 512), F32)), (SM,), (pos, recv))
    parts = call(
        cold_kernel,
        (block,) * 4,
        (SM,),
        (pos, peer, *sums, hot.reshape(12, 8, 512), spill.reshape(2, 8, 512)),
    )
    parts = [parts[0]] + [shift_x(parts[d], d) for d in (1, 2, 3)]
    agg = call(
        agg_kernel,
        sds((144, 512), BF16),
        (ANY, ANY, ANY),
        (parts[2], parts[3], parts[1], parts[0]),
        (pltpu.VMEM((3, 136, 512), F32), pltpu.VMEM((144, 512), BF16), pltpu.SemaphoreType.DMA((4,))),
        ANY,
    )
    near, far, back = [shift_x(agg, d) for d in (1, 2, 3)]
    shared = (memory, cot_cold, hot_mem, hot_cot, w_in, w_hid)
    rows, sums = sds((256, 256), F32), sds((128, 1024), F32)
    new_own, hot_own, acc = call(
        functools.partial(update_kernel, (0,), ()),
        (rows, sds((8, 128), F32), sums),
        (SM,),
        (pos, agg, swap_core(agg), *shared),
    )
    far, back, near, new_own = lax.optimization_barrier((far, back, near, new_own))
    parts = (back, swap_core(back), far, swap_core(far), near, swap_core(near))
    new_memory, grad = last_update(pos, parts, shared, (new_own,), hot_own, acc)

    grad = lax.all_to_all(grad, "node", split_axis=0, concat_axis=0, tiled=True)
    grad, hot_new = call(piece_kernel, (sds((32, 5, 4, 128), F32), sds((32, 2, 4, 128), F32)), (), (grad,))
    grad = lax.all_to_all(grad, "node", split_axis=0, concat_axis=0, tiled=True)
    hot_parts = gather_rep(hot_new)
    grad, hot_parts = lax.optimization_barrier((grad, hot_parts))
    new_hot = call(
        hot_place_kernel,
        sds((1024, 256), F32),
        (SM,),
        (pos, hot_ids[None, :], *hot_parts),
        (pltpu.VMEM((8, 128, 256), F32),),
    )
    own = [grad[0:29]] + [shift_x(grad[0:29], d) for d in (1, 2, 3)]
    own[2], new_hot = lax.optimization_barrier((own[2], new_hot))
    grads = ()
    for other in (False, True):
        grads = call(
            functools.partial(place_kernel, tuple((d, other) for d in range(4))),
            (sds((512, 768), F32), sds((256, 768), F32)),
            (SM, VM, VM, VM, VM) + (ANY,) * len(grads),
            (pos, *[swap_core(v) if other else v for v in own], *grads),
            (pltpu.VMEM((384, 768), F32), pltpu.SemaphoreType.DMA((8,))),
            (ANY, ANY),
            aliases={5: 0, 6: 1} if grads else {},
        )
    grad_in, grad_hid = grads
    return (new_memory, new_hot, grad_in, grad_hid)


def solution(mesh):
    in_specs = (
        P("node", None),
        P(),
        P("node", None),
        P(),
        P(("node", "rep")),
        P(("node", "rep")),
        P(("node", "rep")),
        P(("node", "rep"), None),
        P(("node", "rep"), None),
        P(("node", "rep")),
        P(),
        P(),
        P(),
        P(),
        P(),
        P(),
        P(),
    )
    out_specs = (P("node", None), P(), P(), P())
    return jax.shard_map(
        on_device, mesh=mesh, in_specs=in_specs, out_specs=out_specs, check_vma=False
    )
```

```python
import functools

import jax
import jax.numpy as jnp
from jax import lax
from jax.experimental import pallas as pl
from jax.experimental.pallas import tpu as pltpu
from jax.sharding import PartitionSpec as P

GRAD_SCALE = 1.0 / 64.0
DEAD = 2.0**100
F32, BF16, I32 = jnp.float32, jnp.bfloat16, jnp.int32
VM = pl.BlockSpec(memory_space=pltpu.VMEM)
SM = pl.BlockSpec(memory_space=pltpu.SMEM)
HB = pl.BlockSpec(memory_space=pltpu.HBM)
ANY = pl.BlockSpec(memory_space=pl.ANY)


def iota(shape, dim):
    return lax.broadcasted_iota(I32, shape, dim)


def one_hot(mask):
    return jnp.where(mask, 1.0, 0.0).astype(BF16)


def mm(a, b, dims=((1,), (0,))):
    return lax.dot_general(a, b, (dims, ((), ())), preferred_element_type=F32)


def call(body, out_shape, places, args, scratch=(), out_places=None, mib=48, aliases=None):
    if out_places is None:
        out_places = jax.tree.map(lambda _: VM, out_shape)
    return pl.pallas_call(
        body,
        out_shape=out_shape,
        in_specs=list(places) + [VM] * (len(args) - len(places)),
        out_specs=out_places,
        scratch_shapes=list(scratch),
        input_output_aliases=aliases or {},
        compiler_params=pltpu.CompilerParams(vmem_limit_bytes=mib * 1024 * 1024),
    )(*args)


def column(row):
    return jnp.broadcast_to(row, (8, row.shape[1])).T[:, 0:1]


def cosine(x):
    k = jnp.round(x * 0.15915494309189535)
    r = x - k * 6.28125
    r = r - k * 0.0019350051879882812
    r = r - k * 3.019916e-07
    u = 1.5707963267948966 - jnp.abs(r)
    u2 = u * u
    p = 2.6083159809786593e-06
    for c in (-0.00019810690719168633, 0.0083330785855650902, -0.16666659712791443, 1.0):
        p = p * u2 + c
    return u * p


def message_kernel(
    pos, mem_h, edge_h, w_h, src_h, times_h, dst_h, listed_h, used_h, freq_h, phase_h, b_h, send_h, hot,
    mem, edge, w, src, times, dst_v, listed, used, freq, phase, b, encs, msgs, out, cols, sems,
):
    loads = [
        pltpu.make_async_copy(h, v, sems.at[i])
        for i, (h, v) in enumerate(
            (
                (src_h, src), (times_h, times), (dst_h, dst_v), (listed_h, listed), (used_h, used),
                (freq_h, freq), (phase_h, phase), (b_h, b), (mem_h, mem), (edge_h, edge), (w_h, w),
            )
        )
    ]
    for c in loads:
        c.start()
    for c in loads[:8]:
        c.wait()
    n_ev, step = 1024, 256
    dst = dst_v[...]
    line = iota((8, n_ev), 0)
    packed = jnp.where(line == 0, src[...], jnp.where(line == 1, times[...], dst))
    cols[...] = packed.T
    slot = iota((32, 32), 0)
    eye = one_hot(slot == iota((32, 32), 1))
    names = listed[...]
    hi = mm(eye, (names >> 5).astype(F32).astype(BF16), ((1,), (1,)))
    lo = mm(eye, (names & 31).astype(F32).astype(BF16), ((1,), (1,)))
    names = jnp.where(slot < used[...], (hi * 32.0 + lo).astype(I32), -1)
    encs[...] = cosine(cols[:, 1:2].astype(F32) * freq[...] + phase[...]).astype(BF16)
    for c in loads[8:]:
        c.wait()
    mem16 = mem[...].astype(BF16)
    for e in range(0, n_ev, step):
        at = cols[e : e + step, :]
        src_mem = mm(one_hot(iota((step, 1024), 1) == at[:, 0:1]), mem16).astype(BF16)
        raw = jnp.concatenate([src_mem, edge[e : e + step, :], encs[e : e + step, :]], axis=1)
        pre = mm(raw, w[...]) + b[...]
        msgs[e : e + step, :] = (pre * jax.nn.sigmoid(pre)).astype(BF16)
    row = dst & 1023
    facts = jnp.where(line == 0, row >> 5, jnp.where(line == 1, row & 31, jnp.where(line == 2, 1, 0)))
    facts = facts.astype(F32).astype(BF16)
    lane = iota((8, 128), 1)
    stores = []
    for t in range(4):
        pick = jnp.concatenate(
            [one_hot(iota((32, n_ev), 1) == names[:, o : o + 1]) for o in range(8 * t, 8 * t + 8)], axis=0
        )
        moved = mm(pick, msgs[...]).astype(BF16)
        tail = mm(facts, pick, ((1,), (1,)))
        for i in range(8):
            o = 8 * t + i
            for q in range(4):
                out[o, 32 * q : 32 * q + 32, :] = moved[32 * i : 32 * i + 32, 128 * q : 128 * q + 128]
            k = o % 4
            own = tail[:, 128 * (i // 4) : 128 * (i // 4) + 128]
            own = jnp.where((lane >> 5) == k, own, 0.0)
            own = pltpu.roll(own, ((pos[0] & 3) + 4 - k) * 32 & 127, 1)
            out[o, 128:144, :] = jnp.concatenate([own, jnp.zeros((8, 128), F32)], axis=0).astype(BF16)
        here = pl.ds(8 * t, 8)
        stores.append(pltpu.make_async_copy(out.at[here], send_h.at[here], sems.at[11 + t]))
        stores[-1].start()
    window = jnp.where(dst >= 32768, (dst - 32768 - 32 * pos[0] + 1024) & 1023, -1)
    q = iota((96, n_ev), 0)
    block = jnp.where(q < 64, 2 * ((q >> 3) & 3) + ((q >> 5) & 1), 8 + 2 * ((q >> 3) & 1) + ((q >> 4) & 1))
    hit = one_hot(4 * block + (q & 3) == window)
    total = mm(hit, msgs[...])
    count = jnp.sum(hit.astype(F32), axis=1, keepdims=True)
    hot[...] = jnp.where((iota((96, 512), 0) & 7) < 4, total, count)
    for c in stores:
        c.wait()


def cold_hits(pos, got):
    q = iota((512, 128), 0)
    want = (q & 127) + 256 * ((pos[0] + (q >> 7)) & 3) + 128 * pos[1]
    hits = []
    for g in range(8):
        tail = got[4 * g, 128:144, :].astype(F32)
        for i in range(1, 4):
            tail = tail + got[4 * g + i, 128:144, :].astype(F32)
        row = jnp.where(tail[2:3, :] > 0.5, tail[0:1, :] * 32.0 + tail[1:2, :], -1.0).astype(I32)
        hits.append(one_hot(want == row))
    return jnp.concatenate(hits, axis=1)


def cold_sums(hit, got, n):
    msgs = [got[:, 32 * k : 32 * k + 32, :].reshape(1024, 128) for k in (2 * n, 2 * n + 1)]
    return mm(hit, jnp.concatenate(msgs, axis=1))


def own_cold_kernel(pos, own, sums, counts):
    hit = cold_hits(pos, own)
    counts[...] = mm(jnp.ones((8, 1024), BF16), hit, ((1,), (1,)))
    for n in range(2):
        sums[:, 256 * n : 256 * n + 256] = cold_sums(hit, own, n)


def cold_kernel(pos, peer, sums, counts, hot, spill, o0, o1, o2, o3):
    hit = cold_hits(pos, peer)
    count = counts[...] + mm(jnp.ones((8, 1024), BF16), hit, ((1,), (1,)))
    for n in range(2):
        cols = slice(256 * n, 256 * n + 256)
        total = sums[:, cols] + cold_sums(hit, peer, n)
        for d, to in enumerate((o0, o1, o2, o3)):
            here = slice(128 * d, 128 * d + 128)
            to[0:128, cols] = total[here, :]
            j = (pos[0] + d) & 3
            tile = hot[4 * pos[1] + j, :, cols] + jnp.where(j < 2, 1.0, 0.0) * spill[j & 1, :, cols]
            if n == 0:
                rows = jnp.concatenate([count[:, here], tile[:, 128:256]], axis=1)
                tile = jnp.where((iota((8, 256), 0) >= 4) & (iota((8, 256), 1) < 128), rows, tile)
            to[128:136, cols] = tile


def agg_kernel(p1_h, p2_h, p3_h, p0, out_h, part, out, sems):
    loads = [pltpu.make_async_copy(h, part.at[i], sems.at[i]) for i, h in enumerate((p1_h, p2_h, p3_h))]
    for c in loads:
        c.start()
    for c in loads:
        c.wait()
    total = p0[...] + part[0] + part[1] + part[2]
    count = column(total[132:133, 0:128])
    agg = jnp.where(count > 0.0, total[0:128, :] / jnp.maximum(count, 1.0), DEAD)
    out[0:128, :] = agg.astype(BF16)
    count = total[132:136, 128:129]
    agg = jnp.where(count > 0.0, total[128:132, :] / jnp.maximum(count, 1.0), DEAD)
    out[128:144, :] = jnp.concatenate([agg, jnp.full((12, 512), DEAD, F32)], axis=0).astype(BF16)
    store = pltpu.make_async_copy(out, out_h, sems.at[3])
    store.start()
    store.wait()


def gates(agg, mem, w_in, w_hid):
    gi = mm(agg, w_in)
    gh = mm(mem.astype(BF16), w_hid)
    reset = jax.nn.sigmoid(gi[:, 0:256] + gh[:, 0:256])
    update = jax.nn.sigmoid(gi[:, 256:512] + gh[:, 256:512])
    cand = jnp.tanh(gi[:, 512:768] + reset * gh[:, 512:768])
    return reset, update, cand, gh[:, 512:768]


def hot_place_kernel(pos, ids, a0, a1, a2, a3, b0, b1, b2, b3, out, rows):
    x, core = pos[0], pos[1]
    for group, c in (((a0, a1, a2, a3), core), ((b0, b1, b2, b3), 1 - core)):
        for d, part in enumerate(group):
            block = 2 * ((x - d + 4) & 3) + c
            for n in range(32):
                rows[block, 4 * n : 4 * n + 4, 0:128] = part[n, 0]
                rows[block, 4 * n : 4 * n + 4, 128:256] = part[n, 1]
    name = column(ids[...]) - 32768
    at = 128 * ((name >> 2) & 7) + 4 * (name >> 5) + (name & 3)
    full = rows[...].reshape(1024, 256)
    hi = full.astype(BF16)
    rest = full - hi.astype(F32)
    mid = rest.astype(BF16)
    low = (rest - mid.astype(F32)).astype(BF16)
    for h in range(0, 1024, 256):
        pick = one_hot(iota((256, 1024), 1) == at[h : h + 256, :])
        out[h : h + 256, :] = mm(pick, hi) + (mm(pick, mid) + mm(pick, low))


def update_kernel(ds, done, pos, *refs):
    last = len(done) > 0
    parts, refs = refs[: 2 * len(ds)], refs[2 * len(ds) :]
    mem, cot, hot_mem, hot_cot, w_in, w_hid = refs[:6]
    refs = refs[6:]
    if last:
        olds, (own_hot, old_acc, new_h, grad, acc, new, flat, sems) = refs[: len(done)], refs[len(done) :]
        stores = []
        for d, old in zip(done, olds):
            at = pl.ds(pl.multiple_of(256 * ((pos[0] - d + 4) & 3), 256), 256)
            stores.append(pltpu.make_async_copy(old, new_h.at[at], sems.at[d]))
            stores[-1].start()
    elif 0 in ds:
        new, hot, acc = refs
        old_acc = None
    else:
        old_acc, new, acc = refs
    if old_acc is not None:
        acc[...] = old_acc[...]
    x, core, rep = pos[0], pos[1], pos[2]
    q, k = iota((128, 512), 0), iota((128, 512), 1)
    sel_a = one_hot((k == 64 * rep + q) & (q < 64))
    q, k = iota((128, 256), 0), iota((128, 256), 1)
    sel_m = one_hot((k == 32 * rep + q - 64) & (q >= 64) & (q < 96))
    chips = [(x - d + 4) & 3 for d in ds]
    ats = [pl.ds(pl.multiple_of(256 * c, 256), 256) for c in chips]
    hot_ats = [pl.ds(pl.multiple_of(32 * c, 32), 32) for c in chips]
    rows = []
    for i in range(len(ds)):
        mine, other = parts[2 * i][...], parts[2 * i + 1][...]
        low = jnp.where(core == 0, mine, other)
        high = jnp.where(core == 0, other, mine)
        rows += [low[0:128], high[0:128], low[128:144], high[128:144]]
    wide = jnp.concatenate(rows, axis=0).astype(F32)
    live = wide[:, 0:1] < DEAD * 0.5
    a = jnp.where(live, wide, 0.0).astype(BF16)
    m = jnp.concatenate([v for h, k in zip(ats, hot_ats) for v in (mem[h, :], hot_mem[k, :])], axis=0)
    g = jnp.concatenate([v for h, k in zip(ats, hot_ats) for v in (cot[h, :], hot_cot[k, :])], axis=0)
    reset, update, cand, hid_cand = gates(a, m, w_in[...], w_hid[...])
    fresh = jnp.where(live, (1.0 - update) * cand + update * m, m)
    for i, d in enumerate(ds):
        part = fresh[288 * i : 288 * i + 256, :]
        if last:
            new[256 * i : 256 * i + 256, :] = part
            stores.append(pltpu.make_async_copy(new.at[256 * i : 256 * i + 256], new_h.at[ats[i]], sems.at[d]))
            stores[-1].start()
        else:
            new[...] = part
            if d == 0:
                own = jnp.where(core == 0, fresh[256:264, :], fresh[272:280, :])
                hot[...] = jnp.concatenate([own[0:4, 0:128], own[0:4, 128:256]], axis=0)
    g = jnp.where(live, g, 0.0)
    d_cand = g * (1.0 - update) * (1.0 - cand * cand)
    d_upd = g * (m - cand) * update * (1.0 - update)
    d_reset = d_cand * hid_cand * reset * (1.0 - reset)
    left = (mm(sel_a, a, ((1,), (1,))) + mm(sel_m, m.astype(BF16), ((1,), (1,)))).astype(BF16)
    for j, v in enumerate((d_reset, d_upd, d_cand, d_cand * reset)):
        hi = v.astype(BF16)
        low = (v - hi.astype(F32)).astype(BF16)
        part = mm(left, hi) + mm(left, low)
        cols = slice(256 * j, 256 * j + 256)
        if old_acc is None:
            acc[:, cols] = part
        else:
            acc[:, cols] += part
    if last:
        total = acc[...] * GRAD_SCALE
        third = jnp.where(iota((128, 256), 0) < 64, total[:, 512:768], total[:, 768:1024])
        total = jnp.concatenate([total[:, 0:512], third], axis=1)
        for c in range(6):
            flat[96 * c : 96 * c + 96, :] = total[0:96, 128 * c : 128 * c + 128]
        flat[576:640, :] = jnp.zeros((64, 128), F32)
        for p in range(32):
            for j in range(5):
                grad[p, j] = flat[20 * p + 4 * j : 20 * p + 4 * j + 4, :]
            for j in range(2):
                grad[p, 5 + j] = own_hot[4 * j : 4 * j + 4, :]
        for c in stores:
            c.wait()


def piece_kernel(parts, out, hot):
    for j in range(5):
        total = parts[0, j]
        for k in range(1, 32):
            total = total + parts[k, j]
        for k in range(32):
            out[k, j] = total
    for k in range(32):
        hot[k] = parts[k, 5:7]


def place_kernel(blocks, pos, *refs):
    parts, (g_in, g_hid, both, sems) = refs[: len(blocks)], refs[-4:]
    stores = []
    for n, ((d, other), part) in enumerate(zip(blocks, parts)):
        block = 2 * ((pos[0] - d + 4) & 3) + (1 - pos[1] if other else pos[1])
        for k in range(144):
            i, c = 4 * k % 96, 4 * k // 96
            both[96 * n + i : 96 * n + i + 4, 128 * c : 128 * c + 128] = part[k // 5, k % 5]
        for rows, at, dst in (
            (64, 96 * n, g_in.at[pl.ds(pl.multiple_of(block * 64, 64), 64)]),
            (32, 96 * n + 64, g_hid.at[pl.ds(pl.multiple_of(block * 32, 32), 32)]),
        ):
            stores.append(pltpu.make_async_copy(both.at[at : at + rows], dst, sems.at[len(stores)]))
            stores[-1].start()
    for c in stores:
        c.wait()


def swap_core(v):
    return lax.ppermute(v, "rep", [(k, k ^ 1) for k in range(8)])


def shift_x(v, d):
    return lax.ppermute(v, "rep", [(k, (k + 2 * d) % 8) for k in range(8)])


def gather_rep(v):
    own = [v] + [shift_x(v, d) for d in (1, 2, 3)]
    return own + [swap_core(u) for u in own]


def message_call(*args):
    sds = jax.ShapeDtypeStruct
    return call(
        message_kernel,
        (sds((32, 144, 128), BF16), sds((96, 512), F32)),
        (SM,) + (HB,) * 11,
        args,
        (
            pltpu.VMEM((1024, 256), F32), pltpu.VMEM((1024, 128), BF16), pltpu.VMEM((512, 512), BF16),
            pltpu.VMEM((1, 1024), I32), pltpu.VMEM((1, 1024), I32), pltpu.VMEM((1, 1024), I32),
            pltpu.VMEM((32, 32), I32), pltpu.VMEM((1, 32), I32), pltpu.VMEM((1, 128), F32),
            pltpu.VMEM((1, 128), F32), pltpu.VMEM((1, 512), F32),
            pltpu.VMEM((1024, 128), BF16), pltpu.VMEM((1024, 512), BF16), pltpu.VMEM((32, 144, 128), BF16),
            pltpu.VMEM((1024, 8), I32),
            pltpu.SemaphoreType.DMA((15,)),
        ),
        (ANY, VM),
        63,
    )


def last_update(pos, parts, shared, olds, hot_own, acc):
    sds = jax.ShapeDtypeStruct
    return call(
        functools.partial(update_kernel, (3, 2), (0, 1)),
        (sds((1024, 256), F32), sds((32, 7, 4, 128), F32)),
        (SM,),
        (pos, *parts, *shared, *olds, hot_own, acc),
        (
            pltpu.VMEM((128, 1024), F32), pltpu.VMEM((512, 256), F32), pltpu.VMEM((640, 128), F32),
            pltpu.SemaphoreType.DMA((4,)),
        ),
        (ANY, VM),
    )


def on_device(
    memory,
    hot_memory,
    cot_cold,
    cot_hot,
    src_local,
    dst_ids,
    times,
    edge_feat,
    cold_list,
    cold_count,
    hot_ids,
    time_freq,
    time_phase,
    w_msg,
    b_msg,
    w_in,
    w_hid,
):
    node = lax.axis_index("node")
    rep = lax.axis_index("rep")
    pos = jnp.stack([rep // 2, rep % 2, rep]).astype(I32)
    sds = jax.ShapeDtypeStruct

    chip, core = rep // 2, rep % 2
    send, hot = message_call(
        node.astype(I32)[None], memory, edge_feat, w_msg, src_local[None, :], times[None, :],
        dst_ids[None, :], cold_list, cold_count[None, :], time_freq[None, :], time_phase[None, :],
        b_msg[None, :],
    )
    recv = lax.all_to_all(send, "node", split_axis=0, concat_axis=0, tiled=True)

    hot = hot + swap_core(hot)
    spill = lax.dynamic_slice_in_dim(hot, 64 + 16 * core, 16, 0)
    spill = lax.ppermute(spill, "node", [(k, (k + 1) % 32) for k in range(32)])
    k = jnp.arange(128, dtype=I32)
    want = 32768 + 32 * node + 4 * (k // 16) + k % 4
    at = jnp.sum(jnp.where(want[:, None] == hot_ids[None, :], jnp.arange(1024, dtype=I32)[None, :], 0), axis=1)
    hot_mem = jnp.take(hot_memory, at, axis=0, mode="clip")
    hot_cot = jnp.take(cot_hot, at, axis=0, mode="clip")

    recv, hot_mem, hot_cot, _ = lax.optimization_barrier((recv, hot_mem, hot_cot, spill))
    block = sds((136, 512), F32)
    peer = swap_core(recv)
    sums = call(own_cold_kernel, (sds((512, 512), F32), sds((8, 512), F32)), (SM,), (pos, recv))
    parts = call(
        cold_kernel,
        (block,) * 4,
        (SM,),
        (pos, peer, *sums, hot.reshape(12, 8, 512), spill.reshape(2, 8, 512)),
    )
    parts = [parts[0]] + [shift_x(parts[d], d) for d in (1, 2, 3)]
    agg = call(
        agg_kernel,
        sds((144, 512), BF16),
        (ANY, ANY, ANY),
        (parts[2], parts[3], parts[1], parts[0]),
        (pltpu.VMEM((3, 136, 512), F32), pltpu.VMEM((144, 512), BF16), pltpu.SemaphoreType.DMA((4,))),
        ANY,
    )
    near, far, back = [shift_x(agg, d) for d in (1, 2, 3)]
    shared = (memory, cot_cold, hot_mem, hot_cot, w_in, w_hid)
    rows, sums = sds((256, 256), F32), sds((128, 1024), F32)
    new_own, hot_own, acc = call(
        functools.partial(update_kernel, (0,), ()),
        (rows, sds((8, 128), F32), sums),
        (SM,),
        (pos, agg, swap_core(agg), *shared),
    )
    near_swap = swap_core(near)
    far, near_swap = lax.optimization_barrier((far, near_swap))
    back, new_own = lax.optimization_barrier((back, new_own))
    new_near, acc = call(
        functools.partial(update_kernel, (1,), ()),
        (rows, sums),
        (SM,),
        (pos, near, near_swap, *shared, acc),
    )
    parts = (back, swap_core(back), far, swap_core(far))
    new_memory, grad = last_update(pos, parts, shared, (new_own, new_near), hot_own, acc)

    grad = lax.all_to_all(grad, "node", split_axis=0, concat_axis=0, tiled=True)
    grad, hot_new = call(piece_kernel, (sds((32, 5, 4, 128), F32), sds((32, 2, 4, 128), F32)), (), (grad,))
    grad = lax.all_to_all(grad, "node", split_axis=0, concat_axis=0, tiled=True)
    hot_parts = gather_rep(hot_new)
    grad, hot_parts = lax.optimization_barrier((grad, hot_parts))
    new_hot = call(
        hot_place_kernel,
        sds((1024, 256), F32),
        (SM,),
        (pos, hot_ids[None, :], *hot_parts),
        (pltpu.VMEM((8, 128, 256), F32),),
    )
    own = [grad[0:29]] + [shift_x(grad[0:29], d) for d in (1, 2, 3)]
    own[2], new_hot = lax.optimization_barrier((own[2], new_hot))
    grads = ()
    for other in (False, True):
        grads = call(
            functools.partial(place_kernel, tuple((d, other) for d in range(4))),
            (sds((512, 768), F32), sds((256, 768), F32)),
            (SM, VM, VM, VM, VM) + (ANY,) * len(grads),
            (pos, *[swap_core(v) if other else v for v in own], *grads),
            (pltpu.VMEM((384, 768), F32), pltpu.SemaphoreType.DMA((8,))),
            (ANY, ANY),
            aliases={5: 0, 6: 1} if grads else {},
        )
    grad_in, grad_hid = grads
    return (new_memory, new_hot, grad_in, grad_hid)


def solution(mesh):
    in_specs = (
        P("node", None),
        P(),
        P("node", None),
        P(),
        P(("node", "rep")),
        P(("node", "rep")),
        P(("node", "rep")),
        P(("node", "rep"), None),
        P(("node", "rep"), None),
        P(("node", "rep")),
        P(),
        P(),
        P(),
        P(),
        P(),
        P(),
        P(),
    )
    out_specs = (P("node", None), P(), P(), P())
    return jax.shard_map(
        on_device, mesh=mesh, in_specs=in_specs, out_specs=out_specs, check_vma=False
    )
```

```python
import functools

import jax
import jax.numpy as jnp
from jax import lax
from jax.experimental import pallas as pl
from jax.experimental.pallas import tpu as pltpu
from jax.sharding import PartitionSpec as P

GRAD_SCALE = 1.0 / 64.0
DEAD = 2.0**100
F32, BF16, I32 = jnp.float32, jnp.bfloat16, jnp.int32
VM = pl.BlockSpec(memory_space=pltpu.VMEM)
SM = pl.BlockSpec(memory_space=pltpu.SMEM)
HB = pl.BlockSpec(memory_space=pltpu.HBM)
ANY = pl.BlockSpec(memory_space=pl.ANY)


def iota(shape, dim):
    return lax.broadcasted_iota(I32, shape, dim)


def one_hot(mask):
    return jnp.where(mask, 1.0, 0.0).astype(BF16)


def mm(a, b, dims=((1,), (0,))):
    return lax.dot_general(a, b, (dims, ((), ())), preferred_element_type=F32)


def call(body, out_shape, places, args, scratch=(), out_places=None, mib=48, aliases=None):
    if out_places is None:
        out_places = jax.tree.map(lambda _: VM, out_shape)
    return pl.pallas_call(
        body,
        out_shape=out_shape,
        in_specs=list(places) + [VM] * (len(args) - len(places)),
        out_specs=out_places,
        scratch_shapes=list(scratch),
        input_output_aliases=aliases or {},
        compiler_params=pltpu.CompilerParams(vmem_limit_bytes=mib * 1024 * 1024),
    )(*args)


def column(row):
    return jnp.broadcast_to(row, (8, row.shape[1])).T[:, 0:1]


def cosine(x):
    k = jnp.round(x * 0.15915494309189535)
    r = x - k * 6.28125
    r = r - k * 0.0019350051879882812
    r = r - k * 3.019916e-07
    u = 1.5707963267948966 - jnp.abs(r)
    u2 = u * u
    p = 2.6083159809786593e-06
    for c in (-0.00019810690719168633, 0.0083330785855650902, -0.16666659712791443, 1.0):
        p = p * u2 + c
    return u * p


def message_kernel(
    pos, mem_h, edge_h, w_h, src_h, times_h, dst_h, listed_h, used_h, freq_h, phase_h, b_h, send_h, hot,
    mem, edge, w, src, times, dst_v, listed, used, freq, phase, b, encs, msgs, out, cols, sems,
):
    loads = [
        pltpu.make_async_copy(h, v, sems.at[i])
        for i, (h, v) in enumerate(
            (
                (src_h, src), (times_h, times), (dst_h, dst_v), (listed_h, listed), (used_h, used),
                (freq_h, freq), (phase_h, phase), (b_h, b), (mem_h, mem), (edge_h, edge), (w_h, w),
            )
        )
    ]
    for c in loads:
        c.start()
    for c in loads[:8]:
        c.wait()
    n_ev, step = 1024, 256
    dst = dst_v[...]
    line = iota((8, n_ev), 0)
    packed = jnp.where(line == 0, src[...], jnp.where(line == 1, times[...], dst))
    cols[...] = packed.T
    slot = iota((32, 32), 0)
    eye = one_hot(slot == iota((32, 32), 1))
    names = listed[...]
    hi = mm(eye, (names >> 5).astype(F32).astype(BF16), ((1,), (1,)))
    lo = mm(eye, (names & 31).astype(F32).astype(BF16), ((1,), (1,)))
    names = jnp.where(slot < used[...], (hi * 32.0 + lo).astype(I32), -1)
    encs[...] = cosine(cols[:, 1:2].astype(F32) * freq[...] + phase[...]).astype(BF16)
    for c in loads[8:]:
        c.wait()
    mem16 = mem[...].astype(BF16)
    for e in range(0, n_ev, step):
        at = cols[e : e + step, :]
        src_mem = mm(one_hot(iota((step, 1024), 1) == at[:, 0:1]), mem16).astype(BF16)
        raw = jnp.concatenate([src_mem, edge[e : e + step, :], encs[e : e + step, :]], axis=1)
        pre = mm(raw, w[...]) + b[...]
        msgs[e : e + step, :] = (pre * jax.nn.sigmoid(pre)).astype(BF16)
    row = dst & 1023
    facts = jnp.where(line == 0, row >> 5, jnp.where(line == 1, row & 31, jnp.where(line == 2, 1, 0)))
    facts = facts.astype(F32).astype(BF16)
    lane = iota((8, 128), 1)
    stores = []
    for t in range(4):
        pick = jnp.concatenate(
            [one_hot(iota((32, n_ev), 1) == names[:, o : o + 1]) for o in range(8 * t, 8 * t + 8)], axis=0
        )
        moved = mm(pick, msgs[...]).astype(BF16)
        tail = mm(facts, pick, ((1,), (1,)))
        for i in range(8):
            o = 8 * t + i
            for q in range(4):
                out[o, 32 * q : 32 * q + 32, :] = moved[32 * i : 32 * i + 32, 128 * q : 128 * q + 128]
            k = o % 4
            own = tail[:, 128 * (i // 4) : 128 * (i // 4) + 128]
            own = jnp.where((lane >> 5) == k, own, 0.0)
            own = pltpu.roll(own, ((pos[0] & 3) + 4 - k) * 32 & 127, 1)
            out[o, 128:144, :] = jnp.concatenate([own, jnp.zeros((8, 128), F32)], axis=0).astype(BF16)
        here = pl.ds(8 * t, 8)
        stores.append(pltpu.make_async_copy(out.at[here], send_h.at[here], sems.at[11 + t]))
        stores[-1].start()
    window = jnp.where(dst >= 32768, (dst - 32768 - 32 * pos[0] + 1024) & 1023, -1)
    q = iota((96, n_ev), 0)
    block = jnp.where(q < 64, 2 * ((q >> 3) & 3) + ((q >> 5) & 1), 8 + 2 * ((q >> 3) & 1) + ((q >> 4) & 1))
    hit = one_hot(4 * block + (q & 3) == window)
    total = mm(hit, msgs[...])
    count = jnp.sum(hit.astype(F32), axis=1, keepdims=True)
    hot[...] = jnp.where((iota((96, 512), 0) & 7) < 4, total, count)
    for c in stores:
        c.wait()


def cold_hits(pos, got):
    q = iota((512, 128), 0)
    want = (q & 127) + 256 * ((pos[0] + (q >> 7)) & 3) + 128 * pos[1]
    hits = []
    for g in range(8):
        tail = got[4 * g, 128:144, :].astype(F32)
        for i in range(1, 4):
            tail = tail + got[4 * g + i, 128:144, :].astype(F32)
        row = jnp.where(tail[2:3, :] > 0.5, tail[0:1, :] * 32.0 + tail[1:2, :], -1.0).astype(I32)
        hits.append(one_hot(want == row))
    return jnp.concatenate(hits, axis=1)


def cold_sums(hit, got, n):
    msgs = [got[:, 32 * k : 32 * k + 32, :].reshape(1024, 128) for k in (2 * n, 2 * n + 1)]
    return mm(hit, jnp.concatenate(msgs, axis=1))


def own_cold_kernel(pos, own, sums, counts):
    hit = cold_hits(pos, own)
    counts[...] = mm(jnp.ones((8, 1024), BF16), hit, ((1,), (1,)))
    for n in range(2):
        sums[:, 256 * n : 256 * n + 256] = cold_sums(hit, own, n)


def cold_kernel(pos, peer, sums, counts, hot, spill, o0, o1, o2, o3):
    hit = cold_hits(pos, peer)
    count = counts[...] + mm(jnp.ones((8, 1024), BF16), hit, ((1,), (1,)))
    for n in range(2):
        cols = slice(256 * n, 256 * n + 256)
        total = sums[:, cols] + cold_sums(hit, peer, n)
        for d, to in enumerate((o0, o1, o2, o3)):
            here = slice(128 * d, 128 * d + 128)
            to[0:128, cols] = total[here, :]
            j = (pos[0] + d) & 3
            tile = hot[4 * pos[1] + j, :, cols] + jnp.where(j < 2, 1.0, 0.0) * spill[j & 1, :, cols]
            if n == 0:
                rows = jnp.concatenate([count[:, here], tile[:, 128:256]], axis=1)
                tile = jnp.where((iota((8, 256), 0) >= 4) & (iota((8, 256), 1) < 128), rows, tile)
            to[128:136, cols] = tile


def agg_kernel(p1_h, p2_h, p3_h, p0, out_h, part, out, sems):
    loads = [pltpu.make_async_copy(h, part.at[i], sems.at[i]) for i, h in enumerate((p1_h, p2_h, p3_h))]
    for c in loads:
        c.start()
    for c in loads:
        c.wait()
    total = p0[...] + part[0] + part[1] + part[2]
    count = column(total[132:133, 0:128])
    agg = jnp.where(count > 0.0, total[0:128, :] / jnp.maximum(count, 1.0), DEAD)
    out[0:128, :] = agg.astype(BF16)
    count = total[132:136, 128:129]
    agg = jnp.where(count > 0.0, total[128:132, :] / jnp.maximum(count, 1.0), DEAD)
    out[128:144, :] = jnp.concatenate([agg, jnp.full((12, 512), DEAD, F32)], axis=0).astype(BF16)
    store = pltpu.make_async_copy(out, out_h, sems.at[3])
    store.start()
    store.wait()


def gates(agg, mem, w_in, w_hid):
    gi = mm(agg, w_in)
    gh = mm(mem.astype(BF16), w_hid)
    reset = jax.nn.sigmoid(gi[:, 0:256] + gh[:, 0:256])
    update = jax.nn.sigmoid(gi[:, 256:512] + gh[:, 256:512])
    cand = jnp.tanh(gi[:, 512:768] + reset * gh[:, 512:768])
    return reset, update, cand, gh[:, 512:768]


def hot_place_kernel(pos, ids, a0, a1, a2, a3, b0, b1, b2, b3, out, rows):
    x, core = pos[0], pos[1]
    for group, c in (((a0, a1, a2, a3), core), ((b0, b1, b2, b3), 1 - core)):
        for d, part in enumerate(group):
            block = 2 * ((x - d + 4) & 3) + c
            for n in range(32):
                rows[block, 4 * n : 4 * n + 4, 0:128] = part[n, 0]
                rows[block, 4 * n : 4 * n + 4, 128:256] = part[n, 1]
    name = column(ids[...]) - 32768
    at = 128 * ((name >> 2) & 7) + 4 * (name >> 5) + (name & 3)
    full = rows[...].reshape(1024, 256)
    hi = full.astype(BF16)
    rest = full - hi.astype(F32)
    mid = rest.astype(BF16)
    low = (rest - mid.astype(F32)).astype(BF16)
    for h in range(0, 1024, 256):
        pick = one_hot(iota((256, 1024), 1) == at[h : h + 256, :])
        out[h : h + 256, :] = mm(pick, hi) + (mm(pick, mid) + mm(pick, low))


def update_kernel(ds, done, pos, *refs):
    last = len(done) > 0
    parts, refs = refs[: 2 * len(ds)], refs[2 * len(ds) :]
    mem, cot, hot_mem, hot_cot, w_in, w_hid = refs[:6]
    refs = refs[6:]
    if last:
        olds, (own_hot, old_acc, new_h, grad, acc, new, flat, sems) = refs[: len(done)], refs[len(done) :]
        stores = []
        for d, old in zip(done, olds):
            at = pl.ds(pl.multiple_of(256 * ((pos[0] - d + 4) & 3), 256), 256)
            stores.append(pltpu.make_async_copy(old, new_h.at[at], sems.at[d]))
            stores[-1].start()
    elif 0 in ds:
        new, hot, acc = refs
        old_acc = None
    else:
        old_acc, new, acc = refs
    if old_acc is not None:
        acc[...] = old_acc[...]
    x, core, rep = pos[0], pos[1], pos[2]
    q, k = iota((128, 512), 0), iota((128, 512), 1)
    sel_a = one_hot((k == 64 * rep + q) & (q < 64))
    q, k = iota((128, 256), 0), iota((128, 256), 1)
    sel_m = one_hot((k == 32 * rep + q - 64) & (q >= 64) & (q < 96))
    chips = [(x - d + 4) & 3 for d in ds]
    ats = [pl.ds(pl.multiple_of(256 * c, 256), 256) for c in chips]
    hot_ats = [pl.ds(pl.multiple_of(32 * c, 32), 32) for c in chips]
    rows = []
    for i in range(len(ds)):
        mine, other = parts[2 * i][...], parts[2 * i + 1][...]
        low = jnp.where(core == 0, mine, other)
        high = jnp.where(core == 0, other, mine)
        rows += [low[0:128], high[0:128], low[128:144], high[128:144]]
    wide = jnp.concatenate(rows, axis=0).astype(F32)
    live = wide[:, 0:1] < DEAD * 0.5
    a = jnp.where(live, wide, 0.0).astype(BF16)
    m = jnp.concatenate([v for h, k in zip(ats, hot_ats) for v in (mem[h, :], hot_mem[k, :])], axis=0)
    g = jnp.concatenate([v for h, k in zip(ats, hot_ats) for v in (cot[h, :], hot_cot[k, :])], axis=0)
    reset, update, cand, hid_cand = gates(a, m, w_in[...], w_hid[...])
    fresh = jnp.where(live, (1.0 - update) * cand + update * m, m)
    for i, d in enumerate(ds):
        part = fresh[288 * i : 288 * i + 256, :]
        if last:
            new[256 * i : 256 * i + 256, :] = part
            stores.append(pltpu.make_async_copy(new.at[256 * i : 256 * i + 256], new_h.at[ats[i]], sems.at[d]))
            stores[-1].start()
        else:
            new[...] = part
            if d == 0:
                own = jnp.where(core == 0, fresh[256:264, :], fresh[272:280, :])
                hot[...] = jnp.concatenate([own[0:4, 0:128], own[0:4, 128:256]], axis=0)
    g = jnp.where(live, g, 0.0)
    d_cand = g * (1.0 - update) * (1.0 - cand * cand)
    d_upd = g * (m - cand) * update * (1.0 - update)
    d_reset = d_cand * hid_cand * reset * (1.0 - reset)
    left = (mm(sel_a, a, ((1,), (1,))) + mm(sel_m, m.astype(BF16), ((1,), (1,)))).astype(BF16)
    for j, v in enumerate((d_reset, d_upd, d_cand, d_cand * reset)):
        hi = v.astype(BF16)
        low = (v - hi.astype(F32)).astype(BF16)
        part = mm(left, hi) + mm(left, low)
        cols = slice(256 * j, 256 * j + 256)
        if old_acc is None:
            acc[:, cols] = part
        else:
            acc[:, cols] += part
    if last:
        total = acc[...] * GRAD_SCALE
        third = jnp.where(iota((128, 256), 0) < 64, total[:, 512:768], total[:, 768:1024])
        total = jnp.concatenate([total[:, 0:512], third], axis=1)
        for c in range(6):
            flat[96 * c : 96 * c + 96, :] = total[0:96, 128 * c : 128 * c + 128]
        flat[576:640, :] = jnp.zeros((64, 128), F32)
        for p in range(32):
            for j in range(5):
                grad[p, j] = flat[20 * p + 4 * j : 20 * p + 4 * j + 4, :]
            for j in range(2):
                grad[p, 5 + j] = own_hot[4 * j : 4 * j + 4, :]
        for c in stores:
            c.wait()


def piece_kernel(parts, out, hot):
    for j in range(5):
        total = parts[0, j]
        for k in range(1, 32):
            total = total + parts[k, j]
        for k in range(32):
            out[k, j] = total
    for k in range(32):
        hot[k] = parts[k, 5:7]


def place_kernel(blocks, pos, *refs):
    parts, (g_in, g_hid, both, sems) = refs[: len(blocks)], refs[-4:]
    stores = []
    for n, ((d, other), part) in enumerate(zip(blocks, parts)):
        block = 2 * ((pos[0] - d + 4) & 3) + (1 - pos[1] if other else pos[1])
        for k in range(144):
            i, c = 4 * k % 96, 4 * k // 96
            both[96 * n + i : 96 * n + i + 4, 128 * c : 128 * c + 128] = part[k // 5, k % 5]
        for rows, at, dst in (
            (64, 96 * n, g_in.at[pl.ds(pl.multiple_of(block * 64, 64), 64)]),
            (32, 96 * n + 64, g_hid.at[pl.ds(pl.multiple_of(block * 32, 32), 32)]),
        ):
            stores.append(pltpu.make_async_copy(both.at[at : at + rows], dst, sems.at[len(stores)]))
            stores[-1].start()
    for c in stores:
        c.wait()


def swap_core(v):
    return lax.ppermute(v, "rep", [(k, k ^ 1) for k in range(8)])


def shift_x(v, d):
    return lax.ppermute(v, "rep", [(k, (k + 2 * d) % 8) for k in range(8)])


def gather_rep(v):
    own = [v] + [shift_x(v, d) for d in (1, 2, 3)]
    return own + [swap_core(u) for u in own]


def message_call(*args):
    sds = jax.ShapeDtypeStruct
    return call(
        message_kernel,
        (sds((32, 144, 128), BF16), sds((96, 512), F32)),
        (SM,) + (HB,) * 11,
        args,
        (
            pltpu.VMEM((1024, 256), F32), pltpu.VMEM((1024, 128), BF16), pltpu.VMEM((512, 512), BF16),
            pltpu.VMEM((1, 1024), I32), pltpu.VMEM((1, 1024), I32), pltpu.VMEM((1, 1024), I32),
            pltpu.VMEM((32, 32), I32), pltpu.VMEM((1, 32), I32), pltpu.VMEM((1, 128), F32),
            pltpu.VMEM((1, 128), F32), pltpu.VMEM((1, 512), F32),
            pltpu.VMEM((1024, 128), BF16), pltpu.VMEM((1024, 512), BF16), pltpu.VMEM((32, 144, 128), BF16),
            pltpu.VMEM((1024, 8), I32),
            pltpu.SemaphoreType.DMA((15,)),
        ),
        (ANY, VM),
        63,
    )


def last_update(pos, parts, shared, olds, hot_own, acc):
    sds = jax.ShapeDtypeStruct
    return call(
        functools.partial(update_kernel, (3, 2), (0, 1)),
        (sds((1024, 256), F32), sds((32, 7, 4, 128), F32)),
        (SM,),
        (pos, *parts, *shared, *olds, hot_own, acc),
        (
            pltpu.VMEM((128, 1024), F32), pltpu.VMEM((512, 256), F32), pltpu.VMEM((640, 128), F32),
            pltpu.SemaphoreType.DMA((4,)),
        ),
        (ANY, VM),
    )


def on_device(
    memory,
    hot_memory,
    cot_cold,
    cot_hot,
    src_local,
    dst_ids,
    times,
    edge_feat,
    cold_list,
    cold_count,
    hot_ids,
    time_freq,
    time_phase,
    w_msg,
    b_msg,
    w_in,
    w_hid,
):
    node = lax.axis_index("node")
    rep = lax.axis_index("rep")
    pos = jnp.stack([rep // 2, rep % 2, rep]).astype(I32)
    sds = jax.ShapeDtypeStruct

    chip, core = rep // 2, rep % 2
    send, hot = message_call(
        node.astype(I32)[None], memory, edge_feat, w_msg, src_local[None, :], times[None, :],
        dst_ids[None, :], cold_list, cold_count[None, :], time_freq[None, :], time_phase[None, :],
        b_msg[None, :],
    )
    recv = lax.all_to_all(send, "node", split_axis=0, concat_axis=0, tiled=True)

    hot = hot + swap_core(hot)
    spill = lax.dynamic_slice_in_dim(hot, 64 + 16 * core, 16, 0)
    spill = lax.ppermute(spill, "node", [(k, (k + 1) % 32) for k in range(32)])
    k = jnp.arange(128, dtype=I32)
    want = 32768 + 32 * node + 4 * (k // 16) + k % 4
    at = jnp.sum(jnp.where(want[:, None] == hot_ids[None, :], jnp.arange(1024, dtype=I32)[None, :], 0), axis=1)
    hot_mem = jnp.take(hot_memory, at, axis=0, mode="clip")
    hot_cot = jnp.take(cot_hot, at, axis=0, mode="clip")

    recv, hot_mem, hot_cot, _ = lax.optimization_barrier((recv, hot_mem, hot_cot, spill))
    block = sds((136, 512), F32)
    peer = swap_core(recv)
    sums = call(own_cold_kernel, (sds((512, 512), F32), sds((8, 512), F32)), (SM,), (pos, recv))
    parts = call(
        cold_kernel,
        (block,) * 4,
        (SM,),
        (pos, peer, *sums, hot.reshape(12, 8, 512), spill.reshape(2, 8, 512)),
    )
    parts = [parts[0]] + [shift_x(parts[d], d) for d in (1, 2, 3)]
    agg = call(
        agg_kernel,
        sds((144, 512), BF16),
        (ANY, ANY, ANY),
        (parts[2], parts[3], parts[1], parts[0]),
        (pltpu.VMEM((3, 136, 512), F32), pltpu.VMEM((144, 512), BF16), pltpu.SemaphoreType.DMA((4,))),
        ANY,
    )
    near, far, back = [shift_x(agg, d) for d in (1, 2, 3)]
    shared = (memory, cot_cold, hot_mem, hot_cot, w_in, w_hid)
    rows, sums = sds((256, 256), F32), sds((128, 1024), F32)
    new_own, hot_own, acc = call(
        functools.partial(update_kernel, (0,), ()),
        (rows, sds((8, 128), F32), sums),
        (SM,),
        (pos, agg, swap_core(agg), *shared),
    )
    near_swap = swap_core(near)
    far, near_swap = lax.optimization_barrier((far, near_swap))
    back, new_own = lax.optimization_barrier((back, new_own))
    new_near, acc = call(
        functools.partial(update_kernel, (1,), ()),
        (rows, sums),
        (SM,),
        (pos, near, near_swap, *shared, acc),
    )
    parts = (back, swap_core(back), far, swap_core(far))
    new_memory, grad = last_update(pos, parts, shared, (new_own, new_near), hot_own, acc)

    grad = lax.all_to_all(grad, "node", split_axis=0, concat_axis=0, tiled=True)
    grad, hot_new = call(piece_kernel, (sds((32, 5, 4, 128), F32), sds((32, 2, 4, 128), F32)), (), (grad,))
    grad = lax.all_to_all(grad, "node", split_axis=0, concat_axis=0, tiled=True)
    hot_parts = gather_rep(hot_new)
    grad, hot_parts = lax.optimization_barrier((grad, hot_parts))
    new_hot = call(
        hot_place_kernel,
        sds((1024, 256), F32),
        (SM,),
        (pos, hot_ids[None, :], *hot_parts),
        (pltpu.VMEM((8, 128, 256), F32),),
    )
    own = [grad[0:29]] + [shift_x(grad[0:29], d) for d in (1, 2, 3)]
    grads = ()
    for blocks in (((0, False),), ((1, False), (2, False), (3, False)), tuple((d, True) for d in range(4))):
        n = len(blocks)
        grads = call(
            functools.partial(place_kernel, blocks),
            (sds((512, 768), F32), sds((256, 768), F32)),
            (SM,) + (VM,) * n + (ANY,) * len(grads),
            (pos, *[swap_core(own[d]) if other else own[d] for d, other in blocks], *grads),
            (pltpu.VMEM((96 * n, 768), F32), pltpu.SemaphoreType.DMA((2 * n,))),
            (ANY, ANY),
            aliases={n + 1: 0, n + 2: 1} if grads else {},
        )
        if n == 1:
            own[2], new_hot, *grads = lax.optimization_barrier((own[2], new_hot, *grads))
    grad_in, grad_hid = grads
    return (new_memory, new_hot, grad_in, grad_hid)


def solution(mesh):
    in_specs = (
        P("node", None),
        P(),
        P("node", None),
        P(),
        P(("node", "rep")),
        P(("node", "rep")),
        P(("node", "rep")),
        P(("node", "rep"), None),
        P(("node", "rep"), None),
        P(("node", "rep")),
        P(),
        P(),
        P(),
        P(),
        P(),
        P(),
        P(),
    )
    out_specs = (P("node", None), P(), P(), P())
    return jax.shard_map(
        on_device, mesh=mesh, in_specs=in_specs, out_specs=out_specs, check_vma=False
    )
```
